128 devices in a mesh: rows: 16 (over z, x_hi, core), kern: 8 (over y, x_lo).
Axes of the slice: x: 4 (x_hi: 2, x_lo: 2; x = x_hi * 2 + x_lo), y: 4, z: 4, core: 2. Of those that a mesh axis runs over, the one named last changes fastest.
Arguments:
- mask_params: float32 [16384, 16384], P(('rows', 'kern')), may hold values from -6 to 6
- pupil_kernels: float32 [16, 2, 2, 256, 256], P('kern'), may hold values from -0.005859375 to 0.005859375
- target_pattern: int32 [4096, 4096], P('rows', 'kern'), may hold values 0 or 1
Outputs:
- stepped_params: float32 [16384, 16384], P(('rows', 'kern'))
The draws below stay inside these ranges and needn't reach their ends.
All inputs are finite; a program needn't handle non-finite values. No bound on the sum of `target_pattern` on one device may be relied on, other than what follows from the above.
Results may differ from the reference program's by a relative error of at most 0.0081.
Values may be sent and summed in bfloat16 or wider, within the bound.
No kernel may reach another device: no remote copies, remote signals or barrier semaphores. Data moves between devices by JAX's collectives and lax.ppermute only.
A program may use at most 256 MiB of HBM per device.

```python
import math
import jax
import jax.numpy as jnp
from jax import lax

MASK = 16384
GRID = 4096
BAND = 256
KERNELS = 16


def place_ends(values, stream_key, least, largest):
    dims = values.shape
    place = [jax.random.randint(jax.random.fold_in(stream_key, axis), (), 0, dims[axis]) for axis in range(len(dims))]
    values = values.at[tuple(place)].set(least)
    longest = dims.index(max(dims))
    place[longest] = (place[longest] + 1) % dims[longest]
    return values.at[tuple(place)].set(largest)


def shard_levels(stream_key, extent, cuts, least, largest):
    factor_of = 1.0
    for position, shards_of in cuts:
        draws = jax.random.uniform(jax.random.fold_in(jax.random.fold_in(stream_key, 6), position), (shards_of,), jnp.float32, least / len(cuts), largest / len(cuts))
        factor_of = factor_of * jnp.repeat(jnp.exp(draws), extent[position] // shards_of).reshape((-1,) + (1,) * (len(extent) - 1 - position))
    return factor_of


def noise(key, extent, spread, limit, shards=(), held_as=jnp.bfloat16):
    entries = jax.random.normal(key, extent, jnp.float32) * spread
    if len(shards) > 0:
        entries = shard_levels(key, extent, shards, -0.22, 0.18) * entries
    return jnp.clip(entries, min=-limit, max=limit).astype(held_as)


def setup_inputs(seed: int = 0) -> dict:
    key_of = jax.random.split(jax.random.key(seed), 4)
    mask_params = noise(key_of[0], (MASK, MASK), 1.0, 6.0, ((0, 128),), jnp.float32)
    pupil_kernels = noise(key_of[1], (KERNELS, 2, 2, BAND, BAND), (16 * BAND * BAND) ** -0.5, 0.005859375, ((0, 8),), jnp.float32)
    target_pattern = place_ends((jax.random.randint(key_of[2], (GRID, GRID), 0, 2) < 1).astype(jnp.int32), jax.random.fold_in(key_of[2], 1), 0, 1)
    return {"mask_params": mask_params, "pupil_kernels": pupil_kernels, "target_pattern": target_pattern}


steepness = 4.0
threshold = 0.75
step_size = 1.0
dose_levels = (1.0, 1.15)


def band_table(positions, period, band_size):
    frequency = (jnp.arange(band_size, dtype=jnp.int32) - band_size // 2) % period
    product = (positions[:, None] * frequency[None, :]) % period
    angles = product.astype(jnp.float32) * (2.0 * math.pi / period)
    return jnp.cos(angles), jnp.sin(angles)


def column_table():
    cosine, sine = band_table(jnp.arange(MASK, dtype=jnp.int32), MASK, BAND)
    return (jnp.concatenate([cosine, -sine], 1) * (1.0 / MASK)).astype(jnp.bfloat16)


def grid_tables(row_positions):
    cosine, sine = band_table(row_positions, GRID, BAND)
    rows_table = jnp.concatenate([cosine, sine], 1).astype(jnp.bfloat16)
    all_cos, all_sin = band_table(jnp.arange(GRID, dtype=jnp.int32), GRID, BAND)
    upper = jnp.concatenate([all_cos.T, all_sin.T], 1)
    lower = jnp.concatenate([-all_sin.T, all_cos.T], 1)
    column_map = jnp.concatenate([upper, lower], 0).astype(jnp.bfloat16)
    return rows_table, column_map


def hdot(left, right):
    return jnp.dot(left, right, precision=lax.Precision.HIGHEST, preferred_element_type=jnp.float32)


def row_spectrum(column_spec, row_cos, row_sin):
    band_size = row_cos.shape[1]
    col_re = column_spec[:, :band_size]
    col_im = column_spec[:, band_size:]
    real_part = hdot(row_cos.T, col_re) + hdot(row_sin.T, col_im)
    imag_part = hdot(row_cos.T, col_im) - hdot(row_sin.T, col_re)
    return real_part, imag_part


def field_of(spec_re, spec_im, kernel_re, kernel_im, rows_table, column_map):
    amp_re = kernel_re * spec_re - kernel_im * spec_im
    amp_im = kernel_re * spec_im + kernel_im * spec_re
    block = jnp.concatenate([jnp.concatenate([amp_re, amp_im], 1), jnp.concatenate([-amp_im, amp_re], 1)], 0).astype(jnp.bfloat16)
    partial_value = jnp.dot(rows_table, block, preferred_element_type=jnp.float32).astype(jnp.bfloat16)
    return jnp.dot(partial_value, column_map, preferred_element_type=jnp.float32)


def spectrum_adjoint(field, adjoint, kernel_re, kernel_im, rows_table, column_map):
    row_count = field.shape[0]
    grid_size = adjoint.shape[1]
    weighted = (2.0 * field.reshape(row_count, 2, grid_size) * adjoint.astype(jnp.float32)[:, None, :]).reshape(row_count, 2 * grid_size).astype(jnp.bfloat16)
    back = jnp.dot(weighted, column_map.T, preferred_element_type=jnp.float32).astype(jnp.bfloat16)
    grads = jnp.dot(rows_table.T, back, preferred_element_type=jnp.float32)
    band_size = kernel_re.shape[0]
    grad_re = grads[:band_size, :band_size] + grads[band_size:, band_size:]
    grad_im = grads[:band_size, band_size:] - grads[band_size:, :band_size]
    return kernel_re * grad_re + kernel_im * grad_im, kernel_re * grad_im - kernel_im * grad_re


def resist_adjoint(intensity, target):
    dose = jnp.array(dose_levels, jnp.float32)[:, None, None]
    resist = jax.nn.sigmoid(steepness * (dose * intensity - threshold))
    wanted = target.astype(jnp.float32)[None]
    return (2.0 * (resist - wanted) * resist * (1.0 - resist) * steepness * dose).astype(jnp.bfloat16)


def reference(mask_params, pupil_kernels, target_pattern):
    transmit = jnp.tanh(mask_params)
    table = column_table()
    column_spec = jnp.dot(transmit.astype(jnp.bfloat16), table, preferred_element_type=jnp.float32)
    row_cos, row_sin = band_table(jnp.arange(MASK, dtype=jnp.int32), MASK, BAND)
    spec_re, spec_im = row_spectrum(column_spec, row_cos, row_sin)
    rows_table, column_map = grid_tables(jnp.arange(GRID, dtype=jnp.int32))

    def forward_step(carry, kernel):
        powers = []
        for corner in range(2):
            field = field_of(spec_re, spec_im, kernel[corner, 0], kernel[corner, 1], rows_table, column_map)
            powers.append(carry[corner] + field[:, :GRID] * field[:, :GRID] + field[:, GRID:] * field[:, GRID:])
        return jnp.stack(powers), None

    intensity, _ = lax.scan(forward_step, jnp.zeros((2, GRID, GRID), jnp.float32), pupil_kernels)
    adjoint = resist_adjoint(intensity, target_pattern)

    def backward_step(carry, kernel):
        total_re, total_im = carry
        for corner in range(2):
            field = field_of(spec_re, spec_im, kernel[corner, 0], kernel[corner, 1], rows_table, column_map)
            grad_re, grad_im = spectrum_adjoint(field, adjoint[corner], kernel[corner, 0], kernel[corner, 1], rows_table, column_map)
            total_re = total_re + grad_re
            total_im = total_im + grad_im
        return (total_re, total_im), None

    zeros_band = jnp.zeros((BAND, BAND), jnp.float32)
    (spec_grad_re, spec_grad_im), _ = lax.scan(backward_step, (zeros_band, zeros_band), pupil_kernels)
    col_grad_re = hdot(row_cos, spec_grad_re) - hdot(row_sin, spec_grad_im)
    col_grad_im = hdot(row_sin, spec_grad_re) + hdot(row_cos, spec_grad_im)
    col_grad = jnp.concatenate([col_grad_re, col_grad_im], 1).astype(jnp.bfloat16)
    pixel_grad = jnp.dot(col_grad, table.T, preferred_element_type=jnp.float32)
    return mask_params - step_size * pixel_grad * (1.0 - transmit * transmit)
```

```python
import math

import jax
import jax.numpy as jnp
import numpy as np
from jax import lax
from jax.experimental import pallas as pl
from jax.experimental.pallas import tpu as pltpu
from jax.sharding import PartitionSpec as P

MASK = 16384
GRID = 4096
BAND = 256
COARSE = 512
STEP = 256
STEPS = MASK // STEP
ROWS = 16
KERN = 8
DEVICES = ROWS * KERN

steepness = 4.0
threshold = 0.75
step_size = 1.0
dose_levels = (1.0, 1.15)

VMEM_LIMIT = 56 * 1024 * 1024
HIGHEST = lax.Precision.HIGHEST


def tables(positions, period):
    frequency = np.arange(BAND) - BAND // 2
    angles = (np.outer(positions, frequency) % period) * (2.0 * math.pi / period)
    return np.cos(angles), np.sin(angles)


def bfloat(values):
    return np.asarray(values, np.float32).astype(jnp.bfloat16)


def wide_table(positions, period):
    return np.concatenate(tables(positions, period), 1).astype(np.float32)


def step_table():
    cosine, sine = tables(np.arange(STEP), MASK)
    return bfloat(np.concatenate([cosine, -sine], 1) / MASK)


def step_phases():
    return wide_table(np.arange(STEPS) * STEP, MASK)


def coarse_map():
    cosine, sine = tables(np.arange(COARSE), COARSE)
    upper = np.concatenate([cosine.T, sine.T], 1)
    lower = np.concatenate([-sine.T, cosine.T], 1)
    return bfloat(np.concatenate([upper, lower], 0))


def interpolation():
    ratio = GRID // COARSE
    frequency = np.arange(1, COARSE // 2)
    offset = np.arange(GRID)
    profile = 1.0 + 2.0 * np.cos(2.0 * math.pi * (np.outer(offset, frequency) % GRID) / GRID).sum(1)
    profile = (profile + np.cos(math.pi * offset / ratio)) / COARSE
    matrix = profile[(offset[None, :] - ratio * np.arange(COARSE)[:, None]) % GRID]
    high = bfloat(matrix)
    low = bfloat(matrix - high.astype(np.float64))
    return high, low


def shifted_table(base, shift):
    cosine = base[:, :BAND] * shift[:, :BAND] - base[:, BAND:] * shift[:, BAND:]
    sine = base[:, BAND:] * shift[:, :BAND] + base[:, :BAND] * shift[:, BAND:]
    return jnp.concatenate([cosine, sine], 1)


def whole_spec(shape):
    return pl.BlockSpec(shape, lambda i: (0,) * len(shape))


def params():
    return pltpu.CompilerParams(vmem_limit_bytes=VMEM_LIMIT)


def store_tiles(out_ref, value, row, column):
    for i in range(value.shape[0] // 8):
        for j in range(value.shape[1] // 128):
            out_ref[(row // 8 + i) * 4 + column // 128 + j] = value[8 * i : 8 * i + 8, 128 * j : 128 * j + 128]


def load_tiles(tiles_ref, held_ref):
    for i in range(32):
        for j in range(4):
            held_ref[8 * i : 8 * i + 8, 128 * j : 128 * j + 128] = tiles_ref[4 * i + j]


def spectrum_kernel(mask_ref, step_ref, phase_ref, rows_ref, out_ref, acc_ref):
    index = pl.program_id(0)
    per = mask_ref.shape[1] // STEP

    @pl.when(index == 0)
    def _():
        acc_ref[...] = jnp.zeros_like(acc_ref)

    for part in range(per):
        transmit = jnp.tanh(mask_ref[:, part * STEP : (part + 1) * STEP]).astype(jnp.bfloat16)
        product = jnp.dot(transmit, step_ref[...], preferred_element_type=jnp.float32)
        first = product[:, :BAND]
        second = product[:, BAND:]
        phase = phase_ref[pl.ds(index * per + part, 1), :]
        cosine = phase[:, :BAND]
        sine = phase[:, BAND:]
        acc_ref[:, :BAND] += first * cosine + second * sine
        acc_ref[:, BAND:] += second * cosine - first * sine

    @pl.when(index == pl.num_programs(0) - 1)
    def _():
        product = lax.dot_general(
            rows_ref[...],
            acc_ref[...],
            (((0,), (0,)), ((), ())),
            precision=HIGHEST,
            preferred_element_type=jnp.float32,
        )
        store_tiles(out_ref, product[:BAND, :BAND] + product[BAND:, BAND:], 0, 0)
        store_tiles(out_ref, product[:BAND, BAND:] - product[BAND:, :BAND], 0, BAND)


def mask_spectrum(mask_params, step_value, phases, mask_rows):
    rows = mask_params.shape[0]
    width = 2048
    return pl.pallas_call(
        spectrum_kernel,
        grid=(MASK // width,),
        in_specs=[
            pl.BlockSpec((rows, width), lambda i: (0, i)),
            whole_spec(step_value.shape),
            whole_spec(phases.shape),
            whole_spec(mask_rows.shape),
        ],
        out_specs=whole_spec((DEVICES, 8, 128)),
        out_shape=jax.ShapeDtypeStruct((DEVICES, 8, 128), jnp.float32),
        scratch_shapes=[pltpu.VMEM((rows, 2 * BAND), jnp.float32)],
        compiler_params=params(),
        name="mask_spectrum",
    )(mask_params, step_value, phases, mask_rows)


def field_kernel(tiles_ref, pupil_ref, rows_ref, map_ref, field_ref, power_ref, spec_ref, sum_ref):
    index = pl.program_id(0)

    @pl.when(index == 0)
    def _():
        load_tiles(tiles_ref, spec_ref)

    spec_re = spec_ref[:, :BAND]
    spec_im = spec_ref[:, BAND:]
    kernel_re = pupil_ref[0, 0]
    kernel_im = pupil_ref[0, 1]
    amp_re = kernel_re * spec_re - kernel_im * spec_im
    amp_im = kernel_re * spec_im + kernel_im * spec_re
    block = jnp.concatenate(
        [jnp.concatenate([amp_re, amp_im], 1), jnp.concatenate([-amp_im, amp_re], 1)], 0
    ).astype(jnp.bfloat16)
    partial = jnp.dot(rows_ref[...], block, preferred_element_type=jnp.float32).astype(jnp.bfloat16)
    field = jnp.dot(partial, map_ref[...], preferred_element_type=jnp.float32)
    field_ref[0] = field
    power = field[:, :COARSE] * field[:, :COARSE] + field[:, COARSE:] * field[:, COARSE:]
    corner = index % 2

    @pl.when(index < 2)
    def _():
        sum_ref[corner] = power

    @pl.when(index >= 2)
    def _():
        total = (sum_ref[corner] + power).astype(jnp.bfloat16)
        slab = total.shape[0] // KERN
        for owner in range(KERN):
            power_ref[owner, corner] = total[owner * slab : (owner + 1) * slab]


def coarse_fields(tiles, pupils, rows_table, column_map):
    pairs = pupils.shape[0]
    rows = rows_table.shape[0]
    return pl.pallas_call(
        field_kernel,
        grid=(pairs,),
        in_specs=[
            whole_spec(tiles.shape),
            pl.BlockSpec((1, 2, BAND, BAND), lambda i: (i, 0, 0, 0)),
            whole_spec(rows_table.shape),
            whole_spec(column_map.shape),
        ],
        out_specs=[
            pl.BlockSpec((1, rows, 2 * COARSE), lambda i: (i, 0, 0)),
            whole_spec((KERN, 2, rows // KERN, COARSE)),
        ],
        out_shape=[
            jax.ShapeDtypeStruct((pairs, rows, 2 * COARSE), jnp.float32),
            jax.ShapeDtypeStruct((KERN, 2, rows // KERN, COARSE), jnp.bfloat16),
        ],
        scratch_shapes=[
            pltpu.VMEM((BAND, 2 * BAND), jnp.float32),
            pltpu.VMEM((2, rows, COARSE), jnp.float32),
        ],
        compiler_params=params(),
        name="coarse_fields",
    )(tiles, pupils, rows_table, column_map)


def adjoint_kernel(parts_ref, target_ref, high_ref, low_ref, out_ref, power_ref, acc_ref):
    index = pl.program_id(0)
    rows = parts_ref.shape[2]

    @pl.when(index == 0)
    def _():
        total = parts_ref[0].astype(jnp.float32)
        for owner in range(1, KERN):
            total = total + parts_ref[owner].astype(jnp.float32)
        total = total.reshape(2 * rows, COARSE)
        high = total.astype(jnp.bfloat16)
        power_ref[: 2 * rows] = high
        power_ref[2 * rows :] = (total - high.astype(jnp.float32)).astype(jnp.bfloat16)
        acc_ref[...] = jnp.zeros_like(acc_ref)

    both = jnp.dot(power_ref[...], high_ref[...], preferred_element_type=jnp.float32)
    rest = jnp.dot(power_ref[: 2 * rows], low_ref[...], preferred_element_type=jnp.float32)
    fine = both[: 2 * rows] + (both[2 * rows :] + rest)
    wanted = target_ref[...].astype(jnp.float32)
    corners = []
    for corner in range(2):
        dose = dose_levels[corner]
        resist = jax.nn.sigmoid(steepness * (dose * fine[corner * rows : (corner + 1) * rows] - threshold))
        corners.append(
            (2.0 * (resist - wanted) * resist * (1.0 - resist) * steepness * dose).astype(jnp.bfloat16)
        )
    adjoint = jnp.concatenate(corners, 0)
    contract = (((1,), (1,)), ((), ()))
    acc_ref[...] += lax.dot_general(
        adjoint, high_ref[...], contract, preferred_element_type=jnp.float32
    ) + lax.dot_general(adjoint, low_ref[...], contract, preferred_element_type=jnp.float32)

    @pl.when(index == pl.num_programs(0) - 1)
    def _():
        out_ref[...] = acc_ref[...].reshape(2, rows, COARSE).astype(jnp.bfloat16)


def coarse_adjoint(parts, target, high, low):
    rows = target.shape[0]
    width = 512
    return pl.pallas_call(
        adjoint_kernel,
        grid=(GRID // width,),
        in_specs=[
            whole_spec(parts.shape),
            pl.BlockSpec((rows, width), lambda i: (0, i)),
            pl.BlockSpec((COARSE, width), lambda i: (0, i)),
            pl.BlockSpec((COARSE, width), lambda i: (0, i)),
        ],
        out_specs=whole_spec((2, rows, COARSE)),
        out_shape=jax.ShapeDtypeStruct((2, rows, COARSE), jnp.bfloat16),
        scratch_shapes=[
            pltpu.VMEM((4 * rows, COARSE), jnp.bfloat16),
            pltpu.VMEM((2 * rows, COARSE), jnp.float32),
        ],
        compiler_params=params(),
        name="coarse_adjoint",
    )(parts, target, high, low)


def gradient_kernel(field_ref, adjoint_ref, pupil_ref, rows_ref, map_ref, out_ref, acc_ref):
    index = pl.program_id(0)
    corner = index % 2

    @pl.when(index == 0)
    def _():
        acc_ref[...] = jnp.zeros_like(acc_ref)

    adjoint = jnp.concatenate([adjoint_ref[owner, corner] for owner in range(KERN)], 0)
    adjoint = 2.0 * adjoint.astype(jnp.float32)
    field = field_ref[0]
    weighted = jnp.concatenate(
        [field[:, :COARSE] * adjoint, field[:, COARSE:] * adjoint], 1
    ).astype(jnp.bfloat16)
    back = lax.dot_general(
        weighted, map_ref[...], (((1,), (1,)), ((), ())), preferred_element_type=jnp.float32
    ).astype(jnp.bfloat16)
    grads = lax.dot_general(
        rows_ref[...], back, (((0,), (0,)), ((), ())), preferred_element_type=jnp.float32
    )
    grad_re = grads[:BAND, :BAND] + grads[BAND:, BAND:]
    grad_im = grads[:BAND, BAND:] - grads[BAND:, :BAND]
    kernel_re = pupil_ref[0, 0]
    kernel_im = pupil_ref[0, 1]
    acc_ref[:, :BAND] += kernel_re * grad_re + kernel_im * grad_im
    acc_ref[:, BAND:] += kernel_re * grad_im - kernel_im * grad_re

    @pl.when(index == pl.num_programs(0) - 1)
    def _():
        store_tiles(out_ref, acc_ref[...], 0, 0)


def spectrum_gradient(fields, adjoint, pupils, rows_table, column_map):
    pairs, rows, _ = fields.shape
    return pl.pallas_call(
        gradient_kernel,
        grid=(pairs,),
        in_specs=[
            pl.BlockSpec((1, rows, 2 * COARSE), lambda i: (i, 0, 0)),
            whole_spec(adjoint.shape),
            pl.BlockSpec((1, 2, BAND, BAND), lambda i: (i, 0, 0, 0)),
            whole_spec(rows_table.shape),
            whole_spec(column_map.shape),
        ],
        out_specs=whole_spec((DEVICES, 8, 128)),
        out_shape=jax.ShapeDtypeStruct((DEVICES, 8, 128), jnp.float32),
        scratch_shapes=[pltpu.VMEM((BAND, 2 * BAND), jnp.float32)],
        compiler_params=params(),
        name="spectrum_gradient",
    )(fields, adjoint, pupils, rows_table, column_map)


def update_kernel(tiles_ref, rows_ref, mask_ref, step_ref, phase_ref, out_ref, held_ref, column_ref):
    index = pl.program_id(0)
    per = mask_ref.shape[1] // STEP

    @pl.when(index == 0)
    def _():
        load_tiles(tiles_ref, held_ref)
        rows = rows_ref[...]
        product_cos = jnp.dot(
            rows[:, :BAND], held_ref[...], precision=HIGHEST, preferred_element_type=jnp.float32
        )
        product_sin = jnp.dot(
            rows[:, BAND:], held_ref[...], precision=HIGHEST, preferred_element_type=jnp.float32
        )
        column_ref[:, :BAND] = product_cos[:, :BAND] - product_sin[:, BAND:]
        column_ref[:, BAND:] = product_sin[:, :BAND] + product_cos[:, BAND:]

    for part in range(per):
        phase = phase_ref[pl.ds(index * per + part, 1), :]
        cosine = phase[:, :BAND]
        sine = phase[:, BAND:]
        col_re = column_ref[:, :BAND]
        col_im = column_ref[:, BAND:]
        turned = jnp.concatenate(
            [
                (col_re * cosine - col_im * sine).astype(jnp.bfloat16),
                (col_re * sine + col_im * cosine).astype(jnp.bfloat16),
            ],
            1,
        )
        pixel_grad = lax.dot_general(
            turned, step_ref[...], (((1,), (1,)), ((), ())), preferred_element_type=jnp.float32
        )
        mask = mask_ref[:, part * STEP : (part + 1) * STEP]
        transmit = jnp.tanh(mask)
        out_ref[:, part * STEP : (part + 1) * STEP] = mask - step_size * pixel_grad * (
            1.0 - transmit * transmit
        )


def mask_update(tiles, mask_rows, mask_params, step_value, phases):
    rows = mask_params.shape[0]
    width = 2048
    return pl.pallas_call(
        update_kernel,
        grid=(MASK // width,),
        in_specs=[
            whole_spec(tiles.shape),
            whole_spec(mask_rows.shape),
            pl.BlockSpec((rows, width), lambda i: (0, i)),
            whole_spec(step_value.shape),
            whole_spec(phases.shape),
        ],
        out_specs=pl.BlockSpec((rows, width), lambda i: (0, i)),
        out_shape=jax.ShapeDtypeStruct((rows, MASK), jnp.float32),
        scratch_shapes=[
            pltpu.VMEM((BAND, 2 * BAND), jnp.float32),
            pltpu.VMEM((rows, 2 * BAND), jnp.float32),
        ],
        compiler_params=params(),
        name="mask_update",
    )(tiles, mask_rows, mask_params, step_value, phases)


def exchange(values, axes):
    return lax.all_to_all(values, axes, 0, 0, tiled=True)


def sum_tiles(tiles):
    everyone = ("rows", "kern")
    own = jnp.sum(exchange(tiles, everyone), 0, keepdims=True)
    return exchange(jnp.broadcast_to(own, tiles.shape), everyone)


def local(mask_params, pupil_kernels, target_pattern):
    rows = mask_params.shape[0]
    device = lax.axis_index(("rows", "kern"))
    grid_rows, slab_cols = target_pattern.shape
    slab_rows = grid_rows // KERN
    target = exchange(target_pattern.astype(jnp.bfloat16).reshape(KERN, slab_rows, slab_cols), "kern")
    target = jnp.transpose(target, (1, 0, 2)).reshape(slab_rows, GRID)

    step_value = jnp.asarray(step_table())
    phases = jnp.asarray(step_phases())
    mask_rows = shifted_table(
        jnp.asarray(wide_table(np.arange(rows), MASK)),
        lax.dynamic_slice_in_dim(jnp.asarray(wide_table(np.arange(DEVICES) * rows, MASK)), device, 1, 0),
    )
    rows_table = shifted_table(
        jnp.asarray(wide_table(np.arange(grid_rows), GRID)),
        lax.dynamic_slice_in_dim(
            jnp.asarray(wide_table(np.arange(ROWS) * grid_rows, GRID)), lax.axis_index("rows"), 1, 0
        ),
    ).astype(jnp.bfloat16)
    column_map = jnp.asarray(coarse_map())
    high, low = interpolation()

    spectrum = sum_tiles(mask_spectrum(mask_params, step_value, phases, mask_rows))
    pupils = pupil_kernels.reshape(-1, 2, BAND, BAND)
    fields, powers = coarse_fields(spectrum, pupils, rows_table, column_map)
    parts = exchange(powers, "kern")
    slab_adjoint = coarse_adjoint(parts, target, jnp.asarray(high), jnp.asarray(low))
    adjoint = exchange(jnp.broadcast_to(slab_adjoint[None], (KERN,) + slab_adjoint.shape), "kern")
    gradient = sum_tiles(spectrum_gradient(fields, adjoint, pupils, rows_table, column_map))
    return mask_update(gradient, mask_rows, mask_params, step_value, phases)


def solution(mesh):
    placed = (P(("rows", "kern"), None), P("kern", None, None, None, None), P("rows", "kern"))
    return jax.shard_map(
        local, mesh=mesh, in_specs=placed, out_specs=P(("rows", "kern"), None), check_vma=False
    )
```

```python
import math

import jax
import jax.numpy as jnp
import numpy as np
from jax import lax
from jax.experimental import pallas as pl
from jax.experimental.pallas import tpu as pltpu
from jax.sharding import PartitionSpec as P

MASK = 16384
GRID = 4096
BAND = 256
COARSE = 512
STEP = 256
STEPS = MASK // STEP
ROWS = 16
KERN = 8
DEVICES = ROWS * KERN

steepness = 4.0
threshold = 0.75
step_size = 1.0
dose_levels = (1.0, 1.15)

VMEM_LIMIT = 24 * 1024 * 1024
STREAM_LIMIT = 60 * 1024 * 1024
HIGHEST = lax.Precision.HIGHEST


def tables(positions, period):
    frequency = np.arange(BAND) - BAND // 2
    angles = (np.outer(positions, frequency) % period) * (2.0 * math.pi / period)
    return np.cos(angles), np.sin(angles)


def bfloat(values):
    return np.asarray(values, np.float32).astype(jnp.bfloat16)


def wide_table(positions, period):
    return np.concatenate(tables(positions, period), 1).astype(np.float32)


def step_table():
    cosine, sine = tables(np.arange(STEP), MASK)
    return bfloat(np.concatenate([cosine, -sine], 1) / MASK)


def step_phases():
    return wide_table(np.arange(STEPS) * STEP, MASK)


def coarse_map():
    cosine, sine = tables(np.arange(COARSE), COARSE)
    upper = np.concatenate([cosine.T, sine.T], 1)
    lower = np.concatenate([-sine.T, cosine.T], 1)
    return bfloat(np.concatenate([upper, lower], 0))


def interpolation():
    ratio = GRID // COARSE
    frequency = np.arange(1, COARSE // 2)
    offset = np.arange(GRID)
    profile = 1.0 + 2.0 * np.cos(2.0 * math.pi * (np.outer(offset, frequency) % GRID) / GRID).sum(1)
    profile = (profile + np.cos(math.pi * offset / ratio)) / COARSE
    matrix = profile[(offset[None, :] - ratio * np.arange(COARSE)[:, None]) % GRID]
    return bfloat(matrix)


def shifted_table(base_ref, shift):
    cosine = base_ref[:, :BAND] * shift[:, :BAND] - base_ref[:, BAND:] * shift[:, BAND:]
    sine = base_ref[:, BAND:] * shift[:, :BAND] + base_ref[:, :BAND] * shift[:, BAND:]
    return cosine, sine


def mask_table(base_ref, shift_ref):
    device = lax.axis_index("rows") * KERN + lax.axis_index("kern")
    return shifted_table(base_ref, shift_ref[pl.ds(device, 1), :])


def grid_table(base_ref, shift_ref):
    cosine, sine = shifted_table(base_ref, shift_ref[pl.ds(lax.axis_index("rows"), 1), :])
    return jnp.concatenate([cosine, sine], 1).astype(jnp.bfloat16)


def whole_spec(shape):
    return pl.BlockSpec(shape, lambda i: (0,) * len(shape))


def params(limit=VMEM_LIMIT):
    return pltpu.CompilerParams(vmem_limit_bytes=limit)


def kern_place(shift):
    return lax.rem(lax.axis_index("kern") + (shift + KERN), KERN)


def float_dot(left, right):
    return jnp.dot(left, right, preferred_element_type=jnp.float32)


def split(values):
    high = values.astype(jnp.bfloat16)
    return high, (values - high.astype(jnp.float32)).astype(jnp.bfloat16)


def store_tiles(out_ref, value, row, column):
    for i in range(value.shape[0] // 8):
        for j in range(value.shape[1] // 128):
            out_ref[(row // 8 + i) * 4 + column // 128 + j] = value[
                8 * i : 8 * i + 8, 128 * j : 128 * j + 128
            ].astype(out_ref.dtype)


def load_tiles(tiles_ref, held_ref):
    for i in range(BAND // 8):
        for j in range(4):
            held_ref[8 * i : 8 * i + 8, 128 * j : 128 * j + 128] = tiles_ref[4 * i + j].astype(jnp.float32)


def spectrum_kernel(mask_ref, step_ref, phase_ref, base_ref, shift_ref, target_ref, out_ref, *refs):
    wanted_refs = refs[:KERN]
    stack_ref, product_ref, acc_ref = refs[KERN:]
    index = pl.program_id(0)
    rows = mask_ref.shape[0]
    per = mask_ref.shape[1] // STEP

    @pl.when(index == 0)
    def _():
        acc_ref[...] = jnp.zeros_like(acc_ref)
        slab = target_ref.shape[0] // KERN
        for shift in range(KERN):
            at = pl.multiple_of(kern_place(shift) * slab, slab)
            wanted_refs[shift][...] = target_ref[pl.ds(at, slab), :].astype(jnp.float32).astype(jnp.bfloat16)

    for part in range(per):
        stack_ref[part * rows : (part + 1) * rows] = jnp.tanh(
            mask_ref[:, part * STEP : (part + 1) * STEP]
        ).astype(jnp.bfloat16)
    product_ref[...] = float_dot(stack_ref[...], step_ref[...])
    chunk = 32
    for start in range(0, rows, chunk):
        total_re = acc_ref[start : start + chunk, :BAND]
        total_im = acc_ref[start : start + chunk, BAND:]
        for part in range(per):
            phase = phase_ref[pl.ds(index * per + part, 1), :]
            cosine = phase[:, :BAND]
            sine = phase[:, BAND:]
            at = part * rows + start
            first = product_ref[at : at + chunk, :BAND]
            second = product_ref[at : at + chunk, BAND:]
            total_re = total_re + (first * cosine + second * sine)
            total_im = total_im + (second * cosine - first * sine)
        acc_ref[start : start + chunk, :BAND] = total_re
        acc_ref[start : start + chunk, BAND:] = total_im

    @pl.when(index == pl.num_programs(0) - 1)
    def _():
        table = jnp.concatenate(mask_table(base_ref, shift_ref), 1)
        product = lax.dot_general(
            table,
            acc_ref[...],
            (((0,), (0,)), ((), ())),
            precision=HIGHEST,
            preferred_element_type=jnp.float32,
        )
        store_tiles(out_ref, product[:BAND, :BAND] + product[BAND:, BAND:], 0, 0)
        store_tiles(out_ref, product[:BAND, BAND:] - product[BAND:, :BAND], 0, BAND)


def mask_spectrum(mask_params, step_value, phases, base, shifts, target):
    rows = mask_params.shape[0]
    chunk = (target.shape[0] // KERN, target.shape[1])
    width = 2048
    stacked = rows * (width // STEP)
    return pl.pallas_call(
        spectrum_kernel,
        grid=(MASK // width,),
        in_specs=[
            pl.BlockSpec((rows, width), lambda i: (0, i)),
            whole_spec(step_value.shape),
            whole_spec(phases.shape),
            whole_spec(base.shape),
            whole_spec(shifts.shape),
            whole_spec(target.shape),
        ],
        out_specs=[whole_spec((DEVICES, 8, 128))] + [whole_spec(chunk)] * KERN,
        out_shape=[jax.ShapeDtypeStruct((DEVICES, 8, 128), jnp.bfloat16)]
        + [jax.ShapeDtypeStruct(chunk, jnp.bfloat16)] * KERN,
        scratch_shapes=[
            pltpu.VMEM((stacked, STEP), jnp.bfloat16),
            pltpu.VMEM((stacked, 2 * BAND), jnp.float32),
            pltpu.VMEM((rows, 2 * BAND), jnp.float32),
        ],
        compiler_params=params(STREAM_LIMIT),
        name="mask_spectrum",
    )(mask_params, step_value, phases, base, shifts, target)


def field_kernel(
    tiles_ref, pupil_ref, base_ref, shift_ref, map_ref, field_ref, power_ref,
    spec_ref, rows_ref, partial_ref, sum_ref,
):
    index = pl.program_id(0)
    rows = base_ref.shape[0]
    slab = rows // KERN

    @pl.when(index == 0)
    def _():
        load_tiles(tiles_ref, spec_ref)
        rows_ref[...] = grid_table(base_ref, shift_ref)

    spec_re = spec_ref[:, :BAND]
    spec_im = spec_ref[:, BAND:]
    for corner in range(2):
        kernel_re = pupil_ref[0, corner, 0]
        kernel_im = pupil_ref[0, corner, 1]
        amp_re = (kernel_re * spec_re - kernel_im * spec_im).astype(jnp.bfloat16)
        amp_im = (kernel_re * spec_im + kernel_im * spec_re).astype(jnp.bfloat16)
        block = jnp.concatenate(
            [jnp.concatenate([amp_re, amp_im], 1), jnp.concatenate([-amp_im, amp_re], 1)], 0
        )
        partial_ref[corner * rows : (corner + 1) * rows] = float_dot(rows_ref[...], block).astype(
            jnp.bfloat16
        )
    field_ref[0] = float_dot(partial_ref[...], map_ref[...])

    for corner in range(2):
        for owner in range(KERN):
            at = corner * rows + owner * slab
            real = field_ref[0, at : at + slab, :COARSE]
            imag = field_ref[0, at : at + slab, COARSE:]
            power = real * real + imag * imag

            @pl.when(index == 0)
            def _():
                sum_ref[at : at + slab] = power

            @pl.when(index == 1)
            def _():
                power_ref[owner, corner] = (sum_ref[at : at + slab] + power).astype(jnp.bfloat16)


def coarse_fields(tiles, pupils, base, shifts, column_map):
    members = pupils.shape[0]
    rows = base.shape[0]
    return pl.pallas_call(
        field_kernel,
        grid=(members,),
        in_specs=[
            whole_spec(tiles.shape),
            pl.BlockSpec((1, 2, 2, BAND, BAND), lambda i: (i, 0, 0, 0, 0)),
            whole_spec(base.shape),
            whole_spec(shifts.shape),
            whole_spec(column_map.shape),
        ],
        out_specs=[
            pl.BlockSpec((1, 2 * rows, 2 * COARSE), lambda i: (i, 0, 0)),
            whole_spec((KERN, 2, rows // KERN, COARSE)),
        ],
        out_shape=[
            jax.ShapeDtypeStruct((members, 2 * rows, 2 * COARSE), jnp.float32),
            jax.ShapeDtypeStruct((KERN, 2, rows // KERN, COARSE), jnp.bfloat16),
        ],
        scratch_shapes=[
            pltpu.VMEM((BAND, 2 * BAND), jnp.float32),
            pltpu.VMEM((rows, 2 * BAND), jnp.bfloat16),
            pltpu.VMEM((2 * rows, 2 * BAND), jnp.bfloat16),
            pltpu.VMEM((2 * rows, COARSE), jnp.float32),
        ],
        compiler_params=params(),
        name="coarse_fields",
    )(tiles, pupils, base, shifts, column_map)


def adjoint_kernel(parts_ref, matrix_ref, *refs):
    wanted_refs = refs[:KERN]
    out_ref, power_ref, acc_ref, wanted_ref = refs[KERN:]
    index = pl.program_id(0)
    rows = parts_ref.shape[2]

    @pl.when(index == 0)
    def _():
        for shift in range(KERN):
            wanted_ref[kern_place(-shift)] = wanted_refs[shift][...]
        for corner in range(2):
            total = parts_ref[0, corner].astype(jnp.float32)
            for owner in range(1, KERN):
                total = total + parts_ref[owner, corner].astype(jnp.float32)
            power_ref[corner * rows : (corner + 1) * rows] = total.astype(jnp.bfloat16)
        acc_ref[...] = jnp.zeros_like(acc_ref)

    fine = float_dot(power_ref[...], matrix_ref[...])
    wanted = wanted_ref[index].astype(jnp.float32)
    corners = []
    for corner in range(2):
        dose = dose_levels[corner]
        resist = jax.nn.sigmoid(steepness * (dose * fine[corner * rows : (corner + 1) * rows] - threshold))
        corners.append(
            (2.0 * (resist - wanted) * resist * (1.0 - resist) * steepness * dose).astype(jnp.bfloat16)
        )
    acc_ref[...] += lax.dot_general(
        jnp.concatenate(corners, 0),
        matrix_ref[...],
        (((1,), (1,)), ((), ())),
        preferred_element_type=jnp.float32,
    )

    @pl.when(index == pl.num_programs(0) - 1)
    def _():
        out_ref[...] = acc_ref[...].reshape(2, rows, COARSE).astype(jnp.bfloat16)


def coarse_adjoint(parts, matrix, wanted):
    rows = parts.shape[2]
    width = GRID // KERN
    return pl.pallas_call(
        adjoint_kernel,
        grid=(KERN,),
        in_specs=[
            whole_spec(parts.shape),
            pl.BlockSpec((COARSE, width), lambda i: (0, i)),
        ]
        + [whole_spec(wanted[0].shape)] * KERN,
        out_specs=whole_spec((2, rows, COARSE)),
        out_shape=jax.ShapeDtypeStruct((2, rows, COARSE), jnp.bfloat16),
        scratch_shapes=[
            pltpu.VMEM((2 * rows, COARSE), jnp.bfloat16),
            pltpu.VMEM((2 * rows, COARSE), jnp.float32),
            pltpu.VMEM((KERN,) + wanted[0].shape, jnp.bfloat16),
        ],
        compiler_params=params(),
        name="coarse_adjoint",
    )(parts, matrix, *wanted)


def gradient_kernel(field_ref, pupil_ref, base_ref, shift_ref, map_ref, *refs):
    adjoint_refs = refs[:KERN]
    out_ref, rows_ref, weighted_ref, back_ref, acc_ref, adjoint_ref = refs[KERN:]
    index = pl.program_id(0)
    slab = adjoint_ref.shape[2]
    rows = slab * KERN

    @pl.when(index == 0)
    def _():
        acc_ref[...] = jnp.zeros_like(acc_ref)
        rows_ref[...] = grid_table(base_ref, shift_ref)
        for shift in range(KERN):
            adjoint_ref[kern_place(-shift)] = adjoint_refs[shift][...]

    for corner in range(2):
        for owner in range(KERN):
            at = corner * rows + owner * slab
            adjoint = 2.0 * adjoint_ref[owner, corner].astype(jnp.float32)
            for half in range(2):
                columns = slice(half * COARSE, (half + 1) * COARSE)
                weighted_ref[at : at + slab, columns] = (field_ref[0, at : at + slab, columns] * adjoint).astype(
                    jnp.bfloat16
                )
    back_ref[...] = lax.dot_general(
        weighted_ref[...], map_ref[...], (((1,), (1,)), ((), ())), preferred_element_type=jnp.float32
    ).astype(jnp.bfloat16)
    for corner in range(2):
        grads = lax.dot_general(
            rows_ref[...],
            back_ref[corner * rows : (corner + 1) * rows],
            (((0,), (0,)), ((), ())),
            preferred_element_type=jnp.float32,
        )
        grad_re = grads[:BAND, :BAND] + grads[BAND:, BAND:]
        grad_im = grads[:BAND, BAND:] - grads[BAND:, :BAND]
        kernel_re = pupil_ref[0, corner, 0]
        kernel_im = pupil_ref[0, corner, 1]
        acc_ref[:, :BAND] += kernel_re * grad_re + kernel_im * grad_im
        acc_ref[:, BAND:] += kernel_re * grad_im - kernel_im * grad_re

    @pl.when(index == pl.num_programs(0) - 1)
    def _():
        store_tiles(out_ref, acc_ref[...], 0, 0)


def spectrum_gradient(fields, adjoint, pupils, base, shifts, column_map):
    members = pupils.shape[0]
    slab = adjoint[0].shape
    rows = slab[1] * KERN
    return pl.pallas_call(
        gradient_kernel,
        grid=(members,),
        in_specs=[
            pl.BlockSpec((1, 2 * rows, 2 * COARSE), lambda i: (i, 0, 0)),
            pl.BlockSpec((1, 2, 2, BAND, BAND), lambda i: (i, 0, 0, 0, 0)),
            whole_spec(base.shape),
            whole_spec(shifts.shape),
            whole_spec(column_map.shape),
        ]
        + [whole_spec(slab)] * KERN,
        out_specs=whole_spec((DEVICES, 8, 128)),
        out_shape=jax.ShapeDtypeStruct((DEVICES, 8, 128), jnp.bfloat16),
        scratch_shapes=[
            pltpu.VMEM((rows, 2 * BAND), jnp.bfloat16),
            pltpu.VMEM((2 * rows, 2 * COARSE), jnp.bfloat16),
            pltpu.VMEM((2 * rows, 2 * BAND), jnp.bfloat16),
            pltpu.VMEM((BAND, 2 * BAND), jnp.float32),
            pltpu.VMEM((KERN,) + slab, jnp.bfloat16),
        ],
        compiler_params=params(),
        name="spectrum_gradient",
    )(fields, pupils, base, shifts, column_map, *adjoint)


def update_kernel(
    tiles_ref, base_ref, shift_ref, mask_ref, step_ref, phase_ref, out_ref, held_ref, column_ref, stack_ref, product_ref
):
    index = pl.program_id(0)
    rows = mask_ref.shape[0]
    per = mask_ref.shape[1] // STEP

    @pl.when(index == 0)
    def _():
        cosine, sine = mask_table(base_ref, shift_ref)
        table = jnp.concatenate(split(cosine) + split(sine), 0)
        load_tiles(tiles_ref, held_ref)
        product = float_dot(table, held_ref[...].astype(jnp.bfloat16))
        by_cos = product[:rows] + product[rows : 2 * rows]
        by_sin = product[2 * rows : 3 * rows] + product[3 * rows :]
        column_ref[:, :BAND] = by_cos[:, :BAND] - by_sin[:, BAND:]
        column_ref[:, BAND:] = by_sin[:, :BAND] + by_cos[:, BAND:]

    chunk = 32
    for start in range(0, rows, chunk):
        col_re = column_ref[start : start + chunk, :BAND]
        col_im = column_ref[start : start + chunk, BAND:]
        for part in range(per):
            phase = phase_ref[pl.ds(index * per + part, 1), :]
            cosine = phase[:, :BAND]
            sine = phase[:, BAND:]
            at = part * rows + start
            stack_ref[at : at + chunk, :BAND] = (col_re * cosine - col_im * sine).astype(jnp.bfloat16)
            stack_ref[at : at + chunk, BAND:] = (col_re * sine + col_im * cosine).astype(jnp.bfloat16)
    product_ref[...] = float_dot(stack_ref[...], step_ref[...])
    for part in range(per):
        columns = slice(part * STEP, (part + 1) * STEP)
        mask = mask_ref[:, columns]
        transmit = jnp.tanh(mask)
        out_ref[:, columns] = mask - step_size * product_ref[part * rows : (part + 1) * rows] * (
            1.0 - transmit * transmit
        )


def mask_update(gradient, base, shifts, mask_params, step_value, phases):
    rows = mask_params.shape[0]
    width = 2048
    stacked = rows * (width // STEP)
    return pl.pallas_call(
        update_kernel,
        grid=(MASK // width,),
        in_specs=[
            whole_spec(gradient.shape),
            whole_spec(base.shape),
            whole_spec(shifts.shape),
            pl.BlockSpec((rows, width), lambda i: (0, i)),
            whole_spec(step_value.shape),
            whole_spec(phases.shape),
        ],
        out_specs=pl.BlockSpec((rows, width), lambda i: (0, i)),
        out_shape=jax.ShapeDtypeStruct((rows, MASK), jnp.float32),
        scratch_shapes=[
            pltpu.VMEM((BAND, 2 * BAND), jnp.float32),
            pltpu.VMEM((rows, 2 * BAND), jnp.float32),
            pltpu.VMEM((stacked, 2 * BAND), jnp.bfloat16),
            pltpu.VMEM((stacked, STEP), jnp.float32),
        ],
        compiler_params=params(STREAM_LIMIT),
        name="mask_update",
    )(gradient, base, shifts, mask_params, step_value, phases)


def exchange(values, axes):
    return lax.all_to_all(values, axes, 0, 0, tiled=True)


def summed(parts, copies, dtype):
    total = jnp.sum(parts.astype(jnp.float32), 0).astype(dtype)
    return jnp.broadcast_to(total[None], (copies,) + total.shape)


def sum_tiles(tiles):
    everyone = ("rows", "kern")
    return exchange(summed(exchange(tiles, everyone), DEVICES, jnp.bfloat16), everyone)


def shifted(values, shift):
    return lax.ppermute(values, "kern", [(place, (place + shift) % KERN) for place in range(KERN)])


def local(mask_params, pupil_kernels, target_pattern):
    rows = mask_params.shape[0]
    grid_rows = target_pattern.shape[0]
    step_value = step_table()
    phases = jnp.asarray(step_phases())
    mask_base = jnp.asarray(wide_table(np.arange(rows), MASK))
    mask_shifts = jnp.asarray(wide_table(np.arange(DEVICES) * rows, MASK))
    grid_base = jnp.asarray(wide_table(np.arange(grid_rows), GRID))
    grid_shifts = jnp.asarray(wide_table(np.arange(ROWS) * grid_rows, GRID))
    column_map = jnp.asarray(coarse_map())

    tiles, *wanted = mask_spectrum(
        mask_params, jnp.asarray(step_value), phases, mask_base, mask_shifts, target_pattern
    )
    wanted = wanted[:1] + [shifted(wanted[shift], shift) for shift in range(1, KERN)]
    spectrum = sum_tiles(tiles)
    fields, powers = coarse_fields(spectrum, pupil_kernels, grid_base, grid_shifts, column_map)
    slab = coarse_adjoint(exchange(powers, "kern"), jnp.asarray(interpolation()), wanted)
    adjoint = [slab] + [shifted(slab, shift) for shift in range(1, KERN)]
    gradient = sum_tiles(spectrum_gradient(fields, adjoint, pupil_kernels, grid_base, grid_shifts, column_map))
    return mask_update(gradient, mask_base, mask_shifts, mask_params, jnp.asarray(step_value.T), phases)


def solution(mesh):
    placed = (P(("rows", "kern"), None), P("kern", None, None, None, None), P("rows", "kern"))
    return jax.shard_map(
        local, mesh=mesh, in_specs=placed, out_specs=P(("rows", "kern"), None), check_vma=False
    )
```

```python
import math

import jax
import jax.numpy as jnp
import numpy as np
from jax import lax
from jax.experimental import pallas as pl
from jax.experimental.pallas import tpu as pltpu
from jax.sharding import PartitionSpec as P

MASK = 16384
GRID = 4096
BAND = 256
HALF = BAND // 2
COARSE = 512
STEP = 256
STEPS = MASK // STEP
ROWS = 16
KERN = 8
DEVICES = ROWS * KERN
WIDTH = 2048
CHUNKS = MASK // WIDTH
PER = WIDTH // STEP

steepness = 4.0
threshold = 0.75
step_size = 1.0
dose_levels = (1.0, 1.15)

VMEM_LIMIT = 24 * 1024 * 1024
STREAM_LIMIT = 56 * 1024 * 1024
HIGHEST = lax.Precision.HIGHEST


def tables(positions, period, count=BAND):
    frequency = np.arange(count) - BAND // 2
    angles = (np.outer(positions, frequency) % period) * (2.0 * math.pi / period)
    return np.cos(angles), np.sin(angles)


def bfloat(values):
    return np.asarray(values, np.float32).astype(jnp.bfloat16)


def wide_table(positions, period, count=BAND):
    return np.concatenate(tables(positions, period, count), 1).astype(np.float32)


def step_table():
    cosine, sine = tables(np.arange(STEP), MASK, HALF)
    return bfloat(np.concatenate([cosine, -sine], 1) / MASK)


def coarse_map():
    cosine, sine = tables(np.arange(COARSE), COARSE)
    upper = np.concatenate([cosine.T, sine.T], 1)
    lower = np.concatenate([-sine.T, cosine.T], 1)
    return bfloat(np.concatenate([upper, lower], 0))


def interpolation():
    ratio = GRID // COARSE
    frequency = np.arange(1, COARSE // 2)
    offset = np.arange(GRID)
    profile = 1.0 + 2.0 * np.cos(2.0 * math.pi * (np.outer(offset, frequency) % GRID) / GRID).sum(1)
    profile = (profile + np.cos(math.pi * offset / ratio)) / COARSE
    return bfloat(profile[(offset[None, :] - ratio * np.arange(COARSE)[:, None]) % GRID])


def device_place():
    return lax.axis_index("rows") * KERN + lax.axis_index("kern")


def turned_table(base, shift):
    cosine = base[:, :BAND] * shift[:, :BAND] - base[:, BAND:] * shift[:, BAND:]
    sine = base[:, BAND:] * shift[:, :BAND] + base[:, :BAND] * shift[:, BAND:]
    return cosine, sine


def whole_spec(shape):
    return pl.BlockSpec(shape, lambda i: (0,) * len(shape))


def params(limit=VMEM_LIMIT):
    return pltpu.CompilerParams(vmem_limit_bytes=limit)


def float_dot(left, right):
    return jnp.dot(left, right, preferred_element_type=jnp.float32)


def dot_first(left, right, precision=None):
    return lax.dot_general(
        left, right, (((0,), (0,)), ((), ())), precision=precision, preferred_element_type=jnp.float32
    )


def dot_last(left, right):
    return lax.dot_general(left, right, (((1,), (1,)), ((), ())), preferred_element_type=jnp.float32)


def split(values):
    high = values.astype(jnp.bfloat16)
    return high, (values - high.astype(jnp.float32)).astype(jnp.bfloat16)


def iotas(shape):
    return lax.broadcasted_iota(jnp.int32, shape, 0), lax.broadcasted_iota(jnp.int32, shape, 1)


def row_mirror():
    row, column = iotas((BAND, BAND))
    return jnp.where(row + column == BAND, 1.0, 0.0).astype(jnp.bfloat16)


def conjugate_mirror():
    row, column = iotas((BAND, BAND))
    real = (row + column == HALF) & (row < HALF) & (column > 0) & (column < HALF)
    imag = (row + column == 2 * HALF + HALF) & (row >= HALF) & (column > HALF)
    return (jnp.where(real, 1.0, 0.0) - jnp.where(imag, 1.0, 0.0)).astype(jnp.bfloat16)


def diagonal():
    row, column = iotas((BAND, BAND))
    return row == column


def store_tiles(out_ref, real, imag):
    for part, value in enumerate((real, imag)):
        for i in range(BAND // 8):
            for j in range(2):
                out_ref[4 * i + 2 * part + j] = value[8 * i : 8 * i + 8, 128 * j : 128 * j + 128].astype(
                    out_ref.dtype
                )


def load_tiles(tiles_ref, held_ref):
    for part in range(2):
        for i in range(BAND // 8):
            for j in range(2):
                held_ref[part, 8 * i : 8 * i + 8, 128 * j : 128 * j + 128] = tiles_ref[
                    4 * i + 2 * part + j
                ].astype(jnp.float32)


def spectrum_kernel(
    mask_ref, step_ref, phase_ref, base_ref, shift_ref, grid_base_ref, grid_shift_ref, target_ref,
    out_ref, rows_ref, wanted_ref,
    held_ref, steps_ref, phases_ref, bases_ref, shifts_ref, grid_bases_ref, grid_shifts_ref, targets_ref,
    stack_a, stack_b, product_a, product_b, re_ref, im_ref, flat_ref, sems,
):
    rows = mask_ref.shape[0]
    stacks = (stack_a, stack_b)
    products = (product_a, product_b)
    chunks = [
        pltpu.make_async_copy(mask_ref.at[:, pl.ds(i * WIDTH, WIDTH)], held_ref.at[i], sems.at[i])
        for i in range(CHUNKS)
    ]
    small = [
        pltpu.make_async_copy(source, target, sems.at[CHUNKS + i])
        for i, (source, target) in enumerate(
            (
                (step_ref, steps_ref),
                (phase_ref, phases_ref),
                (grid_base_ref, grid_bases_ref),
                (grid_shift_ref.at[lax.axis_index("rows")], grid_shifts_ref),
                (target_ref, targets_ref),
                (base_ref, bases_ref),
                (shift_ref.at[device_place()], shifts_ref),
            )
        )
    ]
    chunks[0].start()
    small[0].start()
    chunks[1].start()
    for copy in small[1:] + chunks[2:]:
        copy.start()

    def transmit(i):
        chunks[i].wait()
        total = jnp.zeros((rows, HALF), jnp.float32)
        for part in range(PER):
            value = jnp.tanh(held_ref[i, :, part * STEP : (part + 1) * STEP]).astype(jnp.bfloat16)
            stacks[i % 2][part * rows : (part + 1) * rows] = value
            wide = value.astype(jnp.float32)
            total = total + (wide[:, :HALF] + wide[:, HALF:])
        flat_ref[...] = total if i == 0 else flat_ref[...] + total

    def gather(i):
        piece = 32
        for start in range(0, rows, piece):
            total_re = None
            for part in range(PER):
                at = part * rows + start
                step = i * PER + part
                cosine = phases_ref[step : step + 1, :HALF]
                sine = phases_ref[step : step + 1, HALF:]
                first = products[i % 2][at : at + piece, :HALF]
                second = products[i % 2][at : at + piece, HALF:]
                turned_re = first * cosine + second * sine
                turned_im = second * cosine - first * sine
                total_re = turned_re if part == 0 else total_re + turned_re
                total_im = turned_im if part == 0 else total_im + turned_im
            here = slice(start, start + piece)
            re_ref[here] = total_re if i == 0 else re_ref[here] + total_re
            im_ref[here] = total_im if i == 0 else im_ref[here] + total_im

    transmit(0)
    small[0].wait()
    small[1].wait()
    for i in range(CHUNKS):
        products[i % 2][...] = float_dot(stacks[i % 2][...], steps_ref[...])
        if i + 1 < CHUNKS:
            transmit(i + 1)
        if i > 0:
            gather(i - 1)
    gather(CHUNKS - 1)
    for copy in small[2:]:
        copy.wait()
    cosine, sine = turned_table(grid_bases_ref[...], grid_shifts_ref[...])
    rows_ref[:, :BAND] = cosine.astype(jnp.bfloat16)
    rows_ref[:, BAND:] = sine.astype(jnp.bfloat16)
    wanted_ref[...] = targets_ref[...].astype(jnp.float32).astype(jnp.bfloat16)
    table = jnp.concatenate(turned_table(bases_ref[...], shifts_ref[...]), 1)
    product = dot_first(table, jnp.concatenate([re_ref[...], im_ref[...]], 1), HIGHEST)
    by_cos = product[:BAND]
    by_sin = product[BAND:]
    half_re = by_cos[:, :HALF] + by_sin[:, HALF:]
    half_im = by_cos[:, HALF:] - by_sin[:, :HALF]
    beyond_re = by_cos[:1, :HALF] - by_sin[:1, HALF:]
    beyond_im = by_cos[:1, HALF:] + by_sin[:1, :HALF]
    centre = jnp.sum(dot_first(flat_ref[...], table, HIGHEST), 0, keepdims=True) * (1.0 / MASK)
    mirror = conjugate_mirror()
    flip = row_mirror()
    row, column = iotas((BAND, HALF))
    whole = jnp.concatenate([half_re, half_im], 1)
    ends = jnp.concatenate([beyond_re, beyond_im], 1)
    other = 0.0
    for piece, end in zip(split(whole), split(jnp.concatenate([ends] * 8, 0))):
        turned = float_dot(flip, float_dot(piece, mirror).astype(jnp.bfloat16))
        other = other + jnp.where(iotas((BAND, BAND))[0] == 0, float_dot(end, mirror)[:1], turned)
    parts = []
    for part, value in enumerate((centre[:, :BAND], -centre[:, BAND:])):
        line = jnp.sum(jnp.where(diagonal(), value, 0.0), 1, keepdims=True)
        parts.append(jnp.where(column == 0, line, other[:, part * HALF : (part + 1) * HALF]))
    store_tiles(
        out_ref, jnp.concatenate([half_re, parts[0]], 1), jnp.concatenate([half_im, parts[1]], 1)
    )


def mask_spectrum(mask_params, step_value, phases, base, shifts, grid_base, grid_shifts, target):
    rows = mask_params.shape[0]
    stacked = rows * PER
    arguments = (mask_params, step_value, phases, base, shifts, grid_base, grid_shifts, target)
    grid_rows = grid_base.shape[0]
    return pl.pallas_call(
        spectrum_kernel,
        in_specs=[pl.BlockSpec(memory_space=pltpu.HBM)] * len(arguments),
        out_specs=[pl.BlockSpec(memory_space=pltpu.VMEM)] * 3,
        out_shape=[
            jax.ShapeDtypeStruct((DEVICES, 8, 128), jnp.bfloat16),
            jax.ShapeDtypeStruct((grid_rows, 2 * BAND), jnp.bfloat16),
            jax.ShapeDtypeStruct(target.shape, jnp.bfloat16),
        ],
        scratch_shapes=[
            pltpu.VMEM((CHUNKS, rows, WIDTH), jnp.float32),
            pltpu.VMEM(step_value.shape, jnp.bfloat16),
            pltpu.VMEM(phases.shape, jnp.float32),
            pltpu.VMEM(base.shape, jnp.float32),
            pltpu.VMEM((1, 2 * BAND), jnp.float32),
            pltpu.VMEM(grid_base.shape, jnp.float32),
            pltpu.VMEM((1, 2 * BAND), jnp.float32),
            pltpu.VMEM(target.shape, jnp.int32),
            pltpu.VMEM((stacked, STEP), jnp.bfloat16),
            pltpu.VMEM((stacked, STEP), jnp.bfloat16),
            pltpu.VMEM((stacked, BAND), jnp.float32),
            pltpu.VMEM((stacked, BAND), jnp.float32),
            pltpu.VMEM((rows, HALF), jnp.float32),
            pltpu.VMEM((rows, HALF), jnp.float32),
            pltpu.VMEM((rows, HALF), jnp.float32),
            pltpu.SemaphoreType.DMA((CHUNKS + 7,)),
        ],
        compiler_params=params(STREAM_LIMIT),
        name="mask_spectrum",
    )(*arguments)


def field_kernel(
    tiles_ref, pupil_ref, wanted_ref, rows_ref, map_ref, field_ref, power_ref,
    spec_ref, partial_ref, sum_ref,
):
    index = pl.program_id(0)
    rows = wanted_ref.shape[0]
    slab = rows // KERN

    @pl.when(index == 0)
    def _():
        load_tiles(tiles_ref, spec_ref)
        for owner in range(KERN):
            power_ref[owner, 2] = wanted_ref[owner * slab : (owner + 1) * slab]

    spec_re = spec_ref[0]
    spec_im = spec_ref[1]
    for corner in range(2):
        kernel_re = pupil_ref[0, corner, 0]
        kernel_im = pupil_ref[0, corner, 1]
        amp_re = (kernel_re * spec_re - kernel_im * spec_im).astype(jnp.bfloat16)
        amp_im = (kernel_re * spec_im + kernel_im * spec_re).astype(jnp.bfloat16)
        block = jnp.concatenate(
            [jnp.concatenate([amp_re, amp_im], 1), jnp.concatenate([-amp_im, amp_re], 1)], 0
        )
        partial_ref[corner * rows : (corner + 1) * rows] = float_dot(rows_ref[...], block).astype(
            jnp.bfloat16
        )
    field_ref[0] = float_dot(partial_ref[...], map_ref[...])

    for corner in range(2):
        for owner in range(KERN):
            at = corner * rows + owner * slab
            real = field_ref[0, at : at + slab, :COARSE]
            imag = field_ref[0, at : at + slab, COARSE:]
            power = real * real + imag * imag

            @pl.when(index == 0)
            def _():
                sum_ref[at : at + slab] = power

            @pl.when(index == 1)
            def _():
                power_ref[owner, corner] = (sum_ref[at : at + slab] + power).astype(jnp.bfloat16)


def coarse_fields(tiles, pupils, wanted, rows_table, column_map):
    members = pupils.shape[0]
    rows = wanted.shape[0]
    return pl.pallas_call(
        field_kernel,
        grid=(members,),
        in_specs=[
            whole_spec(tiles.shape),
            pl.BlockSpec((1, 2, 2, BAND, BAND), lambda i: (i, 0, 0, 0, 0)),
            whole_spec(wanted.shape),
            whole_spec(rows_table.shape),
            whole_spec(column_map.shape),
        ],
        out_specs=[
            pl.BlockSpec((1, 2 * rows, 2 * COARSE), lambda i: (i, 0, 0)),
            whole_spec((KERN, 3, rows // KERN, COARSE)),
        ],
        out_shape=[
            jax.ShapeDtypeStruct((members, 2 * rows, 2 * COARSE), jnp.float32),
            jax.ShapeDtypeStruct((KERN, 3, rows // KERN, COARSE), jnp.bfloat16),
        ],
        scratch_shapes=[
            pltpu.VMEM((2, BAND, BAND), jnp.float32),
            pltpu.VMEM((2 * rows, 2 * BAND), jnp.bfloat16),
            pltpu.VMEM((2 * rows, COARSE), jnp.float32),
        ],
        compiler_params=params(),
        name="coarse_fields",
    )(tiles, pupils, wanted, rows_table, column_map)


def adjoint_kernel(parts_ref, matrix_ref, out_ref, power_ref, acc_ref):
    index = pl.program_id(0)
    rows = parts_ref.shape[2]

    @pl.when(index == 0)
    def _():
        for corner in range(2):
            total = parts_ref[0, corner].astype(jnp.float32)
            for owner in range(1, KERN):
                total = total + parts_ref[owner, corner].astype(jnp.float32)
            power_ref[corner * rows : (corner + 1) * rows] = total.astype(jnp.bfloat16)
        acc_ref[...] = jnp.zeros_like(acc_ref)

    fine = float_dot(power_ref[...], matrix_ref[...])
    wanted = parts_ref[index, 2].astype(jnp.float32)
    corners = []
    for corner in range(2):
        dose = dose_levels[corner]
        resist = jax.nn.sigmoid(steepness * (dose * fine[corner * rows : (corner + 1) * rows] - threshold))
        corners.append(
            (2.0 * (resist - wanted) * resist * (1.0 - resist) * steepness * dose).astype(jnp.bfloat16)
        )
    acc_ref[...] += dot_last(jnp.concatenate(corners, 0), matrix_ref[...])

    @pl.when(index == pl.num_programs(0) - 1)
    def _():
        folded = acc_ref[...].reshape(2, rows, COARSE).astype(jnp.bfloat16)
        for owner in range(KERN):
            out_ref[owner] = folded


def coarse_adjoint(parts, matrix):
    rows = parts.shape[2]
    width = GRID // KERN
    return pl.pallas_call(
        adjoint_kernel,
        grid=(KERN,),
        in_specs=[
            whole_spec(parts.shape),
            pl.BlockSpec((COARSE, width), lambda i: (0, i)),
        ],
        out_specs=whole_spec((KERN, 2, rows, COARSE)),
        out_shape=jax.ShapeDtypeStruct((KERN, 2, rows, COARSE), jnp.bfloat16),
        scratch_shapes=[
            pltpu.VMEM((2 * rows, COARSE), jnp.bfloat16),
            pltpu.VMEM((2 * rows, COARSE), jnp.float32),
        ],
        compiler_params=params(),
        name="coarse_adjoint",
    )(parts, matrix)


def gradient_kernel(
    field_ref, adjoint_ref, pupil_ref, rows_ref, map_ref, out_ref, weighted_ref, back_ref, acc_ref
):
    index = pl.program_id(0)
    slab = adjoint_ref.shape[2]
    rows = slab * KERN

    @pl.when(index == 0)
    def _():
        acc_ref[...] = jnp.zeros_like(acc_ref)

    for corner in range(2):
        for owner in range(KERN):
            at = corner * rows + owner * slab
            adjoint = 2.0 * adjoint_ref[owner, corner].astype(jnp.float32)
            for half in range(2):
                columns = slice(half * COARSE, (half + 1) * COARSE)
                weighted_ref[at : at + slab, columns] = (field_ref[0, at : at + slab, columns] * adjoint).astype(
                    jnp.bfloat16
                )
    back_ref[...] = dot_last(weighted_ref[...], map_ref[...]).astype(jnp.bfloat16)
    for corner in range(2):
        grads = dot_first(rows_ref[...], back_ref[corner * rows : (corner + 1) * rows])
        grad_re = grads[:BAND, :BAND] + grads[BAND:, BAND:]
        grad_im = grads[:BAND, BAND:] - grads[BAND:, :BAND]
        kernel_re = pupil_ref[0, corner, 0]
        kernel_im = pupil_ref[0, corner, 1]
        acc_ref[0] += kernel_re * grad_re + kernel_im * grad_im
        acc_ref[1] += kernel_re * grad_im - kernel_im * grad_re

    @pl.when(index == pl.num_programs(0) - 1)
    def _():
        store_tiles(out_ref, acc_ref[0], acc_ref[1])


def spectrum_gradient(fields, adjoint, pupils, rows_table, column_map):
    members = pupils.shape[0]
    rows = rows_table.shape[0]
    return pl.pallas_call(
        gradient_kernel,
        grid=(members,),
        in_specs=[
            pl.BlockSpec((1, 2 * rows, 2 * COARSE), lambda i: (i, 0, 0)),
            whole_spec(adjoint.shape),
            pl.BlockSpec((1, 2, 2, BAND, BAND), lambda i: (i, 0, 0, 0, 0)),
            whole_spec(rows_table.shape),
            whole_spec(column_map.shape),
        ],
        out_specs=whole_spec((DEVICES, 8, 128)),
        out_shape=jax.ShapeDtypeStruct((DEVICES, 8, 128), jnp.bfloat16),
        scratch_shapes=[
            pltpu.VMEM((2 * rows, 2 * COARSE), jnp.bfloat16),
            pltpu.VMEM((2 * rows, 2 * BAND), jnp.bfloat16),
            pltpu.VMEM((2, BAND, BAND), jnp.float32),
        ],
        compiler_params=params(),
        name="spectrum_gradient",
    )(fields, adjoint, pupils, rows_table, column_map)


def update_kernel(
    tiles_ref, base_ref, shift_ref, mask_ref, step_ref, phase_ref, out_ref,
    spec_ref, bases_ref, shifts_ref, held_ref, steps_ref, phases_ref, re_ref, im_ref, stack_a, stack_b, product_a, product_b, sems,
):
    rows = mask_ref.shape[0]
    stacks = (stack_a, stack_b)
    products = (product_a, product_b)
    columns = [pl.ds(i * WIDTH, WIDTH) for i in range(CHUNKS)]
    chunks = [
        pltpu.make_async_copy(mask_ref.at[:, columns[i]], held_ref.at[i], sems.at[i]) for i in range(CHUNKS)
    ]
    results = [
        pltpu.make_async_copy(held_ref.at[i], out_ref.at[:, columns[i]], sems.at[CHUNKS + i])
        for i in range(CHUNKS)
    ]
    small = [
        pltpu.make_async_copy(source, target, sems.at[2 * CHUNKS + i])
        for i, (source, target) in enumerate(
            (
                (base_ref, bases_ref),
                (shift_ref.at[device_place()], shifts_ref),
                (phase_ref, phases_ref),
                (step_ref, steps_ref),
            )
        )
    ]
    for copy in small + chunks:
        copy.start()

    load_tiles(tiles_ref, spec_ref)
    left = jnp.concatenate([spec_ref[0, :, :HALF], spec_ref[1, :, :HALF]], 1)
    right = jnp.concatenate([spec_ref[0, :, HALF:], spec_ref[1, :, HALF:]], 1)
    turned = float_dot(right.astype(jnp.bfloat16), conjugate_mirror())
    half = split(left + float_dot(row_mirror(), turned.astype(jnp.bfloat16)))
    beyond_re = turned[:1, :HALF]
    beyond_im = turned[:1, HALF:]
    centres = [
        jnp.sum(jnp.where(diagonal(), spec_ref[part, :, HALF : HALF + 1], 0.0), 0, keepdims=True)
        for part in range(2)
    ]
    small[0].wait()
    small[1].wait()
    cosine, sine = turned_table(bases_ref[...], shifts_ref[...])
    high_cos, low_cos = split(cosine)
    high_sin, low_sin = split(sine)
    product = float_dot(jnp.concatenate([high_cos, low_cos, high_sin, low_sin], 0), half[0])
    rest = float_dot(jnp.concatenate([high_cos, high_sin], 0), half[1])
    by_cos = product[:rows] + (product[rows : 2 * rows] + rest[:rows])
    by_sin = product[2 * rows : 3 * rows] + (product[3 * rows :] + rest[rows:])
    edge_cos = cosine[:, :1]
    edge_sin = -sine[:, :1]
    re_ref[...] = by_cos[:, :HALF] - by_sin[:, HALF:] + (edge_cos * beyond_re - edge_sin * beyond_im)
    im_ref[...] = by_sin[:, :HALF] + by_cos[:, HALF:] + (edge_sin * beyond_re + edge_cos * beyond_im)
    centre = jnp.sum(cosine * centres[0] - sine * centres[1], 1, keepdims=True) * (1.0 / MASK)

    def turn(i):
        piece = 32
        for start in range(0, rows, piece):
            col_re = re_ref[start : start + piece]
            col_im = im_ref[start : start + piece]
            for part in range(PER):
                step = i * PER + part
                cosine = phases_ref[step : step + 1, :HALF]
                sine = phases_ref[step : step + 1, HALF:]
                at = part * rows + start
                stacks[i % 2][at : at + piece, :HALF] = (col_re * cosine - col_im * sine).astype(jnp.bfloat16)
                stacks[i % 2][at : at + piece, HALF:] = (col_re * sine + col_im * cosine).astype(jnp.bfloat16)

    def finish(i):
        for part in range(PER):
            here = slice(part * STEP, (part + 1) * STEP)
            mask = held_ref[i, :, here]
            transmit = jnp.tanh(mask)
            pixel_grad = products[i % 2][part * rows : (part + 1) * rows] + centre
            held_ref[i, :, here] = mask - step_size * pixel_grad * (1.0 - transmit * transmit)
        results[i].start()

    small[2].wait()
    turn(0)
    small[3].wait()
    for i in range(CHUNKS):
        chunks[i].wait()
        products[i % 2][...] = float_dot(stacks[i % 2][...], steps_ref[...])
        if i + 1 < CHUNKS:
            turn(i + 1)
        if i > 0:
            finish(i - 1)
    finish(CHUNKS - 1)
    for copy in results:
        copy.wait()


def mask_update(tiles, base, shifts, mask_params, step_value, phases):
    rows = mask_params.shape[0]
    stacked = rows * PER
    hbm = pl.BlockSpec(memory_space=pltpu.HBM)
    vmem = pl.BlockSpec(memory_space=pltpu.VMEM)
    return pl.pallas_call(
        update_kernel,
        in_specs=[vmem] + [hbm] * 5,
        out_specs=hbm,
        out_shape=jax.ShapeDtypeStruct((rows, MASK), jnp.float32),
        scratch_shapes=[
            pltpu.VMEM((2, BAND, BAND), jnp.float32),
            pltpu.VMEM(base.shape, jnp.float32),
            pltpu.VMEM((1, 2 * BAND), jnp.float32),
            pltpu.VMEM((CHUNKS, rows, WIDTH), jnp.float32),
            pltpu.VMEM(step_value.shape, jnp.bfloat16),
            pltpu.VMEM(phases.shape, jnp.float32),
            pltpu.VMEM((rows, HALF), jnp.float32),
            pltpu.VMEM((rows, HALF), jnp.float32),
            pltpu.VMEM((stacked, BAND), jnp.bfloat16),
            pltpu.VMEM((stacked, BAND), jnp.bfloat16),
            pltpu.VMEM((stacked, STEP), jnp.float32),
            pltpu.VMEM((stacked, STEP), jnp.float32),
            pltpu.SemaphoreType.DMA((2 * CHUNKS + 4,)),
        ],
        compiler_params=params(STREAM_LIMIT),
        name="mask_update",
    )(tiles, base, shifts, mask_params, step_value, phases)


def exchange(values, axes):
    return lax.all_to_all(values, axes, 0, 0, tiled=True)


def summed(parts, copies):
    total = jnp.sum(parts.astype(jnp.float32), 0).astype(parts.dtype)
    return jnp.broadcast_to(total[None], (copies,) + total.shape)


def sum_tiles(tiles):
    everyone = ("rows", "kern")
    return exchange(summed(exchange(tiles, everyone), DEVICES), everyone)


def local(mask_params, pupil_kernels, target_pattern):
    rows = mask_params.shape[0]
    grid_rows = target_pattern.shape[0]
    step_value = step_table()
    phases = jnp.asarray(wide_table(np.arange(STEPS) * STEP, MASK, HALF))
    mask_base = jnp.asarray(wide_table(np.arange(rows), MASK))
    mask_shifts = jnp.asarray(wide_table(np.arange(ROWS * KERN) * rows, MASK)[:, None, :])
    grid_base = jnp.asarray(wide_table(np.arange(grid_rows), GRID))
    grid_shifts = jnp.asarray(wide_table(np.arange(ROWS) * grid_rows, GRID)[:, None, :])
    column_map = jnp.asarray(coarse_map())

    tiles, rows_table, wanted = mask_spectrum(
        mask_params, jnp.asarray(step_value), phases, mask_base, mask_shifts, grid_base, grid_shifts, target_pattern
    )
    fields, powers = coarse_fields(sum_tiles(tiles), pupil_kernels, wanted, rows_table, column_map)
    adjoint = coarse_adjoint(exchange(powers, "kern"), jnp.asarray(interpolation()))
    gradient = spectrum_gradient(fields, exchange(adjoint, "kern"), pupil_kernels, rows_table, column_map)
    return mask_update(
        sum_tiles(gradient), mask_base, mask_shifts, mask_params, jnp.asarray(step_value.T), phases
    )


def solution(mesh):
    placed = (P(("rows", "kern"), None), P("kern", None, None, None, None), P("rows", "kern"))
    return jax.shard_map(
        local, mesh=mesh, in_specs=placed, out_specs=P(("rows", "kern"), None), check_vma=False
    )
```

```python
import math

import jax
import jax.numpy as jnp
import numpy as np
from jax import lax
from jax.experimental import pallas as pl
from jax.experimental.pallas import tpu as pltpu
from jax.sharding import PartitionSpec as P

MASK = 16384
GRID = 4096
BAND = 256
HALF = BAND // 2
COARSE = 512
STEP = 256
STEPS = MASK // STEP
ROWS = 16
KERN = 8
DEVICES = ROWS * KERN
WIDTH = 1024
CHUNKS = MASK // WIDTH
PER = WIDTH // STEP

steepness = 4.0
threshold = 0.75
step_size = 1.0
dose_levels = (1.0, 1.15)

VMEM_LIMIT = 24 * 1024 * 1024
STREAM_LIMIT = 56 * 1024 * 1024


def tables(positions, period, count=BAND):
    frequency = np.arange(count) - BAND // 2
    angles = (np.outer(positions, frequency) % period) * (2.0 * math.pi / period)
    return np.cos(angles), np.sin(angles)


def bfloat(values):
    return np.asarray(values, np.float32).astype(jnp.bfloat16)


def wide_table(positions, period, count=BAND):
    return np.concatenate(tables(positions, period, count), 1).astype(np.float32)


def step_table():
    cosine, sine = tables(np.arange(STEP), MASK, HALF)
    return bfloat(np.concatenate([cosine, -sine], 1) / MASK)


def row_transform(rows):
    table = wide_table(np.arange(rows), MASK).T
    high = bfloat(table)
    return np.concatenate([high, bfloat(table - high.astype(np.float32))], 0)


def coarse_map():
    cosine, sine = tables(np.arange(COARSE), COARSE)
    upper = np.concatenate([cosine.T, sine.T], 1)
    lower = np.concatenate([-sine.T, cosine.T], 1)
    return bfloat(np.concatenate([upper, lower], 0))


def interpolation():
    ratio = GRID // COARSE
    frequency = np.arange(1, COARSE // 2)
    offset = np.arange(GRID)
    profile = 1.0 + 2.0 * np.cos(2.0 * math.pi * (np.outer(offset, frequency) % GRID) / GRID).sum(1)
    profile = (profile + np.cos(math.pi * offset / ratio)) / COARSE
    return bfloat(profile[(offset[None, :] - ratio * np.arange(COARSE)[:, None]) % GRID])


def device_place():
    return lax.axis_index("rows") * KERN + lax.axis_index("kern")


def turned_table(base, shift):
    cosine = base[:, :BAND] * shift[:, :BAND] - base[:, BAND:] * shift[:, BAND:]
    sine = base[:, BAND:] * shift[:, :BAND] + base[:, :BAND] * shift[:, BAND:]
    return cosine, sine


def whole_spec(shape):
    return pl.BlockSpec(shape, lambda i: (0,) * len(shape))


def params(limit=VMEM_LIMIT):
    return pltpu.CompilerParams(vmem_limit_bytes=limit)


def float_dot(left, right):
    return jnp.dot(left, right, preferred_element_type=jnp.float32)


def dot_first(left, right, precision=None):
    return lax.dot_general(
        left, right, (((0,), (0,)), ((), ())), precision=precision, preferred_element_type=jnp.float32
    )


def dot_last(left, right):
    return lax.dot_general(left, right, (((1,), (1,)), ((), ())), preferred_element_type=jnp.float32)


def split(values):
    high = values.astype(jnp.bfloat16)
    return high, (values - high.astype(jnp.float32)).astype(jnp.bfloat16)


def iotas(shape):
    return lax.broadcasted_iota(jnp.int32, shape, 0), lax.broadcasted_iota(jnp.int32, shape, 1)


def conjugate_mirror():
    row, column = iotas((BAND, BAND))
    real = (row + column == HALF) & (row < HALF) & (column > 0) & (column < HALF)
    imag = (row + column == 2 * HALF + HALF) & (row >= HALF) & (column > HALF)
    return (jnp.where(real, 1.0, 0.0) - jnp.where(imag, 1.0, 0.0)).astype(jnp.bfloat16)


def store_tiles(out_ref, real, imag):
    for part, value in enumerate((real, imag)):
        for i in range(BAND // 8):
            for j in range(2):
                out_ref[4 * i + 2 * part + j] = value[8 * i : 8 * i + 8, 128 * j : 128 * j + 128].astype(
                    out_ref.dtype
                )


def load_tiles(tiles_ref, held_ref):
    for part in range(2):
        for i in range(BAND // 8):
            for j in range(2):
                held_ref[part, 8 * i : 8 * i + 8, 128 * j : 128 * j + 128] = tiles_ref[
                    4 * i + 2 * part + j
                ].astype(jnp.float32)


def spectrum_kernel(
    mask_ref, step_ref, phase_ref, base_ref, shift_ref, grid_base_ref, grid_shift_ref, target_ref,
    out_ref, grid_ref,
    held_ref, steps_ref, phases_ref, bases_ref, shifts_ref, grid_bases_ref, grid_shifts_ref, targets_ref,
    stack_a, stack_b, product_a, product_b, re_ref, im_ref, flat_ref, sems,
):
    rows = mask_ref.shape[0]
    grid_rows = target_ref.shape[0]
    stacks = (stack_a, stack_b)
    products = (product_a, product_b)
    chunks = [
        pltpu.make_async_copy(mask_ref.at[:, pl.ds(i * WIDTH, WIDTH)], held_ref.at[i], sems.at[i])
        for i in range(CHUNKS)
    ]
    small = [
        pltpu.make_async_copy(source, target, sems.at[CHUNKS + i])
        for i, (source, target) in enumerate(
            (
                (step_ref, steps_ref),
                (phase_ref, phases_ref),
                (grid_base_ref, grid_bases_ref),
                (grid_shift_ref.at[lax.axis_index("rows")], grid_shifts_ref),
                (target_ref, targets_ref),
                (base_ref, bases_ref),
                (shift_ref.at[device_place()], shifts_ref),
            )
        )
    ]
    chunks[0].start()
    small[0].start()
    small[1].start()
    chunks[1].start()
    for copy in small[2:5] + chunks[2:] + small[5:]:
        copy.start()

    def transmit(i):
        chunks[i].wait()
        total = None
        for part in range(PER):
            value = jnp.tanh(held_ref[i, :, part * STEP : (part + 1) * STEP]).astype(jnp.bfloat16)
            stacks[i % 2][part * rows : (part + 1) * rows] = value
            wide = value.astype(jnp.float32)
            both = wide[:, :HALF] + wide[:, HALF:]
            total = both if part == 0 else total + both
        flat_ref[...] = total if i == 0 else flat_ref[...] + total

    def gather(i):
        piece = 32
        for start in range(0, rows, piece):
            total_re = None
            for part in range(PER):
                at = part * rows + start
                step = i * PER + part
                cosine = phases_ref[step : step + 1, :HALF]
                sine = phases_ref[step : step + 1, HALF:]
                first = products[i % 2][at : at + piece, :HALF]
                second = products[i % 2][at : at + piece, HALF:]
                turned_re = first * cosine + second * sine
                turned_im = second * cosine - first * sine
                total_re = turned_re if part == 0 else total_re + turned_re
                total_im = turned_im if part == 0 else total_im + turned_im
            here = slice(start, start + piece)
            re_ref[here] = total_re if i == 0 else re_ref[here] + total_re
            im_ref[here] = total_im if i == 0 else im_ref[here] + total_im

    transmit(0)
    small[0].wait()
    small[1].wait()
    for i in range(CHUNKS):
        products[i % 2][...] = float_dot(stacks[i % 2][...], steps_ref[...])
        if i + 1 < CHUNKS:
            transmit(i + 1)
        if i > 0:
            gather(i - 1)
        if i == 1:
            for copy in small[2:5]:
                copy.wait()
            cosine, sine = turned_table(grid_bases_ref[...], grid_shifts_ref[...])
            grid_ref[:grid_rows, :BAND] = cosine.astype(jnp.bfloat16)
            grid_ref[:grid_rows, BAND:] = sine.astype(jnp.bfloat16)
            grid_ref[grid_rows:] = targets_ref[...].astype(jnp.float32).astype(jnp.bfloat16)
    gather(CHUNKS - 1)
    for copy in small[5:]:
        copy.wait()
    _, lane = iotas((rows, HALF))
    mirror = conjugate_mirror()
    half_high, half_low = split(jnp.concatenate([re_ref[...], im_ref[...]], 1))
    other = float_dot(half_high, mirror) + float_dot(half_low, mirror)
    centre = jnp.sum(flat_ref[...], 1, keepdims=True) * (1.0 / MASK)
    other_high, other_low = split(
        jnp.concatenate([jnp.where(lane == 0, centre, other[:, :HALF]), other[:, HALF:]], 1)
    )
    high = jnp.concatenate([half_high, other_high], 1)
    low = jnp.concatenate([half_low, other_low], 1)
    product = float_dot(bases_ref[...], high)
    product = product[: 2 * BAND] + (product[2 * BAND :] + float_dot(bases_ref[: 2 * BAND], low))
    diagonal = jnp.equal(*iotas((BAND, BAND)))
    turn_cos, turn_sin = [
        jnp.sum(jnp.where(diagonal, shifts_ref[:, part * BAND : (part + 1) * BAND], 0.0), 1, keepdims=True)
        for part in range(2)
    ]
    by_cos = product[:BAND]
    by_sin = product[BAND:]
    real = []
    imag = []
    for at in (0, 2 * HALF):
        part_re = by_cos[:, at : at + HALF] + by_sin[:, at + HALF : at + 2 * HALF]
        part_im = by_cos[:, at + HALF : at + 2 * HALF] - by_sin[:, at : at + HALF]
        real.append(turn_cos * part_re + turn_sin * part_im)
        imag.append(turn_cos * part_im - turn_sin * part_re)
    store_tiles(out_ref, jnp.concatenate(real, 1), jnp.concatenate(imag, 1))


def mask_spectrum(mask_params, step_value, phases, base, shifts, grid_base, grid_shifts, target):
    rows = mask_params.shape[0]
    stacked = rows * PER
    arguments = (mask_params, step_value, phases, base, shifts, grid_base, grid_shifts, target)
    grid_rows = grid_base.shape[0]
    return pl.pallas_call(
        spectrum_kernel,
        in_specs=[pl.BlockSpec(memory_space=pltpu.HBM)] * len(arguments),
        out_specs=[pl.BlockSpec(memory_space=pltpu.VMEM)] * 2,
        out_shape=[
            jax.ShapeDtypeStruct((DEVICES, 8, 128), jnp.bfloat16),
            jax.ShapeDtypeStruct((2 * grid_rows, 2 * BAND), jnp.bfloat16),
        ],
        scratch_shapes=[
            pltpu.VMEM((CHUNKS, rows, WIDTH), jnp.float32),
            pltpu.VMEM(step_value.shape, jnp.bfloat16),
            pltpu.VMEM(phases.shape, jnp.float32),
            pltpu.VMEM(base.shape, jnp.bfloat16),
            pltpu.VMEM((1, 2 * BAND), jnp.float32),
            pltpu.VMEM(grid_base.shape, jnp.float32),
            pltpu.VMEM((1, 2 * BAND), jnp.float32),
            pltpu.VMEM(target.shape, jnp.int32),
            pltpu.VMEM((stacked, STEP), jnp.bfloat16),
            pltpu.VMEM((stacked, STEP), jnp.bfloat16),
            pltpu.VMEM((stacked, BAND), jnp.float32),
            pltpu.VMEM((stacked, BAND), jnp.float32),
            pltpu.VMEM((rows, HALF), jnp.float32),
            pltpu.VMEM((rows, HALF), jnp.float32),
            pltpu.VMEM((rows, HALF), jnp.float32),
            pltpu.SemaphoreType.DMA((CHUNKS + 7,)),
        ],
        compiler_params=params(STREAM_LIMIT),
        name="mask_spectrum",
    )(*arguments)


def field_kernel(
    tiles_ref, pupil_ref, grid_ref, map_ref, field_ref, power_ref,
    spec_ref, partial_ref, sum_ref,
):
    index = pl.program_id(0)
    rows = grid_ref.shape[0] // 2
    slab = rows // KERN

    @pl.when(index == 0)
    def _():
        load_tiles(tiles_ref, spec_ref)
        for owner in range(KERN):
            power_ref[owner, 2] = grid_ref[rows + owner * slab : rows + (owner + 1) * slab]

    spec_re = spec_ref[0]
    spec_im = spec_ref[1]
    for corner in range(2):
        kernel_re = pupil_ref[0, corner, 0]
        kernel_im = pupil_ref[0, corner, 1]
        amp_re = (kernel_re * spec_re - kernel_im * spec_im).astype(jnp.bfloat16)
        amp_im = (kernel_re * spec_im + kernel_im * spec_re).astype(jnp.bfloat16)
        block = jnp.concatenate(
            [jnp.concatenate([amp_re, amp_im], 1), jnp.concatenate([-amp_im, amp_re], 1)], 0
        )
        partial_ref[corner * rows : (corner + 1) * rows] = float_dot(grid_ref[:rows], block).astype(
            jnp.bfloat16
        )
    field_ref[0] = float_dot(partial_ref[...], map_ref[...])

    for corner in range(2):
        for owner in range(KERN):
            at = corner * rows + owner * slab
            real = field_ref[0, at : at + slab, :COARSE]
            imag = field_ref[0, at : at + slab, COARSE:]
            power = real * real + imag * imag

            @pl.when(index == 0)
            def _():
                sum_ref[at : at + slab] = power

            @pl.when(index == 1)
            def _():
                power_ref[owner, corner] = (sum_ref[at : at + slab] + power).astype(jnp.bfloat16)


def coarse_fields(tiles, pupils, grid_table, column_map):
    members = pupils.shape[0]
    rows = grid_table.shape[0] // 2
    return pl.pallas_call(
        field_kernel,
        grid=(members,),
        in_specs=[
            whole_spec(tiles.shape),
            pl.BlockSpec((1, 2, 2, BAND, BAND), lambda i: (i, 0, 0, 0, 0)),
            whole_spec(grid_table.shape),
            whole_spec(column_map.shape),
        ],
        out_specs=[
            pl.BlockSpec((1, 2 * rows, 2 * COARSE), lambda i: (i, 0, 0)),
            whole_spec((KERN, 3, rows // KERN, COARSE)),
        ],
        out_shape=[
            jax.ShapeDtypeStruct((members, 2 * rows, 2 * COARSE), jnp.float32),
            jax.ShapeDtypeStruct((KERN, 3, rows // KERN, COARSE), jnp.bfloat16),
        ],
        scratch_shapes=[
            pltpu.VMEM((2, BAND, BAND), jnp.float32),
            pltpu.VMEM((2 * rows, 2 * BAND), jnp.bfloat16),
            pltpu.VMEM((2 * rows, COARSE), jnp.float32),
        ],
        compiler_params=params(),
        name="coarse_fields",
    )(tiles, pupils, grid_table, column_map)


def adjoint_kernel(parts_ref, matrix_ref, out_ref):
    rows = parts_ref.shape[2]
    width = GRID // KERN
    powers = []
    for corner in range(2):
        total = parts_ref[0, corner].astype(jnp.float32)
        for owner in range(1, KERN):
            total = total + parts_ref[owner, corner].astype(jnp.float32)
        powers.append(total.astype(jnp.bfloat16))
    power = jnp.concatenate(powers, 0)
    folded = None
    for slab in range(KERN):
        columns = slice(slab * width, (slab + 1) * width)
        fine = float_dot(power, matrix_ref[:, columns])
        wanted = parts_ref[slab, 2].astype(jnp.float32)
        corners = []
        for corner in range(2):
            dose = dose_levels[corner]
            resist = jax.nn.sigmoid(steepness * (dose * fine[corner * rows : (corner + 1) * rows] - threshold))
            corners.append(
                (2.0 * (resist - wanted) * resist * (1.0 - resist) * steepness * dose).astype(jnp.bfloat16)
            )
        term = dot_last(jnp.concatenate(corners, 0), matrix_ref[:, columns])
        folded = term if slab == 0 else folded + term
    folded = folded.reshape(2, rows, COARSE).astype(jnp.bfloat16)
    for owner in range(KERN):
        out_ref[owner] = folded


def coarse_adjoint(parts, matrix):
    rows = parts.shape[2]
    return pl.pallas_call(
        adjoint_kernel,
        in_specs=[pl.BlockSpec(memory_space=pltpu.VMEM)] * 2,
        out_specs=pl.BlockSpec(memory_space=pltpu.VMEM),
        out_shape=jax.ShapeDtypeStruct((KERN, 2, rows, COARSE), jnp.bfloat16),
        compiler_params=params(),
        name="coarse_adjoint",
    )(parts, matrix)


def gradient_kernel(
    field_ref, adjoint_ref, pupil_ref, grid_ref, map_ref, out_ref, weighted_ref, back_ref, acc_ref
):
    index = pl.program_id(0)
    slab = adjoint_ref.shape[2]
    rows = slab * KERN

    @pl.when(index == 0)
    def _():
        acc_ref[...] = jnp.zeros_like(acc_ref)

    for corner in range(2):
        for owner in range(KERN):
            at = corner * rows + owner * slab
            adjoint = 2.0 * adjoint_ref[owner, corner].astype(jnp.float32)
            for half in range(2):
                columns = slice(half * COARSE, (half + 1) * COARSE)
                weighted_ref[at : at + slab, columns] = (field_ref[0, at : at + slab, columns] * adjoint).astype(
                    jnp.bfloat16
                )
    back_ref[...] = dot_last(weighted_ref[...], map_ref[...]).astype(jnp.bfloat16)
    for corner in range(2):
        grads = dot_first(grid_ref[:rows], back_ref[corner * rows : (corner + 1) * rows])
        grad_re = grads[:BAND, :BAND] + grads[BAND:, BAND:]
        grad_im = grads[:BAND, BAND:] - grads[BAND:, :BAND]
        kernel_re = pupil_ref[0, corner, 0]
        kernel_im = pupil_ref[0, corner, 1]
        acc_ref[0] += kernel_re * grad_re + kernel_im * grad_im
        acc_ref[1] += kernel_re * grad_im - kernel_im * grad_re

    @pl.when(index == pl.num_programs(0) - 1)
    def _():
        store_tiles(out_ref, acc_ref[0], acc_ref[1])


def spectrum_gradient(fields, adjoint, pupils, grid_table, column_map):
    members = pupils.shape[0]
    rows = grid_table.shape[0] // 2
    return pl.pallas_call(
        gradient_kernel,
        grid=(members,),
        in_specs=[
            pl.BlockSpec((1, 2 * rows, 2 * COARSE), lambda i: (i, 0, 0)),
            whole_spec(adjoint.shape),
            pl.BlockSpec((1, 2, 2, BAND, BAND), lambda i: (i, 0, 0, 0, 0)),
            whole_spec(grid_table.shape),
            whole_spec(column_map.shape),
        ],
        out_specs=whole_spec((DEVICES, 8, 128)),
        out_shape=jax.ShapeDtypeStruct((DEVICES, 8, 128), jnp.bfloat16),
        scratch_shapes=[
            pltpu.VMEM((2 * rows, 2 * COARSE), jnp.bfloat16),
            pltpu.VMEM((2 * rows, 2 * BAND), jnp.bfloat16),
            pltpu.VMEM((2, BAND, BAND), jnp.float32),
        ],
        compiler_params=params(),
        name="spectrum_gradient",
    )(fields, adjoint, pupils, grid_table, column_map)


def update_kernel(
    tiles_ref, base_ref, shift_ref, mask_ref, step_ref, phase_ref, out_ref,
    spec_ref, bases_ref, shifts_ref, held_ref, steps_ref, phases_ref, re_ref, im_ref, stack_a, stack_b, product_a, product_b, sems,
):
    rows = mask_ref.shape[0]
    stacks = (stack_a, stack_b)
    products = (product_a, product_b)
    columns = [pl.ds(i * WIDTH, WIDTH) for i in range(CHUNKS)]
    chunks = [
        pltpu.make_async_copy(mask_ref.at[:, columns[i]], held_ref.at[i], sems.at[i]) for i in range(CHUNKS)
    ]
    results = [
        pltpu.make_async_copy(held_ref.at[i], out_ref.at[:, columns[i]], sems.at[CHUNKS + i])
        for i in range(CHUNKS)
    ]
    small = [
        pltpu.make_async_copy(source, target, sems.at[2 * CHUNKS + i])
        for i, (source, target) in enumerate(
            (
                (base_ref, bases_ref),
                (shift_ref.at[device_place()], shifts_ref),
                (phase_ref, phases_ref),
                (step_ref, steps_ref),
            )
        )
    ]
    for copy in small + chunks:
        copy.start()

    load_tiles(tiles_ref, spec_ref)
    gradient = jnp.concatenate([spec_ref[0], spec_ref[1]], 1).astype(jnp.bfloat16)
    small[0].wait()
    small[1].wait()
    cosine, sine = turned_table(bases_ref[...], shifts_ref[...])
    product = float_dot(jnp.concatenate(split(cosine) + split(sine), 0), gradient)
    by_cos = product[:rows] + product[rows : 2 * rows]
    by_sin = product[2 * rows : 3 * rows] + product[3 * rows :]
    col_re = by_cos[:, :BAND] - by_sin[:, BAND:]
    col_im = by_sin[:, :BAND] + by_cos[:, BAND:]
    centre = col_re[:, HALF : HALF + 1] * (1.0 / MASK)
    mirror = conjugate_mirror()
    high, low = split(jnp.concatenate([col_re[:, HALF:], col_im[:, HALF:]], 1))
    other = float_dot(high, mirror) + float_dot(low, mirror)
    re_ref[...] = col_re[:, :HALF] + other[:, :HALF]
    im_ref[...] = col_im[:, :HALF] + other[:, HALF:]

    def turn(i):
        piece = 32
        for start in range(0, rows, piece):
            col_re = re_ref[start : start + piece]
            col_im = im_ref[start : start + piece]
            for part in range(PER):
                step = i * PER + part
                cosine = phases_ref[step : step + 1, :HALF]
                sine = phases_ref[step : step + 1, HALF:]
                at = part * rows + start
                stacks[i % 2][at : at + piece, :HALF] = (col_re * cosine - col_im * sine).astype(jnp.bfloat16)
                stacks[i % 2][at : at + piece, HALF:] = (col_re * sine + col_im * cosine).astype(jnp.bfloat16)

    def finish(i):
        for part in range(PER):
            here = slice(part * STEP, (part + 1) * STEP)
            mask = held_ref[i, :, here]
            transmit = jnp.tanh(mask)
            pixel_grad = products[i % 2][part * rows : (part + 1) * rows] + centre
            held_ref[i, :, here] = mask - step_size * pixel_grad * (1.0 - transmit * transmit)
        results[i].start()

    small[2].wait()
    turn(0)
    small[3].wait()
    for i in range(CHUNKS):
        chunks[i].wait()
        products[i % 2][...] = float_dot(stacks[i % 2][...], steps_ref[...])
        if i + 1 < CHUNKS:
            turn(i + 1)
        if i > 0:
            finish(i - 1)
    finish(CHUNKS - 1)
    for copy in results:
        copy.wait()


def mask_update(tiles, base, shifts, mask_params, step_value, phases):
    rows = mask_params.shape[0]
    stacked = rows * PER
    hbm = pl.BlockSpec(memory_space=pltpu.HBM)
    vmem = pl.BlockSpec(memory_space=pltpu.VMEM)
    return pl.pallas_call(
        update_kernel,
        in_specs=[vmem] + [hbm] * 5,
        out_specs=hbm,
        out_shape=jax.ShapeDtypeStruct((rows, MASK), jnp.float32),
        scratch_shapes=[
            pltpu.VMEM((2, BAND, BAND), jnp.float32),
            pltpu.VMEM(base.shape, jnp.float32),
            pltpu.VMEM((1, 2 * BAND), jnp.float32),
            pltpu.VMEM((CHUNKS, rows, WIDTH), jnp.float32),
            pltpu.VMEM(step_value.shape, jnp.bfloat16),
            pltpu.VMEM(phases.shape, jnp.float32),
            pltpu.VMEM((rows, HALF), jnp.float32),
            pltpu.VMEM((rows, HALF), jnp.float32),
            pltpu.VMEM((stacked, BAND), jnp.bfloat16),
            pltpu.VMEM((stacked, BAND), jnp.bfloat16),
            pltpu.VMEM((stacked, STEP), jnp.float32),
            pltpu.VMEM((stacked, STEP), jnp.float32),
            pltpu.SemaphoreType.DMA((2 * CHUNKS + 4,)),
        ],
        compiler_params=params(STREAM_LIMIT),
        name="mask_update",
    )(tiles, base, shifts, mask_params, step_value, phases)


def exchange(values, axes):
    return lax.all_to_all(values, axes, 0, 0, tiled=True)


def summed(parts, copies):
    total = jnp.sum(parts.astype(jnp.float32), 0).astype(parts.dtype)
    return jnp.broadcast_to(total[None], (copies,) + total.shape)


def sum_tiles(tiles):
    everyone = ("rows", "kern")
    return exchange(summed(exchange(tiles, everyone), DEVICES), everyone)


def local(mask_params, pupil_kernels, target_pattern):
    rows = mask_params.shape[0]
    grid_rows = target_pattern.shape[0]
    step_value = step_table()
    phases = jnp.asarray(wide_table(np.arange(STEPS) * STEP, MASK, HALF))
    mask_base = jnp.asarray(wide_table(np.arange(rows), MASK))
    mask_transform = jnp.asarray(row_transform(rows))
    mask_shifts = jnp.asarray(wide_table(np.arange(ROWS * KERN) * rows, MASK)[:, None, :])
    grid_base = jnp.asarray(wide_table(np.arange(grid_rows), GRID))
    grid_shifts = jnp.asarray(wide_table(np.arange(ROWS) * grid_rows, GRID)[:, None, :])
    column_map = jnp.asarray(coarse_map())

    tiles, grid_table = mask_spectrum(
        mask_params, jnp.asarray(step_value), phases, mask_transform, mask_shifts, grid_base, grid_shifts, target_pattern
    )
    fields, powers = coarse_fields(sum_tiles(tiles), pupil_kernels, grid_table, column_map)
    adjoint = coarse_adjoint(exchange(powers, "kern"), jnp.asarray(interpolation()))
    gradient = spectrum_gradient(fields, exchange(adjoint, "kern"), pupil_kernels, grid_table, column_map)
    return mask_update(
        sum_tiles(gradient), mask_base, mask_shifts, mask_params, jnp.asarray(step_value.T), phases
    )


def solution(mesh):
    placed = (P(("rows", "kern"), None), P("kern", None, None, None, None), P("rows", "kern"))
    return jax.shard_map(
        local, mesh=mesh, in_specs=placed, out_specs=P(("rows", "kern"), None), check_vma=False
    )
```

```python
import math

import jax
import jax.numpy as jnp
import numpy as np
from jax import lax
from jax.experimental import pallas as pl
from jax.experimental.pallas import tpu as pltpu
from jax.sharding import PartitionSpec as P

MASK = 16384
GRID = 4096
BAND = 256
HALF = BAND // 2
COARSE = 512
STEP = 256
STEPS = MASK // STEP
ROWS = 16
KERN = 8
DEVICES = ROWS * KERN
CHUNK = 16

steepness = 4.0
threshold = 0.75
step_size = 1.0
dose_levels = (1.0, 1.15)

VMEM_LIMIT = 24 * 1024 * 1024
STREAM_LIMIT = 56 * 1024 * 1024


def tables(positions, period, count=BAND):
    frequency = np.arange(count) - BAND // 2
    angles = (np.outer(positions, frequency) % period) * (2.0 * math.pi / period)
    return np.cos(angles), np.sin(angles)


def bfloat(values):
    return np.asarray(values, np.float32).astype(jnp.bfloat16)


def wide_table(positions, period, count=BAND):
    return np.concatenate(tables(positions, period, count), 1).astype(np.float32)


def step_table():
    cosine, sine = tables(np.arange(STEP), MASK, HALF)
    return bfloat(np.concatenate([cosine, -sine], 1) / MASK)


def row_transform(rows):
    table = wide_table(np.arange(rows), MASK).T
    high = bfloat(table)
    return np.concatenate([high, bfloat(table - high.astype(np.float32))], 0)


def coarse_map():
    cosine, sine = tables(np.arange(COARSE), COARSE)
    upper = np.concatenate([cosine.T, sine.T], 1)
    lower = np.concatenate([-sine.T, cosine.T], 1)
    return bfloat(np.concatenate([upper, lower], 0))


def interpolation():
    ratio = GRID // COARSE
    frequency = np.arange(1, COARSE // 2)
    offset = np.arange(GRID)
    profile = 1.0 + 2.0 * np.cos(2.0 * math.pi * (np.outer(offset, frequency) % GRID) / GRID).sum(1)
    profile = (profile + np.cos(math.pi * offset / ratio)) / COARSE
    return bfloat(profile[(offset[None, :] - ratio * np.arange(COARSE)[:, None]) % GRID])


def device_place():
    return lax.axis_index("rows") * KERN + lax.axis_index("kern")


def turned_table(base, shift):
    cosine = base[:, :BAND] * shift[:, :BAND] - base[:, BAND:] * shift[:, BAND:]
    sine = base[:, BAND:] * shift[:, :BAND] + base[:, :BAND] * shift[:, BAND:]
    return cosine, sine


def params(limit=VMEM_LIMIT):
    return pltpu.CompilerParams(vmem_limit_bytes=limit)


def float_dot(left, right):
    return jnp.dot(left, right, preferred_element_type=jnp.float32)


def dot_first(left, right, precision=None):
    return lax.dot_general(
        left, right, (((0,), (0,)), ((), ())), precision=precision, preferred_element_type=jnp.float32
    )


def dot_last(left, right):
    return lax.dot_general(left, right, (((1,), (1,)), ((), ())), preferred_element_type=jnp.float32)


def split(values):
    high = values.astype(jnp.bfloat16)
    return high, (values - high.astype(jnp.float32)).astype(jnp.bfloat16)


def iotas(shape):
    return lax.broadcasted_iota(jnp.int32, shape, 0), lax.broadcasted_iota(jnp.int32, shape, 1)


def conjugate_mirror():
    row, column = iotas((BAND, BAND))
    real = (row + column == HALF) & (row < HALF) & (column > 0) & (column < HALF)
    imag = (row + column == 2 * HALF + HALF) & (row >= HALF) & (column > HALF)
    return (jnp.where(real, 1.0, 0.0) - jnp.where(imag, 1.0, 0.0)).astype(jnp.bfloat16)


def store_tiles(out_ref, real, imag):
    for part, value in enumerate((real, imag)):
        for i in range(BAND // 8):
            for j in range(2):
                out_ref[4 * i + 2 * part + j] = value[8 * i : 8 * i + 8, 128 * j : 128 * j + 128].astype(
                    out_ref.dtype
                )


def load_tiles(tiles_ref, held_ref):
    for part in range(2):
        for i in range(BAND // 8):
            for j in range(2):
                held_ref[part, 8 * i : 8 * i + 8, 128 * j : 128 * j + 128] = tiles_ref[
                    4 * i + 2 * part + j
                ].astype(jnp.float32)


def spectrum_kernel(
    mask_ref, step_ref, phase_ref, base_ref, shift_ref, grid_base_ref, grid_shift_ref, target_ref,
    out_ref, grid_out_ref,
    grid_ref, held_ref, steps_ref, phases_ref, bases_ref, shifts_ref, grid_bases_ref, grid_shifts_ref, targets_ref,
    stack_a, stack_b, product_a, product_b, re_ref, im_ref, flat_ref, sems,
):
    rows = mask_ref.shape[0]
    grid_rows = target_ref.shape[0]
    stacks = (stack_a, stack_b)
    products = (product_a, product_b)
    count = rows // CHUNK
    places = [pl.ds(i * CHUNK, CHUNK) for i in range(count)]
    chunks = [
        pltpu.make_async_copy(mask_ref.at[places[i]], held_ref.at[places[i]], sems.at[i]) for i in range(count)
    ]
    small = [
        pltpu.make_async_copy(source, target, sems.at[count + i])
        for i, (source, target) in enumerate(
            (
                (step_ref, steps_ref),
                (phase_ref, phases_ref),
                (grid_base_ref, grid_bases_ref),
                (grid_shift_ref.at[lax.axis_index("rows")], grid_shifts_ref),
                (target_ref, targets_ref),
                (base_ref, bases_ref),
                (shift_ref.at[device_place()], shifts_ref),
            )
        )
    ]
    grid_copy = pltpu.make_async_copy(grid_ref, grid_out_ref, sems.at[count + 7])
    chunks[0].start()
    small[0].start()
    small[1].start()
    chunks[1].start()
    for copy in small[2:5] + chunks[2:] + small[5:]:
        copy.start()

    def transmit(i):
        chunks[i].wait()
        total = None
        for step in range(STEPS):
            value = jnp.tanh(held_ref[places[i], step * STEP : (step + 1) * STEP]).astype(jnp.bfloat16)
            stacks[i % 2][step * CHUNK : (step + 1) * CHUNK] = value
            wide = value.astype(jnp.float32)
            both = wide[:, :HALF] + wide[:, HALF:]
            total = both if step == 0 else total + both
        flat_ref[places[i]] = total

    def gather(i):
        totals = [None] * 4
        for step in range(STEPS):
            cosine = phases_ref[step : step + 1, :HALF]
            sine = phases_ref[step : step + 1, HALF:]
            first = products[i % 2][step * CHUNK : (step + 1) * CHUNK, :HALF]
            second = products[i % 2][step * CHUNK : (step + 1) * CHUNK, HALF:]
            at = 2 * (step % 2)
            for part, turned in enumerate(
                (first * cosine + second * sine, second * cosine - first * sine)
            ):
                totals[at + part] = turned if step < 2 else totals[at + part] + turned
        re_ref[places[i]] = totals[0] + totals[2]
        im_ref[places[i]] = totals[1] + totals[3]

    transmit(0)
    small[0].wait()
    small[1].wait()
    for i in range(count):
        products[i % 2][...] = float_dot(stacks[i % 2][...], steps_ref[...])
        if i + 1 < count:
            transmit(i + 1)
        if i > 0:
            gather(i - 1)
        if i == 1:
            for copy in small[2:5]:
                copy.wait()
            cosine, sine = turned_table(grid_bases_ref[...], grid_shifts_ref[...])
            grid_ref[:grid_rows, :BAND] = cosine.astype(jnp.bfloat16)
            grid_ref[:grid_rows, BAND:] = sine.astype(jnp.bfloat16)
            grid_ref[grid_rows:] = targets_ref[...].astype(jnp.float32).astype(jnp.bfloat16)
            grid_copy.start()
    gather(count - 1)
    for copy in small[5:]:
        copy.wait()
    _, lane = iotas((rows, HALF))
    mirror = conjugate_mirror()
    half_high, half_low = split(jnp.concatenate([re_ref[...], im_ref[...]], 1))
    other = float_dot(half_high, mirror) + float_dot(half_low, mirror)
    centre = jnp.sum(flat_ref[...], 1, keepdims=True) * (1.0 / MASK)
    other_high, other_low = split(
        jnp.concatenate([jnp.where(lane == 0, centre, other[:, :HALF]), other[:, HALF:]], 1)
    )
    high = jnp.concatenate([half_high, other_high], 1)
    low = jnp.concatenate([half_low, other_low], 1)
    product = float_dot(bases_ref[...], high)
    product = product[: 2 * BAND] + (product[2 * BAND :] + float_dot(bases_ref[: 2 * BAND], low))
    diagonal = jnp.equal(*iotas((BAND, BAND)))
    turn_cos, turn_sin = [
        jnp.sum(jnp.where(diagonal, shifts_ref[:, part * BAND : (part + 1) * BAND], 0.0), 1, keepdims=True)
        for part in range(2)
    ]
    by_cos = product[:BAND]
    by_sin = product[BAND:]
    real = []
    imag = []
    for at in (0, 2 * HALF):
        part_re = by_cos[:, at : at + HALF] + by_sin[:, at + HALF : at + 2 * HALF]
        part_im = by_cos[:, at + HALF : at + 2 * HALF] - by_sin[:, at : at + HALF]
        real.append(turn_cos * part_re + turn_sin * part_im)
        imag.append(turn_cos * part_im - turn_sin * part_re)
    store_tiles(out_ref, jnp.concatenate(real, 1), jnp.concatenate(imag, 1))
    grid_copy.wait()


def mask_spectrum(mask_params, step_value, phases, base, shifts, grid_base, grid_shifts, target):
    rows = mask_params.shape[0]
    stacked = STEPS * CHUNK
    arguments = (mask_params, step_value, phases, base, shifts, grid_base, grid_shifts, target)
    grid_rows = grid_base.shape[0]
    return pl.pallas_call(
        spectrum_kernel,
        in_specs=[pl.BlockSpec(memory_space=pltpu.HBM)] * len(arguments),
        out_specs=[pl.BlockSpec(memory_space=pltpu.VMEM), pl.BlockSpec(memory_space=pltpu.HBM)],
        out_shape=[
            jax.ShapeDtypeStruct((DEVICES, 8, 128), jnp.bfloat16),
            jax.ShapeDtypeStruct((2 * grid_rows, 2 * BAND), jnp.bfloat16),
        ],
        scratch_shapes=[
            pltpu.VMEM((2 * grid_rows, 2 * BAND), jnp.bfloat16),
            pltpu.VMEM((rows, MASK), jnp.float32),
            pltpu.VMEM(step_value.shape, jnp.bfloat16),
            pltpu.VMEM(phases.shape, jnp.float32),
            pltpu.VMEM(base.shape, jnp.bfloat16),
            pltpu.VMEM((1, 2 * BAND), jnp.float32),
            pltpu.VMEM(grid_base.shape, jnp.float32),
            pltpu.VMEM((1, 2 * BAND), jnp.float32),
            pltpu.VMEM(target.shape, jnp.int32),
            pltpu.VMEM((stacked, STEP), jnp.bfloat16),
            pltpu.VMEM((stacked, STEP), jnp.bfloat16),
            pltpu.VMEM((stacked, BAND), jnp.float32),
            pltpu.VMEM((stacked, BAND), jnp.float32),
            pltpu.VMEM((rows, HALF), jnp.float32),
            pltpu.VMEM((rows, HALF), jnp.float32),
            pltpu.VMEM((rows, HALF), jnp.float32),
            pltpu.SemaphoreType.DMA((rows // CHUNK + 8,)),
        ],
        compiler_params=params(STREAM_LIMIT),
        name="mask_spectrum",
    )(*arguments)


def field_kernel(tiles_ref, pupil_ref, grid_ref, map_ref, field_ref, power_ref, spec_ref, partial_ref):
    members = pupil_ref.shape[0]
    rows = grid_ref.shape[0] // 2
    slab = rows // KERN
    load_tiles(tiles_ref, spec_ref)
    spec_re = spec_ref[0]
    spec_im = spec_ref[1]
    for member in range(members):
        for corner in range(2):
            kernel_re = pupil_ref[member, corner, 0]
            kernel_im = pupil_ref[member, corner, 1]
            amp_re = (kernel_re * spec_re - kernel_im * spec_im).astype(jnp.bfloat16)
            amp_im = (kernel_re * spec_im + kernel_im * spec_re).astype(jnp.bfloat16)
            block = jnp.concatenate(
                [jnp.concatenate([amp_re, amp_im], 1), jnp.concatenate([-amp_im, amp_re], 1)], 0
            )
            partial_ref[member, corner * rows : (corner + 1) * rows] = float_dot(grid_ref[:rows], block).astype(
                jnp.bfloat16
            )
        field_ref[member] = float_dot(partial_ref[member], map_ref[...])
    for owner in range(KERN):
        power_ref[owner, 2] = grid_ref[rows + owner * slab : rows + (owner + 1) * slab]
        for corner in range(2):
            at = corner * rows + owner * slab
            power = None
            for member in range(members):
                real = field_ref[member, at : at + slab, :COARSE]
                imag = field_ref[member, at : at + slab, COARSE:]
                term = real * real + imag * imag
                power = term if member == 0 else power + term
            power_ref[owner, corner] = power.astype(jnp.bfloat16)


def coarse_fields(tiles, pupils, grid_table, column_map):
    members = pupils.shape[0]
    rows = grid_table.shape[0] // 2
    vmem = pl.BlockSpec(memory_space=pltpu.VMEM)
    return pl.pallas_call(
        field_kernel,
        in_specs=[vmem] * 4,
        out_specs=[vmem] * 2,
        out_shape=[
            jax.ShapeDtypeStruct((members, 2 * rows, 2 * COARSE), jnp.float32),
            jax.ShapeDtypeStruct((KERN, 3, rows // KERN, COARSE), jnp.bfloat16),
        ],
        scratch_shapes=[
            pltpu.VMEM((2, BAND, BAND), jnp.float32),
            pltpu.VMEM((members, 2 * rows, 2 * BAND), jnp.bfloat16),
        ],
        compiler_params=params(),
        name="coarse_fields",
    )(tiles, pupils, grid_table, column_map)


def adjoint_kernel(parts_ref, matrix_ref, out_ref):
    rows = parts_ref.shape[2]
    width = GRID // KERN
    powers = []
    for corner in range(2):
        total = parts_ref[0, corner].astype(jnp.float32)
        for owner in range(1, KERN):
            total = total + parts_ref[owner, corner].astype(jnp.float32)
        powers.append(total.astype(jnp.bfloat16))
    power = jnp.concatenate(powers, 0)
    folded = None
    for slab in range(KERN):
        columns = slice(slab * width, (slab + 1) * width)
        fine = float_dot(power, matrix_ref[:, columns])
        wanted = parts_ref[slab, 2].astype(jnp.float32)
        corners = []
        for corner in range(2):
            dose = dose_levels[corner]
            resist = jax.nn.sigmoid(steepness * (dose * fine[corner * rows : (corner + 1) * rows] - threshold))
            corners.append(
                (2.0 * (resist - wanted) * resist * (1.0 - resist) * steepness * dose).astype(jnp.bfloat16)
            )
        term = dot_last(jnp.concatenate(corners, 0), matrix_ref[:, columns])
        folded = term if slab == 0 else folded + term
    folded = folded.reshape(2, rows, COARSE).astype(jnp.bfloat16)
    for owner in range(KERN):
        out_ref[owner] = folded


def coarse_adjoint(parts, matrix):
    rows = parts.shape[2]
    return pl.pallas_call(
        adjoint_kernel,
        in_specs=[pl.BlockSpec(memory_space=pltpu.VMEM)] * 2,
        out_specs=pl.BlockSpec(memory_space=pltpu.VMEM),
        out_shape=jax.ShapeDtypeStruct((KERN, 2, rows, COARSE), jnp.bfloat16),
        compiler_params=params(),
        name="coarse_adjoint",
    )(parts, matrix)


def gradient_kernel(field_ref, adjoint_ref, pupil_ref, grid_ref, map_ref, out_ref, weighted_ref, back_ref, acc_ref):
    members = pupil_ref.shape[0]
    slab = adjoint_ref.shape[2]
    rows = slab * KERN
    for member in range(members):
        for corner in range(2):
            for owner in range(KERN):
                at = corner * rows + owner * slab
                adjoint = 2.0 * adjoint_ref[owner, corner].astype(jnp.float32)
                for half in range(2):
                    columns = slice(half * COARSE, (half + 1) * COARSE)
                    weighted_ref[member, at : at + slab, columns] = (
                        field_ref[member, at : at + slab, columns] * adjoint
                    ).astype(jnp.bfloat16)
        back_ref[member] = dot_last(weighted_ref[member], map_ref[...]).astype(jnp.bfloat16)
        for corner in range(2):
            grads = dot_first(grid_ref[:rows], back_ref[member, corner * rows : (corner + 1) * rows])
            grad_re = grads[:BAND, :BAND] + grads[BAND:, BAND:]
            grad_im = grads[:BAND, BAND:] - grads[BAND:, :BAND]
            kernel_re = pupil_ref[member, corner, 0]
            kernel_im = pupil_ref[member, corner, 1]
            term_re = kernel_re * grad_re + kernel_im * grad_im
            term_im = kernel_re * grad_im - kernel_im * grad_re
            first = member == 0 and corner == 0
            acc_ref[0] = term_re if first else acc_ref[0] + term_re
            acc_ref[1] = term_im if first else acc_ref[1] + term_im
    store_tiles(out_ref, acc_ref[0], acc_ref[1])


def spectrum_gradient(fields, adjoint, pupils, grid_table, column_map):
    members = pupils.shape[0]
    rows = grid_table.shape[0] // 2
    vmem = pl.BlockSpec(memory_space=pltpu.VMEM)
    return pl.pallas_call(
        gradient_kernel,
        in_specs=[vmem] * 5,
        out_specs=vmem,
        out_shape=jax.ShapeDtypeStruct((DEVICES, 8, 128), jnp.bfloat16),
        scratch_shapes=[
            pltpu.VMEM((members, 2 * rows, 2 * COARSE), jnp.bfloat16),
            pltpu.VMEM((members, 2 * rows, 2 * BAND), jnp.bfloat16),
            pltpu.VMEM((2, BAND, BAND), jnp.float32),
        ],
        compiler_params=params(),
        name="spectrum_gradient",
    )(fields, adjoint, pupils, grid_table, column_map)


def update_kernel(
    tiles_ref, base_ref, shift_ref, mask_ref, step_ref, phase_ref, out_ref,
    tile_ref, spec_ref, bases_ref, shifts_ref, held_ref, steps_ref, phases_ref, re_ref, im_ref, flat_ref, stack_a, stack_b, product_a, product_b, sems,
):
    rows = mask_ref.shape[0]
    stacks = (stack_a, stack_b)
    products = (product_a, product_b)
    count = rows // CHUNK
    places = [pl.ds(i * CHUNK, CHUNK) for i in range(count)]
    chunks = [
        pltpu.make_async_copy(mask_ref.at[places[i]], held_ref.at[places[i]], sems.at[i]) for i in range(count)
    ]
    results = [
        pltpu.make_async_copy(held_ref.at[places[i]], out_ref.at[places[i]], sems.at[count + i])
        for i in range(count)
    ]
    small = [
        pltpu.make_async_copy(source, target, sems.at[2 * count + i])
        for i, (source, target) in enumerate(
            (
                (base_ref, bases_ref),
                (shift_ref.at[device_place()], shifts_ref),
                (tiles_ref, tile_ref),
                (phase_ref, phases_ref),
                (step_ref, steps_ref),
            )
        )
    ]
    for copy in small + chunks:
        copy.start()

    small[0].wait()
    small[1].wait()
    cosine, sine = turned_table(bases_ref[...], shifts_ref[...])
    small[2].wait()
    load_tiles(tile_ref, spec_ref)
    gradient = jnp.concatenate([spec_ref[0], spec_ref[1]], 1).astype(jnp.bfloat16)
    product = float_dot(jnp.concatenate(split(cosine) + split(sine), 0), gradient)
    by_cos = product[:rows] + product[rows : 2 * rows]
    by_sin = product[2 * rows : 3 * rows] + product[3 * rows :]
    col_re = by_cos[:, :BAND] - by_sin[:, BAND:]
    col_im = by_sin[:, :BAND] + by_cos[:, BAND:]
    flat_ref[...] = jnp.broadcast_to(col_re[:, HALF : HALF + 1] * (1.0 / MASK), flat_ref.shape)
    mirror = conjugate_mirror()
    high, low = split(jnp.concatenate([col_re[:, HALF:], col_im[:, HALF:]], 1))
    other = float_dot(high, mirror) + float_dot(low, mirror)
    re_ref[...] = col_re[:, :HALF] + other[:, :HALF]
    im_ref[...] = col_im[:, :HALF] + other[:, HALF:]

    def turn(i):
        col_re = re_ref[places[i]]
        col_im = im_ref[places[i]]
        for step in range(STEPS):
            cosine = phases_ref[step : step + 1, :HALF]
            sine = phases_ref[step : step + 1, HALF:]
            here = slice(step * CHUNK, (step + 1) * CHUNK)
            stacks[i % 2][here, :HALF] = (col_re * cosine - col_im * sine).astype(jnp.bfloat16)
            stacks[i % 2][here, HALF:] = (col_re * sine + col_im * cosine).astype(jnp.bfloat16)

    def finish(i):
        centre = flat_ref[places[i]]
        for step in range(STEPS):
            here = slice(step * STEP, (step + 1) * STEP)
            mask = held_ref[places[i], here]
            transmit = jnp.tanh(mask)
            pixel_grad = products[i % 2][step * CHUNK : (step + 1) * CHUNK] + centre
            held_ref[places[i], here] = mask - step_size * pixel_grad * (1.0 - transmit * transmit)
        results[i].start()

    small[3].wait()
    turn(0)
    small[4].wait()
    for i in range(count):
        chunks[i].wait()
        products[i % 2][...] = float_dot(stacks[i % 2][...], steps_ref[...])
        if i + 1 < count:
            turn(i + 1)
        if i > 0:
            finish(i - 1)
    finish(count - 1)
    for copy in results:
        copy.wait()


def mask_update(tiles, base, shifts, mask_params, step_value, phases):
    rows = mask_params.shape[0]
    stacked = STEPS * CHUNK
    hbm = pl.BlockSpec(memory_space=pltpu.HBM)
    return pl.pallas_call(
        update_kernel,
        in_specs=[hbm] * 6,
        out_specs=hbm,
        out_shape=jax.ShapeDtypeStruct((rows, MASK), jnp.float32),
        scratch_shapes=[
            pltpu.VMEM(tiles.shape, jnp.bfloat16),
            pltpu.VMEM((2, BAND, BAND), jnp.float32),
            pltpu.VMEM(base.shape, jnp.float32),
            pltpu.VMEM((1, 2 * BAND), jnp.float32),
            pltpu.VMEM((rows, MASK), jnp.float32),
            pltpu.VMEM(step_value.shape, jnp.bfloat16),
            pltpu.VMEM(phases.shape, jnp.float32),
            pltpu.VMEM((rows, HALF), jnp.float32),
            pltpu.VMEM((rows, HALF), jnp.float32),
            pltpu.VMEM((rows, STEP), jnp.float32),
            pltpu.VMEM((stacked, BAND), jnp.bfloat16),
            pltpu.VMEM((stacked, BAND), jnp.bfloat16),
            pltpu.VMEM((stacked, STEP), jnp.float32),
            pltpu.VMEM((stacked, STEP), jnp.float32),
            pltpu.SemaphoreType.DMA((2 * (rows // CHUNK) + 5,)),
        ],
        compiler_params=params(STREAM_LIMIT),
        name="mask_update",
    )(tiles, base, shifts, mask_params, step_value, phases)


def exchange(values, axes):
    return lax.all_to_all(values, axes, 0, 0, tiled=True)


def summed(parts, copies):
    total = jnp.sum(parts.astype(jnp.float32), 0).astype(parts.dtype)
    return jnp.broadcast_to(total[None], (copies,) + total.shape)


def sum_tiles(tiles):
    everyone = ("rows", "kern")
    return exchange(summed(exchange(tiles, everyone), DEVICES), everyone)


def local(mask_params, pupil_kernels, target_pattern):
    rows = mask_params.shape[0]
    grid_rows = target_pattern.shape[0]
    step_value = step_table()
    phases = jnp.asarray(wide_table(np.arange(STEPS) * STEP, MASK, HALF))
    mask_base = jnp.asarray(wide_table(np.arange(rows), MASK))
    mask_transform = jnp.asarray(row_transform(rows))
    mask_shifts = jnp.asarray(wide_table(np.arange(ROWS * KERN) * rows, MASK)[:, None, :])
    grid_base = jnp.asarray(wide_table(np.arange(grid_rows), GRID))
    grid_shifts = jnp.asarray(wide_table(np.arange(ROWS) * grid_rows, GRID)[:, None, :])
    column_map = jnp.asarray(coarse_map())

    tiles, grid_table = mask_spectrum(
        mask_params, jnp.asarray(step_value), phases, mask_transform, mask_shifts, grid_base, grid_shifts, target_pattern
    )
    fields, powers = coarse_fields(sum_tiles(tiles), pupil_kernels, grid_table, column_map)
    adjoint = coarse_adjoint(exchange(powers, "kern"), jnp.asarray(interpolation()))
    gradient = spectrum_gradient(fields, exchange(adjoint, "kern"), pupil_kernels, grid_table, column_map)
    return mask_update(
        sum_tiles(gradient), mask_base, mask_shifts, mask_params, jnp.asarray(step_value.T), phases
    )


def solution(mesh):
    placed = (P(("rows", "kern"), None), P("kern", None, None, None, None), P("rows", "kern"))
    return jax.shard_map(
        local, mesh=mesh, in_specs=placed, out_specs=P(("rows", "kern"), None), check_vma=False
    )
```

```python
import math

import jax
import jax.numpy as jnp
import numpy as np
from jax import lax
from jax.experimental import pallas as pl
from jax.experimental.pallas import tpu as pltpu
from jax.sharding import PartitionSpec as P

MASK = 16384
GRID = 4096
BAND = 256
HALF = BAND // 2
COARSE = 512
STEP = 256
STEPS = MASK // STEP
ROWS = 16
KERN = 8
DEVICES = ROWS * KERN
CHUNK = 16
QUARTERS = 4

steepness = 4.0
threshold = 0.75
step_size = 1.0
dose_levels = (1.0, 1.15)

VMEM_LIMIT = 24 * 1024 * 1024
STREAM_LIMIT = 56 * 1024 * 1024


def tables(positions, period, count=BAND):
    frequency = np.arange(count) - BAND // 2
    angles = (np.outer(positions, frequency) % period) * (2.0 * math.pi / period)
    return np.cos(angles), np.sin(angles)


def bfloat(values):
    return np.asarray(values, np.float32).astype(jnp.bfloat16)


def wide_table(positions, period, count=BAND):
    return np.concatenate(tables(positions, period, count), 1).astype(np.float32)


def step_table():
    cosine, sine = tables(np.arange(STEP), MASK, HALF)
    return bfloat(np.concatenate([cosine, -sine], 1) / MASK)


def row_transform(rows):
    table = wide_table(np.arange(rows), MASK).T
    high = bfloat(table)
    return np.concatenate([high, bfloat(table - high.astype(np.float32))], 0)


def coarse_map():
    cosine, sine = tables(np.arange(COARSE), COARSE)
    upper = np.concatenate([cosine.T, sine.T], 1)
    lower = np.concatenate([-sine.T, cosine.T], 1)
    return bfloat(np.concatenate([upper, lower], 0))


def interpolation():
    ratio = GRID // COARSE
    frequency = np.arange(1, COARSE // 2)
    offset = np.arange(GRID)
    profile = 1.0 + 2.0 * np.cos(2.0 * math.pi * (np.outer(offset, frequency) % GRID) / GRID).sum(1)
    profile = (profile + np.cos(math.pi * offset / ratio)) / COARSE
    return bfloat(profile[(offset[None, :] - ratio * np.arange(COARSE)[:, None]) % GRID])


def device_place():
    return lax.axis_index("rows") * KERN + lax.axis_index("kern")


def turned_table(base, shift):
    cosine = base[:, :BAND] * shift[:, :BAND] - base[:, BAND:] * shift[:, BAND:]
    sine = base[:, BAND:] * shift[:, :BAND] + base[:, :BAND] * shift[:, BAND:]
    return cosine, sine


def params(limit=VMEM_LIMIT):
    return pltpu.CompilerParams(vmem_limit_bytes=limit)


def float_dot(left, right):
    return jnp.dot(left, right, preferred_element_type=jnp.float32)


def dot_first(left, right, precision=None):
    return lax.dot_general(
        left, right, (((0,), (0,)), ((), ())), precision=precision, preferred_element_type=jnp.float32
    )


def dot_last(left, right):
    return lax.dot_general(left, right, (((1,), (1,)), ((), ())), preferred_element_type=jnp.float32)


def split(values):
    high = values.astype(jnp.bfloat16)
    return high, (values - high.astype(jnp.float32)).astype(jnp.bfloat16)


def iotas(shape):
    return lax.broadcasted_iota(jnp.int32, shape, 0), lax.broadcasted_iota(jnp.int32, shape, 1)


def conjugate_mirror():
    row, column = iotas((BAND, BAND))
    real = (row + column == HALF) & (row < HALF) & (column > 0) & (column < HALF)
    imag = (row + column == 2 * HALF + HALF) & (row >= HALF) & (column > HALF)
    return (jnp.where(real, 1.0, 0.0) - jnp.where(imag, 1.0, 0.0)).astype(jnp.bfloat16)


def store_tiles(out_ref, real, imag):
    for part, value in enumerate((real, imag)):
        for i in range(BAND // 8):
            for j in range(2):
                out_ref[4 * i + 2 * part + j] = value[8 * i : 8 * i + 8, 128 * j : 128 * j + 128].astype(
                    out_ref.dtype
                )


def load_tiles(tiles_ref, held_ref):
    for part in range(2):
        for i in range(BAND // 8):
            for j in range(2):
                held_ref[part, 8 * i : 8 * i + 8, 128 * j : 128 * j + 128] = tiles_ref[
                    4 * i + 2 * part + j
                ].astype(jnp.float32)


def spectrum_kernel(
    mask_ref, step_ref, phase_ref, base_ref, shift_ref, grid_base_ref, grid_shift_ref, target_ref,
    out_ref, grid_out_ref,
    grid_ref, held_ref, steps_ref, phases_ref, bases_ref, shifts_ref, grid_bases_ref, grid_shifts_ref, targets_ref,
    stack_a, stack_b, product_a, product_b, re_ref, im_ref, flat_ref, sems,
):
    rows = mask_ref.shape[0]
    grid_rows = target_ref.shape[0]
    stacks = (stack_a, stack_b)
    products = (product_a, product_b)
    count = rows // CHUNK
    places = [pl.ds(i * CHUNK, CHUNK) for i in range(count)]
    chunks = [
        pltpu.make_async_copy(mask_ref.at[places[i]], held_ref.at[places[i]], sems.at[i]) for i in range(count)
    ]
    small = [
        pltpu.make_async_copy(source, target, sems.at[count + i])
        for i, (source, target) in enumerate(
            (
                (step_ref, steps_ref),
                (phase_ref, phases_ref),
                (grid_base_ref, grid_bases_ref),
                (grid_shift_ref.at[lax.axis_index("rows")], grid_shifts_ref),
                (target_ref, targets_ref),
                (base_ref, bases_ref),
                (shift_ref.at[device_place()], shifts_ref),
            )
        )
    ]
    grid_copy = pltpu.make_async_copy(grid_ref, grid_out_ref, sems.at[count + 7])
    chunks[0].start()
    small[0].start()
    small[1].start()
    chunks[1].start()
    for copy in small[2:5] + chunks[2:] + small[5:]:
        copy.start()

    def steps_of(quarter):
        return range(quarter * STEPS // QUARTERS, (quarter + 1) * STEPS // QUARTERS)

    def transmit(i, quarter):
        total = None
        for step in steps_of(quarter):
            value = jnp.tanh(held_ref[places[i], step * STEP : (step + 1) * STEP])
            stacks[i % 2][step * CHUNK : (step + 1) * CHUNK] = value.astype(jnp.bfloat16)
            both = value[:, :HALF] + value[:, HALF:]
            total = both if total is None else total + both
        flat_ref[places[i]] = total if quarter == 0 else flat_ref[places[i]] + total

    def multiply(i, quarter):
        here = slice(steps_of(quarter).start * CHUNK, steps_of(quarter).stop * CHUNK)
        products[i % 2][here] = float_dot(stacks[i % 2][here], steps_ref[...])

    def gather(i, quarter):
        totals = [None] * 4
        for step in steps_of(quarter):
            cosine = phases_ref[step : step + 1, :HALF]
            sine = phases_ref[step : step + 1, HALF:]
            first = products[i % 2][step * CHUNK : (step + 1) * CHUNK, :HALF]
            second = products[i % 2][step * CHUNK : (step + 1) * CHUNK, HALF:]
            at = 2 * (step % 2)
            for part, turned in enumerate(
                (first * cosine + second * sine, second * cosine - first * sine)
            ):
                totals[at + part] = turned if totals[at + part] is None else totals[at + part] + turned
        total_re = totals[0] + totals[2]
        total_im = totals[1] + totals[3]
        re_ref[places[i]] = total_re if quarter == 0 else re_ref[places[i]] + total_re
        im_ref[places[i]] = total_im if quarter == 0 else im_ref[places[i]] + total_im

    chunks[0].wait()
    for quarter in range(QUARTERS):
        transmit(0, quarter)
    small[0].wait()
    small[1].wait()
    for i in range(count):
        if i + 1 < count:
            chunks[i + 1].wait()
        for quarter in range(QUARTERS):
            multiply(i, quarter)
            if i + 1 < count:
                transmit(i + 1, quarter)
            if i > 0:
                gather(i - 1, quarter)
        if i == 1:
            for copy in small[2:5]:
                copy.wait()
            cosine, sine = turned_table(grid_bases_ref[...], grid_shifts_ref[...])
            grid_ref[:grid_rows, :BAND] = cosine.astype(jnp.bfloat16)
            grid_ref[:grid_rows, BAND:] = sine.astype(jnp.bfloat16)
            grid_ref[grid_rows:] = targets_ref[...].astype(jnp.float32).astype(jnp.bfloat16)
            grid_copy.start()
    for quarter in range(QUARTERS):
        gather(count - 1, quarter)
    for copy in small[5:]:
        copy.wait()
    _, lane = iotas((rows, HALF))
    mirror = conjugate_mirror()
    half_high, half_low = split(jnp.concatenate([re_ref[...], im_ref[...]], 1))
    other = float_dot(half_high, mirror) + float_dot(half_low, mirror)
    centre = jnp.sum(flat_ref[...], 1, keepdims=True) * (1.0 / MASK)
    other_high, other_low = split(
        jnp.concatenate([jnp.where(lane == 0, centre, other[:, :HALF]), other[:, HALF:]], 1)
    )
    high = jnp.concatenate([half_high, other_high], 1)
    low = jnp.concatenate([half_low, other_low], 1)
    product = float_dot(bases_ref[...], high)
    product = product[: 2 * BAND] + (product[2 * BAND :] + float_dot(bases_ref[: 2 * BAND], low))
    diagonal = jnp.equal(*iotas((BAND, BAND)))
    turn_cos, turn_sin = [
        jnp.sum(jnp.where(diagonal, shifts_ref[:, part * BAND : (part + 1) * BAND], 0.0), 1, keepdims=True)
        for part in range(2)
    ]
    by_cos = product[:BAND]
    by_sin = product[BAND:]
    real = []
    imag = []
    for at in (0, 2 * HALF):
        part_re = by_cos[:, at : at + HALF] + by_sin[:, at + HALF : at + 2 * HALF]
        part_im = by_cos[:, at + HALF : at + 2 * HALF] - by_sin[:, at : at + HALF]
        real.append(turn_cos * part_re + turn_sin * part_im)
        imag.append(turn_cos * part_im - turn_sin * part_re)
    store_tiles(out_ref, jnp.concatenate(real, 1), jnp.concatenate(imag, 1))
    grid_copy.wait()


def mask_spectrum(mask_params, step_value, phases, base, shifts, grid_base, grid_shifts, target):
    rows = mask_params.shape[0]
    stacked = STEPS * CHUNK
    arguments = (mask_params, step_value, phases, base, shifts, grid_base, grid_shifts, target)
    grid_rows = grid_base.shape[0]
    return pl.pallas_call(
        spectrum_kernel,
        in_specs=[pl.BlockSpec(memory_space=pltpu.HBM)] * len(arguments),
        out_specs=[pl.BlockSpec(memory_space=pltpu.VMEM), pl.BlockSpec(memory_space=pltpu.HBM)],
        out_shape=[
            jax.ShapeDtypeStruct((DEVICES, 8, 128), jnp.bfloat16),
            jax.ShapeDtypeStruct((2 * grid_rows, 2 * BAND), jnp.bfloat16),
        ],
        scratch_shapes=[
            pltpu.VMEM((2 * grid_rows, 2 * BAND), jnp.bfloat16),
            pltpu.VMEM((rows, MASK), jnp.float32),
            pltpu.VMEM(step_value.shape, jnp.bfloat16),
            pltpu.VMEM(phases.shape, jnp.float32),
            pltpu.VMEM(base.shape, jnp.bfloat16),
            pltpu.VMEM((1, 2 * BAND), jnp.float32),
            pltpu.VMEM(grid_base.shape, jnp.float32),
            pltpu.VMEM((1, 2 * BAND), jnp.float32),
            pltpu.VMEM(target.shape, jnp.int32),
            pltpu.VMEM((stacked, STEP), jnp.bfloat16),
            pltpu.VMEM((stacked, STEP), jnp.bfloat16),
            pltpu.VMEM((stacked, BAND), jnp.float32),
            pltpu.VMEM((stacked, BAND), jnp.float32),
            pltpu.VMEM((rows, HALF), jnp.float32),
            pltpu.VMEM((rows, HALF), jnp.float32),
            pltpu.VMEM((rows, HALF), jnp.float32),
            pltpu.SemaphoreType.DMA((rows // CHUNK + 8,)),
        ],
        compiler_params=params(STREAM_LIMIT),
        name="mask_spectrum",
    )(*arguments)


def field_kernel(tiles_ref, pupil_ref, grid_ref, map_ref, field_ref, power_ref, spec_ref, partial_ref):
    members = pupil_ref.shape[0]
    rows = grid_ref.shape[0] // 2
    slab = rows // KERN
    load_tiles(tiles_ref, spec_ref)
    spec_re = spec_ref[0]
    spec_im = spec_ref[1]
    for member in range(members):
        for corner in range(2):
            kernel_re = pupil_ref[member, corner, 0]
            kernel_im = pupil_ref[member, corner, 1]
            amp_re = (kernel_re * spec_re - kernel_im * spec_im).astype(jnp.bfloat16)
            amp_im = (kernel_re * spec_im + kernel_im * spec_re).astype(jnp.bfloat16)
            block = jnp.concatenate(
                [jnp.concatenate([amp_re, amp_im], 1), jnp.concatenate([-amp_im, amp_re], 1)], 0
            )
            partial_ref[member, corner * rows : (corner + 1) * rows] = float_dot(grid_ref[:rows], block).astype(
                jnp.bfloat16
            )
        field_ref[member] = float_dot(partial_ref[member], map_ref[...])
    for owner in range(KERN):
        power_ref[owner, 2] = grid_ref[rows + owner * slab : rows + (owner + 1) * slab]
        for corner in range(2):
            at = corner * rows + owner * slab
            power = None
            for member in range(members):
                real = field_ref[member, at : at + slab, :COARSE]
                imag = field_ref[member, at : at + slab, COARSE:]
                term = real * real + imag * imag
                power = term if member == 0 else power + term
            power_ref[owner, corner] = power.astype(jnp.bfloat16)


def coarse_fields(tiles, pupils, grid_table, column_map):
    members = pupils.shape[0]
    rows = grid_table.shape[0] // 2
    vmem = pl.BlockSpec(memory_space=pltpu.VMEM)
    return pl.pallas_call(
        field_kernel,
        in_specs=[vmem] * 4,
        out_specs=[vmem] * 2,
        out_shape=[
            jax.ShapeDtypeStruct((members, 2 * rows, 2 * COARSE), jnp.float32),
            jax.ShapeDtypeStruct((KERN, 3, rows // KERN, COARSE), jnp.bfloat16),
        ],
        scratch_shapes=[
            pltpu.VMEM((2, BAND, BAND), jnp.float32),
            pltpu.VMEM((members, 2 * rows, 2 * BAND), jnp.bfloat16),
        ],
        compiler_params=params(),
        name="coarse_fields",
    )(tiles, pupils, grid_table, column_map)


def adjoint_kernel(parts_ref, matrix_ref, out_ref):
    rows = parts_ref.shape[2]
    width = GRID // KERN
    powers = []
    for corner in range(2):
        total = parts_ref[0, corner].astype(jnp.float32)
        for owner in range(1, KERN):
            total = total + parts_ref[owner, corner].astype(jnp.float32)
        powers.append(total.astype(jnp.bfloat16))
    power = jnp.concatenate(powers, 0)
    folded = None
    for slab in range(KERN):
        columns = slice(slab * width, (slab + 1) * width)
        fine = float_dot(power, matrix_ref[:, columns])
        wanted = parts_ref[slab, 2].astype(jnp.float32)
        corners = []
        for corner in range(2):
            dose = dose_levels[corner]
            resist = jax.nn.sigmoid(steepness * (dose * fine[corner * rows : (corner + 1) * rows] - threshold))
            corners.append(
                (2.0 * (resist - wanted) * resist * (1.0 - resist) * steepness * dose).astype(jnp.bfloat16)
            )
        term = dot_last(jnp.concatenate(corners, 0), matrix_ref[:, columns])
        folded = term if slab == 0 else folded + term
    folded = folded.reshape(2, rows, COARSE).astype(jnp.bfloat16)
    for owner in range(KERN):
        out_ref[owner] = folded


def coarse_adjoint(parts, matrix):
    rows = parts.shape[2]
    return pl.pallas_call(
        adjoint_kernel,
        in_specs=[pl.BlockSpec(memory_space=pltpu.VMEM)] * 2,
        out_specs=pl.BlockSpec(memory_space=pltpu.VMEM),
        out_shape=jax.ShapeDtypeStruct((KERN, 2, rows, COARSE), jnp.bfloat16),
        compiler_params=params(),
        name="coarse_adjoint",
    )(parts, matrix)


def gradient_kernel(field_ref, adjoint_ref, pupil_ref, grid_ref, map_ref, out_ref, weighted_ref, back_ref, acc_ref):
    members = pupil_ref.shape[0]
    slab = adjoint_ref.shape[2]
    rows = slab * KERN
    for member in range(members):
        for corner in range(2):
            for owner in range(KERN):
                at = corner * rows + owner * slab
                adjoint = 2.0 * adjoint_ref[owner, corner].astype(jnp.float32)
                for half in range(2):
                    columns = slice(half * COARSE, (half + 1) * COARSE)
                    weighted_ref[member, at : at + slab, columns] = (
                        field_ref[member, at : at + slab, columns] * adjoint
                    ).astype(jnp.bfloat16)
        back_ref[member] = dot_last(weighted_ref[member], map_ref[...]).astype(jnp.bfloat16)
        for corner in range(2):
            grads = dot_first(grid_ref[:rows], back_ref[member, corner * rows : (corner + 1) * rows])
            grad_re = grads[:BAND, :BAND] + grads[BAND:, BAND:]
            grad_im = grads[:BAND, BAND:] - grads[BAND:, :BAND]
            kernel_re = pupil_ref[member, corner, 0]
            kernel_im = pupil_ref[member, corner, 1]
            term_re = kernel_re * grad_re + kernel_im * grad_im
            term_im = kernel_re * grad_im - kernel_im * grad_re
            first = member == 0 and corner == 0
            acc_ref[0] = term_re if first else acc_ref[0] + term_re
            acc_ref[1] = term_im if first else acc_ref[1] + term_im
    store_tiles(out_ref, acc_ref[0], acc_ref[1])


def spectrum_gradient(fields, adjoint, pupils, grid_table, column_map):
    members = pupils.shape[0]
    rows = grid_table.shape[0] // 2
    vmem = pl.BlockSpec(memory_space=pltpu.VMEM)
    return pl.pallas_call(
        gradient_kernel,
        in_specs=[vmem] * 5,
        out_specs=vmem,
        out_shape=jax.ShapeDtypeStruct((DEVICES, 8, 128), jnp.bfloat16),
        scratch_shapes=[
            pltpu.VMEM((members, 2 * rows, 2 * COARSE), jnp.bfloat16),
            pltpu.VMEM((members, 2 * rows, 2 * BAND), jnp.bfloat16),
            pltpu.VMEM((2, BAND, BAND), jnp.float32),
        ],
        compiler_params=params(),
        name="spectrum_gradient",
    )(fields, adjoint, pupils, grid_table, column_map)


def update_kernel(
    tiles_ref, base_ref, shift_ref, mask_ref, step_ref, phase_ref, out_ref,
    tile_ref, spec_ref, bases_ref, shifts_ref, held_ref, steps_ref, phases_ref, re_ref, im_ref, flat_ref, stack_a, stack_b, product_a, product_b, sems,
):
    rows = mask_ref.shape[0]
    stacks = (stack_a, stack_b)
    products = (product_a, product_b)
    count = rows // CHUNK
    places = [pl.ds(i * CHUNK, CHUNK) for i in range(count)]
    chunks = [
        pltpu.make_async_copy(mask_ref.at[places[i]], held_ref.at[places[i]], sems.at[i]) for i in range(count)
    ]
    results = [
        pltpu.make_async_copy(held_ref.at[places[i]], out_ref.at[places[i]], sems.at[count + i])
        for i in range(count)
    ]
    small = [
        pltpu.make_async_copy(source, target, sems.at[2 * count + i])
        for i, (source, target) in enumerate(
            (
                (base_ref, bases_ref),
                (shift_ref.at[device_place()], shifts_ref),
                (tiles_ref, tile_ref),
                (phase_ref, phases_ref),
                (step_ref, steps_ref),
            )
        )
    ]
    for copy in small + chunks:
        copy.start()

    small[0].wait()
    small[1].wait()
    cosine, sine = turned_table(bases_ref[...], shifts_ref[...])
    small[2].wait()
    load_tiles(tile_ref, spec_ref)
    gradient = jnp.concatenate([spec_ref[0], spec_ref[1]], 1).astype(jnp.bfloat16)
    product = float_dot(jnp.concatenate(split(cosine) + split(sine), 0), gradient)
    by_cos = product[:rows] + product[rows : 2 * rows]
    by_sin = product[2 * rows : 3 * rows] + product[3 * rows :]
    col_re = by_cos[:, :BAND] - by_sin[:, BAND:]
    col_im = by_sin[:, :BAND] + by_cos[:, BAND:]
    flat_ref[...] = jnp.broadcast_to(col_re[:, HALF : HALF + 1] * (1.0 / MASK), flat_ref.shape)
    mirror = conjugate_mirror()
    high, low = split(jnp.concatenate([col_re[:, HALF:], col_im[:, HALF:]], 1))
    other = float_dot(high, mirror) + float_dot(low, mirror)
    re_ref[...] = col_re[:, :HALF] + other[:, :HALF]
    im_ref[...] = col_im[:, :HALF] + other[:, HALF:]

    def steps_of(quarter):
        return range(quarter * STEPS // QUARTERS, (quarter + 1) * STEPS // QUARTERS)

    def turn(i, quarter):
        col_re = re_ref[places[i]]
        col_im = im_ref[places[i]]
        for step in steps_of(quarter):
            cosine = phases_ref[step : step + 1, :HALF]
            sine = phases_ref[step : step + 1, HALF:]
            here = slice(step * CHUNK, (step + 1) * CHUNK)
            stacks[i % 2][here, :HALF] = (col_re * cosine - col_im * sine).astype(jnp.bfloat16)
            stacks[i % 2][here, HALF:] = (col_re * sine + col_im * cosine).astype(jnp.bfloat16)

    def multiply(i, quarter):
        here = slice(steps_of(quarter).start * CHUNK, steps_of(quarter).stop * CHUNK)
        products[i % 2][here] = float_dot(stacks[i % 2][here], steps_ref[...])

    def finish(i, quarter):
        centre = flat_ref[places[i]]
        for step in steps_of(quarter):
            here = slice(step * STEP, (step + 1) * STEP)
            mask = held_ref[places[i], here]
            transmit = jnp.tanh(mask)
            pixel_grad = products[i % 2][step * CHUNK : (step + 1) * CHUNK] + centre
            held_ref[places[i], here] = mask - step_size * pixel_grad * (1.0 - transmit * transmit)

    small[3].wait()
    for quarter in range(QUARTERS):
        turn(0, quarter)
    small[4].wait()
    for i in range(count + 1):
        if i > 0:
            chunks[i - 1].wait()
        for quarter in range(QUARTERS):
            if i < count:
                multiply(i, quarter)
            if i + 1 < count:
                turn(i + 1, quarter)
            if i > 0:
                finish(i - 1, quarter)
        if i > 0:
            results[i - 1].start()
    for copy in results:
        copy.wait()


def mask_update(tiles, base, shifts, mask_params, step_value, phases):
    rows = mask_params.shape[0]
    stacked = STEPS * CHUNK
    hbm = pl.BlockSpec(memory_space=pltpu.HBM)
    return pl.pallas_call(
        update_kernel,
        in_specs=[hbm] * 6,
        out_specs=hbm,
        out_shape=jax.ShapeDtypeStruct((rows, MASK), jnp.float32),
        scratch_shapes=[
            pltpu.VMEM(tiles.shape, jnp.bfloat16),
            pltpu.VMEM((2, BAND, BAND), jnp.float32),
            pltpu.VMEM(base.shape, jnp.float32),
            pltpu.VMEM((1, 2 * BAND), jnp.float32),
            pltpu.VMEM((rows, MASK), jnp.float32),
            pltpu.VMEM(step_value.shape, jnp.bfloat16),
            pltpu.VMEM(phases.shape, jnp.float32),
            pltpu.VMEM((rows, HALF), jnp.float32),
            pltpu.VMEM((rows, HALF), jnp.float32),
            pltpu.VMEM((rows, STEP), jnp.float32),
            pltpu.VMEM((stacked, BAND), jnp.bfloat16),
            pltpu.VMEM((stacked, BAND), jnp.bfloat16),
            pltpu.VMEM((stacked, STEP), jnp.float32),
            pltpu.VMEM((stacked, STEP), jnp.float32),
            pltpu.SemaphoreType.DMA((2 * (rows // CHUNK) + 5,)),
        ],
        compiler_params=params(STREAM_LIMIT),
        name="mask_update",
    )(tiles, base, shifts, mask_params, step_value, phases)


def exchange(values, axes):
    return lax.all_to_all(values, axes, 0, 0, tiled=True)


def summed(parts, copies):
    total = jnp.sum(parts.astype(jnp.float32), 0).astype(parts.dtype)
    return jnp.broadcast_to(total[None], (copies,) + total.shape)


def sum_tiles(tiles):
    everyone = ("rows", "kern")
    return exchange(summed(exchange(tiles, everyone), DEVICES), everyone)


def local(mask_params, pupil_kernels, target_pattern):
    rows = mask_params.shape[0]
    grid_rows = target_pattern.shape[0]
    step_value = step_table()
    phases = jnp.asarray(wide_table(np.arange(STEPS) * STEP, MASK, HALF))
    mask_base = jnp.asarray(wide_table(np.arange(rows), MASK))
    mask_transform = jnp.asarray(row_transform(rows))
    mask_shifts = jnp.asarray(wide_table(np.arange(ROWS * KERN) * rows, MASK)[:, None, :])
    grid_base = jnp.asarray(wide_table(np.arange(grid_rows), GRID))
    grid_shifts = jnp.asarray(wide_table(np.arange(ROWS) * grid_rows, GRID)[:, None, :])
    column_map = jnp.asarray(coarse_map())

    tiles, grid_table = mask_spectrum(
        mask_params, jnp.asarray(step_value), phases, mask_transform, mask_shifts, grid_base, grid_shifts, target_pattern
    )
    fields, powers = coarse_fields(sum_tiles(tiles), pupil_kernels, grid_table, column_map)
    adjoint = coarse_adjoint(exchange(powers, "kern"), jnp.asarray(interpolation()))
    gradient = spectrum_gradient(fields, exchange(adjoint, "kern"), pupil_kernels, grid_table, column_map)
    return mask_update(
        sum_tiles(gradient), mask_base, mask_shifts, mask_params, jnp.asarray(step_value.T), phases
    )


def solution(mesh):
    placed = (P(("rows", "kern"), None), P("kern", None, None, None, None), P("rows", "kern"))
    return jax.shard_map(
        local, mesh=mesh, in_specs=placed, out_specs=P(("rows", "kern"), None), check_vma=False
    )
```

```python
import math

import jax
import jax.numpy as jnp
import numpy as np
from jax import lax
from jax.experimental import pallas as pl
from jax.experimental.pallas import tpu as pltpu
from jax.sharding import PartitionSpec as P

MASK = 16384
GRID = 4096
BAND = 256
HALF = BAND // 2
COARSE = 512
STEP = 256
STEPS = MASK // STEP
ROWS = 16
KERN = 8
DEVICES = ROWS * KERN
CHUNK = 16
QUARTERS = 4

steepness = 4.0
threshold = 0.75
step_size = 1.0
dose_levels = (1.0, 1.15)

VMEM_LIMIT = 24 * 1024 * 1024
STREAM_LIMIT = 56 * 1024 * 1024
FIRST_LIMIT = 53 * 1024 * 1024


def tables(positions, period, count=BAND):
    frequency = np.arange(count) - BAND // 2
    angles = (np.outer(positions, frequency) % period) * (2.0 * math.pi / period)
    return np.cos(angles), np.sin(angles)


def bfloat(values):
    return np.asarray(values, np.float32).astype(jnp.bfloat16)


def wide_table(positions, period, count=BAND):
    return np.concatenate(tables(positions, period, count), 1).astype(np.float32)


def step_table():
    cosine, sine = tables(np.arange(STEP), MASK, HALF)
    return bfloat(np.concatenate([cosine, -sine], 1) / MASK)


def row_transform(rows):
    table = wide_table(np.arange(rows), MASK).T
    high = bfloat(table)
    return np.concatenate([high, bfloat(table - high.astype(np.float32))], 0)


def coarse_map():
    cosine, sine = tables(np.arange(COARSE), COARSE)
    upper = np.concatenate([cosine.T, sine.T], 1)
    lower = np.concatenate([-sine.T, cosine.T], 1)
    return bfloat(np.concatenate([upper, lower], 0))


def interpolation():
    ratio = GRID // COARSE
    frequency = np.arange(1, COARSE // 2)
    offset = np.arange(GRID)
    profile = 1.0 + 2.0 * np.cos(2.0 * math.pi * (np.outer(offset, frequency) % GRID) / GRID).sum(1)
    profile = (profile + np.cos(math.pi * offset / ratio)) / COARSE
    return bfloat(profile[(offset[None, :] - ratio * np.arange(COARSE)[:, None]) % GRID])


def device_place():
    return lax.axis_index("rows") * KERN + lax.axis_index("kern")


def turned_table(base, shift):
    cosine = base[:, :BAND] * shift[:, :BAND] - base[:, BAND:] * shift[:, BAND:]
    sine = base[:, BAND:] * shift[:, :BAND] + base[:, :BAND] * shift[:, BAND:]
    return cosine, sine


def params(limit=VMEM_LIMIT):
    return pltpu.CompilerParams(vmem_limit_bytes=limit)


def float_dot(left, right):
    return jnp.dot(left, right, preferred_element_type=jnp.float32)


def dot_first(left, right, precision=None):
    return lax.dot_general(
        left, right, (((0,), (0,)), ((), ())), precision=precision, preferred_element_type=jnp.float32
    )


def dot_last(left, right):
    return lax.dot_general(left, right, (((1,), (1,)), ((), ())), preferred_element_type=jnp.float32)


def split(values):
    high = values.astype(jnp.bfloat16)
    return high, (values - high.astype(jnp.float32)).astype(jnp.bfloat16)


def iotas(shape):
    return lax.broadcasted_iota(jnp.int32, shape, 0), lax.broadcasted_iota(jnp.int32, shape, 1)


def conjugate_mirror():
    row, column = iotas((BAND, BAND))
    real = (row + column == HALF) & (row < HALF) & (column > 0) & (column < HALF)
    imag = (row + column == 2 * HALF + HALF) & (row >= HALF) & (column > HALF)
    return (jnp.where(real, 1.0, 0.0) - jnp.where(imag, 1.0, 0.0)).astype(jnp.bfloat16)


def store_tiles(out_ref, real, imag):
    for part, value in enumerate((real, imag)):
        for i in range(BAND // 8):
            for j in range(2):
                out_ref[4 * i + 2 * part + j] = value[8 * i : 8 * i + 8, 128 * j : 128 * j + 128].astype(
                    out_ref.dtype
                )


def load_tiles(tiles_ref, held_ref):
    for part in range(2):
        for i in range(BAND // 8):
            for j in range(2):
                held_ref[part, 8 * i : 8 * i + 8, 128 * j : 128 * j + 128] = tiles_ref[
                    4 * i + 2 * part + j
                ].astype(jnp.float32)


def spectrum_kernel(
    mask_ref, step_ref, phase_ref, base_ref, shift_ref, grid_base_ref, grid_shift_ref, target_ref,
    out_ref, grid_out_ref,
    grid_ref, held_ref, steps_ref, phases_ref, bases_ref, shifts_ref, grid_bases_ref, grid_shifts_ref, targets_ref,
    stack_a, stack_b, product_a, product_b, re_ref, im_ref, flat_ref, sems,
):
    rows = mask_ref.shape[0]
    grid_rows = target_ref.shape[0]
    stacks = (stack_a, stack_b)
    products = (product_a, product_b)
    count = rows // CHUNK
    places = [pl.ds(i * CHUNK, CHUNK) for i in range(count)]
    chunks = [
        pltpu.make_async_copy(mask_ref.at[places[i]], held_ref.at[places[i]], sems.at[i]) for i in range(count)
    ]
    small = [
        pltpu.make_async_copy(source, target, sems.at[count + i])
        for i, (source, target) in enumerate(
            (
                (step_ref, steps_ref),
                (phase_ref, phases_ref),
                (grid_base_ref, grid_bases_ref),
                (grid_shift_ref.at[lax.axis_index("rows")], grid_shifts_ref),
                (target_ref, targets_ref),
                (base_ref, bases_ref),
                (shift_ref.at[device_place()], shifts_ref),
            )
        )
    ]
    grid_copy = pltpu.make_async_copy(grid_ref, grid_out_ref, sems.at[count + 7])
    chunks[0].start()
    small[0].start()
    small[1].start()
    chunks[1].start()
    for copy in small[2:5] + chunks[2:] + small[5:]:
        copy.start()

    def steps_of(quarter):
        return range(quarter * STEPS // QUARTERS, (quarter + 1) * STEPS // QUARTERS)

    def transmit(i, quarter):
        total = None
        for step in steps_of(quarter):
            value = jnp.tanh(held_ref[places[i], step * STEP : (step + 1) * STEP])
            stacks[i % 2][step * CHUNK : (step + 1) * CHUNK] = value.astype(jnp.bfloat16)
            both = value[:, :HALF] + value[:, HALF:]
            total = both if total is None else total + both
        flat_ref[places[i]] = total if quarter == 0 else flat_ref[places[i]] + total

    def multiply(i, quarter):
        here = slice(steps_of(quarter).start * CHUNK, steps_of(quarter).stop * CHUNK)
        products[i % 2][here] = float_dot(stacks[i % 2][here], steps_ref[...])

    def gather(i, quarter):
        totals = [None] * 4
        for step in steps_of(quarter):
            cosine = phases_ref[step : step + 1, :HALF]
            sine = phases_ref[step : step + 1, HALF:]
            first = products[i % 2][step * CHUNK : (step + 1) * CHUNK, :HALF]
            second = products[i % 2][step * CHUNK : (step + 1) * CHUNK, HALF:]
            at = 2 * (step % 2)
            for part, turned in enumerate(
                (first * cosine + second * sine, second * cosine - first * sine)
            ):
                totals[at + part] = turned if totals[at + part] is None else totals[at + part] + turned
        total_re = totals[0] + totals[2]
        total_im = totals[1] + totals[3]
        re_ref[places[i]] = total_re if quarter == 0 else re_ref[places[i]] + total_re
        im_ref[places[i]] = total_im if quarter == 0 else im_ref[places[i]] + total_im

    chunks[0].wait()
    for quarter in range(QUARTERS):
        transmit(0, quarter)
    small[0].wait()
    small[1].wait()
    for i in range(count):
        if i + 1 < count:
            chunks[i + 1].wait()
        for quarter in range(QUARTERS):
            multiply(i, quarter)
            if i + 1 < count:
                transmit(i + 1, quarter)
            if i > 0:
                gather(i - 1, quarter)
        if i == 1:
            for copy in small[2:5]:
                copy.wait()
            cosine, sine = turned_table(grid_bases_ref[...], grid_shifts_ref[...])
            grid_ref[:grid_rows, :BAND] = cosine.astype(jnp.bfloat16)
            grid_ref[:grid_rows, BAND:] = sine.astype(jnp.bfloat16)
            grid_ref[grid_rows:] = targets_ref[...].astype(jnp.float32).astype(jnp.bfloat16)
            grid_copy.start()
    for quarter in range(QUARTERS):
        gather(count - 1, quarter)
    for copy in small[5:]:
        copy.wait()
    _, lane = iotas((rows, HALF))
    mirror = conjugate_mirror()
    half_high, half_low = split(jnp.concatenate([re_ref[...], im_ref[...]], 1))
    other = float_dot(half_high, mirror) + float_dot(half_low, mirror)
    centre = jnp.sum(flat_ref[...], 1, keepdims=True) * (1.0 / MASK)
    other_high, other_low = split(
        jnp.concatenate([jnp.where(lane == 0, centre, other[:, :HALF]), other[:, HALF:]], 1)
    )
    high = jnp.concatenate([half_high, other_high], 1)
    low = jnp.concatenate([half_low, other_low], 1)
    product = float_dot(bases_ref[...], high)
    product = product[: 2 * BAND] + (product[2 * BAND :] + float_dot(bases_ref[: 2 * BAND], low))
    diagonal = jnp.equal(*iotas((BAND, BAND)))
    turn_cos, turn_sin = [
        jnp.sum(jnp.where(diagonal, shifts_ref[:, part * BAND : (part + 1) * BAND], 0.0), 1, keepdims=True)
        for part in range(2)
    ]
    by_cos = product[:BAND]
    by_sin = product[BAND:]
    real = []
    imag = []
    for at in (0, 2 * HALF):
        part_re = by_cos[:, at : at + HALF] + by_sin[:, at + HALF : at + 2 * HALF]
        part_im = by_cos[:, at + HALF : at + 2 * HALF] - by_sin[:, at : at + HALF]
        real.append(turn_cos * part_re + turn_sin * part_im)
        imag.append(turn_cos * part_im - turn_sin * part_re)
    store_tiles(out_ref, jnp.concatenate(real, 1), jnp.concatenate(imag, 1))
    grid_copy.wait()


def mask_spectrum(mask_params, step_value, phases, base, shifts, grid_base, grid_shifts, target):
    rows = mask_params.shape[0]
    stacked = STEPS * CHUNK
    arguments = (mask_params, step_value, phases, base, shifts, grid_base, grid_shifts, target)
    grid_rows = grid_base.shape[0]
    return pl.pallas_call(
        spectrum_kernel,
        in_specs=[pl.BlockSpec(memory_space=pltpu.HBM)] * len(arguments),
        out_specs=[pl.BlockSpec(memory_space=pltpu.VMEM), pl.BlockSpec(memory_space=pltpu.HBM)],
        out_shape=[
            jax.ShapeDtypeStruct((DEVICES, 8, 128), jnp.bfloat16),
            jax.ShapeDtypeStruct((2 * grid_rows, 2 * BAND), jnp.bfloat16),
        ],
        scratch_shapes=[
            pltpu.VMEM((2 * grid_rows, 2 * BAND), jnp.bfloat16),
            pltpu.VMEM((rows, MASK), jnp.float32),
            pltpu.VMEM(step_value.shape, jnp.bfloat16),
            pltpu.VMEM(phases.shape, jnp.float32),
            pltpu.VMEM(base.shape, jnp.bfloat16),
            pltpu.VMEM((1, 2 * BAND), jnp.float32),
            pltpu.VMEM(grid_base.shape, jnp.float32),
            pltpu.VMEM((1, 2 * BAND), jnp.float32),
            pltpu.VMEM(target.shape, jnp.int32),
            pltpu.VMEM((stacked, STEP), jnp.bfloat16),
            pltpu.VMEM((stacked, STEP), jnp.bfloat16),
            pltpu.VMEM((stacked, BAND), jnp.float32),
            pltpu.VMEM((stacked, BAND), jnp.float32),
            pltpu.VMEM((rows, HALF), jnp.float32),
            pltpu.VMEM((rows, HALF), jnp.float32),
            pltpu.VMEM((rows, HALF), jnp.float32),
            pltpu.SemaphoreType.DMA((rows // CHUNK + 8,)),
        ],
        compiler_params=params(FIRST_LIMIT),
        name="mask_spectrum",
    )(*arguments)


def field_kernel(tiles_ref, pupil_ref, grid_ref, map_ref, field_ref, power_ref, spec_ref, partial_ref):
    members = pupil_ref.shape[0]
    rows = grid_ref.shape[0] // 2
    slab = rows // KERN
    load_tiles(tiles_ref, spec_ref)
    spec_re = spec_ref[0]
    spec_im = spec_ref[1]
    for member in range(members):
        for corner in range(2):
            kernel_re = pupil_ref[member, corner, 0]
            kernel_im = pupil_ref[member, corner, 1]
            amp_re = (kernel_re * spec_re - kernel_im * spec_im).astype(jnp.bfloat16)
            amp_im = (kernel_re * spec_im + kernel_im * spec_re).astype(jnp.bfloat16)
            block = jnp.concatenate(
                [jnp.concatenate([amp_re, amp_im], 1), jnp.concatenate([-amp_im, amp_re], 1)], 0
            )
            partial_ref[member, corner * rows : (corner + 1) * rows] = float_dot(grid_ref[:rows], block).astype(
                jnp.bfloat16
            )
        field_ref[member] = float_dot(partial_ref[member], map_ref[...])
    for owner in range(KERN):
        power_ref[owner, 2] = grid_ref[rows + owner * slab : rows + (owner + 1) * slab]
        for corner in range(2):
            at = corner * rows + owner * slab
            power = None
            for member in range(members):
                real = field_ref[member, at : at + slab, :COARSE]
                imag = field_ref[member, at : at + slab, COARSE:]
                term = real * real + imag * imag
                power = term if member == 0 else power + term
            power_ref[owner, corner] = power.astype(jnp.bfloat16)


def coarse_fields(tiles, pupils, grid_table, column_map):
    members = pupils.shape[0]
    rows = grid_table.shape[0] // 2
    vmem = pl.BlockSpec(memory_space=pltpu.VMEM)
    return pl.pallas_call(
        field_kernel,
        in_specs=[vmem] * 4,
        out_specs=[vmem] * 2,
        out_shape=[
            jax.ShapeDtypeStruct((members, 2 * rows, 2 * COARSE), jnp.float32),
            jax.ShapeDtypeStruct((KERN, 3, rows // KERN, COARSE), jnp.bfloat16),
        ],
        scratch_shapes=[
            pltpu.VMEM((2, BAND, BAND), jnp.float32),
            pltpu.VMEM((members, 2 * rows, 2 * BAND), jnp.bfloat16),
        ],
        compiler_params=params(),
        name="coarse_fields",
    )(tiles, pupils, grid_table, column_map)


def adjoint_kernel(parts_ref, matrix_ref, out_ref):
    rows = parts_ref.shape[2]
    width = GRID // KERN
    powers = []
    for corner in range(2):
        total = parts_ref[0, corner].astype(jnp.float32)
        for owner in range(1, KERN):
            total = total + parts_ref[owner, corner].astype(jnp.float32)
        powers.append(total.astype(jnp.bfloat16))
    power = jnp.concatenate(powers, 0)
    folded = None
    for slab in range(KERN):
        columns = slice(slab * width, (slab + 1) * width)
        fine = float_dot(power, matrix_ref[:, columns])
        wanted = parts_ref[slab, 2].astype(jnp.float32)
        corners = []
        for corner in range(2):
            dose = dose_levels[corner]
            resist = jax.nn.sigmoid(steepness * (dose * fine[corner * rows : (corner + 1) * rows] - threshold))
            corners.append(
                (2.0 * (resist - wanted) * resist * (1.0 - resist) * steepness * dose).astype(jnp.bfloat16)
            )
        term = dot_last(jnp.concatenate(corners, 0), matrix_ref[:, columns])
        folded = term if slab == 0 else folded + term
    folded = folded.reshape(2, rows, COARSE).astype(jnp.bfloat16)
    for owner in range(KERN):
        out_ref[owner] = folded


def coarse_adjoint(parts, matrix):
    rows = parts.shape[2]
    return pl.pallas_call(
        adjoint_kernel,
        in_specs=[pl.BlockSpec(memory_space=pltpu.VMEM)] * 2,
        out_specs=pl.BlockSpec(memory_space=pltpu.VMEM),
        out_shape=jax.ShapeDtypeStruct((KERN, 2, rows, COARSE), jnp.bfloat16),
        compiler_params=params(),
        name="coarse_adjoint",
    )(parts, matrix)


def gradient_kernel(field_ref, adjoint_ref, pupil_ref, grid_ref, map_ref, out_ref, weighted_ref, back_ref, acc_ref):
    members = pupil_ref.shape[0]
    slab = adjoint_ref.shape[2]
    rows = slab * KERN
    for member in range(members):
        for corner in range(2):
            for owner in range(KERN):
                at = corner * rows + owner * slab
                adjoint = 2.0 * adjoint_ref[owner, corner].astype(jnp.float32)
                for half in range(2):
                    columns = slice(half * COARSE, (half + 1) * COARSE)
                    weighted_ref[member, at : at + slab, columns] = (
                        field_ref[member, at : at + slab, columns] * adjoint
                    ).astype(jnp.bfloat16)
        back_ref[member] = dot_last(weighted_ref[member], map_ref[...]).astype(jnp.bfloat16)
        for corner in range(2):
            grads = dot_first(grid_ref[:rows], back_ref[member, corner * rows : (corner + 1) * rows])
            grad_re = grads[:BAND, :BAND] + grads[BAND:, BAND:]
            grad_im = grads[:BAND, BAND:] - grads[BAND:, :BAND]
            kernel_re = pupil_ref[member, corner, 0]
            kernel_im = pupil_ref[member, corner, 1]
            term_re = kernel_re * grad_re + kernel_im * grad_im
            term_im = kernel_re * grad_im - kernel_im * grad_re
            first = member == 0 and corner == 0
            acc_ref[0] = term_re if first else acc_ref[0] + term_re
            acc_ref[1] = term_im if first else acc_ref[1] + term_im
    store_tiles(out_ref, acc_ref[0], acc_ref[1])


def spectrum_gradient(fields, adjoint, pupils, grid_table, column_map):
    members = pupils.shape[0]
    rows = grid_table.shape[0] // 2
    vmem = pl.BlockSpec(memory_space=pltpu.VMEM)
    return pl.pallas_call(
        gradient_kernel,
        in_specs=[vmem] * 5,
        out_specs=vmem,
        out_shape=jax.ShapeDtypeStruct((DEVICES, 8, 128), jnp.bfloat16),
        scratch_shapes=[
            pltpu.VMEM((members, 2 * rows, 2 * COARSE), jnp.bfloat16),
            pltpu.VMEM((members, 2 * rows, 2 * BAND), jnp.bfloat16),
            pltpu.VMEM((2, BAND, BAND), jnp.float32),
        ],
        compiler_params=params(),
        name="spectrum_gradient",
    )(fields, adjoint, pupils, grid_table, column_map)


def update_kernel(
    tiles_ref, base_ref, shift_ref, mask_ref, step_ref, phase_ref, out_ref,
    tile_ref, spec_ref, bases_ref, shifts_ref, held_ref, steps_ref, phases_ref, re_ref, im_ref, flat_ref, stack_a, stack_b, product_a, product_b, sems,
):
    rows = mask_ref.shape[0]
    stacks = (stack_a, stack_b)
    products = (product_a, product_b)
    count = rows // CHUNK
    places = [pl.ds(i * CHUNK, CHUNK) for i in range(count)]
    chunks = [
        pltpu.make_async_copy(mask_ref.at[places[i]], held_ref.at[places[i]], sems.at[i]) for i in range(count)
    ]
    results = [
        pltpu.make_async_copy(held_ref.at[places[i]], out_ref.at[places[i]], sems.at[count + i])
        for i in range(count)
    ]
    small = [
        pltpu.make_async_copy(source, target, sems.at[2 * count + i])
        for i, (source, target) in enumerate(
            (
                (base_ref, bases_ref),
                (shift_ref.at[device_place()], shifts_ref),
                (tiles_ref, tile_ref),
                (phase_ref, phases_ref),
                (step_ref, steps_ref),
            )
        )
    ]
    for copy in small + chunks:
        copy.start()

    small[0].wait()
    small[1].wait()
    cosine, sine = turned_table(bases_ref[...], shifts_ref[...])
    small[2].wait()
    load_tiles(tile_ref, spec_ref)
    gradient = jnp.concatenate([spec_ref[0], spec_ref[1]], 1).astype(jnp.bfloat16)
    product = float_dot(jnp.concatenate(split(cosine) + split(sine), 0), gradient)
    by_cos = product[:rows] + product[rows : 2 * rows]
    by_sin = product[2 * rows : 3 * rows] + product[3 * rows :]
    col_re = by_cos[:, :BAND] - by_sin[:, BAND:]
    col_im = by_sin[:, :BAND] + by_cos[:, BAND:]
    flat_ref[...] = jnp.broadcast_to(col_re[:, HALF : HALF + 1] * (1.0 / MASK), flat_ref.shape)
    mirror = conjugate_mirror()
    high, low = split(jnp.concatenate([col_re[:, HALF:], col_im[:, HALF:]], 1))
    other = float_dot(high, mirror) + float_dot(low, mirror)
    re_ref[...] = col_re[:, :HALF] + other[:, :HALF]
    im_ref[...] = col_im[:, :HALF] + other[:, HALF:]

    def steps_of(quarter):
        return range(quarter * STEPS // QUARTERS, (quarter + 1) * STEPS // QUARTERS)

    def turn(i, quarter):
        col_re = re_ref[places[i]]
        col_im = im_ref[places[i]]
        for step in steps_of(quarter):
            cosine = phases_ref[step : step + 1, :HALF]
            sine = phases_ref[step : step + 1, HALF:]
            here = slice(step * CHUNK, (step + 1) * CHUNK)
            stacks[i % 2][here, :HALF] = (col_re * cosine - col_im * sine).astype(jnp.bfloat16)
            stacks[i % 2][here, HALF:] = (col_re * sine + col_im * cosine).astype(jnp.bfloat16)

    def multiply(i, quarter):
        here = slice(steps_of(quarter).start * CHUNK, steps_of(quarter).stop * CHUNK)
        products[i % 2][here] = float_dot(stacks[i % 2][here], steps_ref[...])

    def finish(i, quarter):
        centre = flat_ref[places[i]]
        for step in steps_of(quarter):
            here = slice(step * STEP, (step + 1) * STEP)
            mask = held_ref[places[i], here]
            transmit = jnp.tanh(mask)
            pixel_grad = products[i % 2][step * CHUNK : (step + 1) * CHUNK] + centre
            held_ref[places[i], here] = mask - step_size * pixel_grad * (1.0 - transmit * transmit)

    small[3].wait()
    for quarter in range(QUARTERS):
        turn(0, quarter)
    small[4].wait()
    for i in range(count + 1):
        if i > 0:
            chunks[i - 1].wait()
        for quarter in range(QUARTERS):
            if i < count:
                multiply(i, quarter)
            if i + 1 < count:
                turn(i + 1, quarter)
            if i > 0:
                finish(i - 1, quarter)
        if i > 0:
            results[i - 1].start()
    for copy in results:
        copy.wait()


def mask_update(tiles, base, shifts, mask_params, step_value, phases):
    rows = mask_params.shape[0]
    stacked = STEPS * CHUNK
    hbm = pl.BlockSpec(memory_space=pltpu.HBM)
    return pl.pallas_call(
        update_kernel,
        in_specs=[hbm] * 6,
        out_specs=hbm,
        out_shape=jax.ShapeDtypeStruct((rows, MASK), jnp.float32),
        scratch_shapes=[
            pltpu.VMEM(tiles.shape, jnp.bfloat16),
            pltpu.VMEM((2, BAND, BAND), jnp.float32),
            pltpu.VMEM(base.shape, jnp.float32),
            pltpu.VMEM((1, 2 * BAND), jnp.float32),
            pltpu.VMEM((rows, MASK), jnp.float32),
            pltpu.VMEM(step_value.shape, jnp.bfloat16),
            pltpu.VMEM(phases.shape, jnp.float32),
            pltpu.VMEM((rows, HALF), jnp.float32),
            pltpu.VMEM((rows, HALF), jnp.float32),
            pltpu.VMEM((rows, STEP), jnp.float32),
            pltpu.VMEM((stacked, BAND), jnp.bfloat16),
            pltpu.VMEM((stacked, BAND), jnp.bfloat16),
            pltpu.VMEM((stacked, STEP), jnp.float32),
            pltpu.VMEM((stacked, STEP), jnp.float32),
            pltpu.SemaphoreType.DMA((2 * (rows // CHUNK) + 5,)),
        ],
        compiler_params=params(STREAM_LIMIT),
        name="mask_update",
    )(tiles, base, shifts, mask_params, step_value, phases)


def exchange(values, axes):
    return lax.all_to_all(values, axes, 0, 0, tiled=True)


def summed(parts, copies):
    total = jnp.sum(parts.astype(jnp.float32), 0).astype(parts.dtype)
    return jnp.broadcast_to(total[None], (copies,) + total.shape)


def sum_tiles(tiles):
    everyone = ("rows", "kern")
    return exchange(summed(exchange(tiles, everyone), DEVICES), everyone)


def local(mask_params, pupil_kernels, target_pattern):
    rows = mask_params.shape[0]
    grid_rows = target_pattern.shape[0]
    step_value = step_table()
    phases = jnp.asarray(wide_table(np.arange(STEPS) * STEP, MASK, HALF))
    mask_base = jnp.asarray(wide_table(np.arange(rows), MASK))
    mask_transform = jnp.asarray(row_transform(rows))
    mask_shifts = jnp.asarray(wide_table(np.arange(ROWS * KERN) * rows, MASK)[:, None, :])
    grid_base = jnp.asarray(wide_table(np.arange(grid_rows), GRID))
    grid_shifts = jnp.asarray(wide_table(np.arange(ROWS) * grid_rows, GRID)[:, None, :])
    column_map = jnp.asarray(coarse_map())

    tiles, grid_table = mask_spectrum(
        mask_params, jnp.asarray(step_value), phases, mask_transform, mask_shifts, grid_base, grid_shifts, target_pattern
    )
    fields, powers = coarse_fields(sum_tiles(tiles), pupil_kernels, grid_table, column_map)
    adjoint = coarse_adjoint(exchange(powers, "kern"), jnp.asarray(interpolation()))
    gradient = spectrum_gradient(fields, exchange(adjoint, "kern"), pupil_kernels, grid_table, column_map)
    return mask_update(
        sum_tiles(gradient), mask_base, mask_shifts, mask_params, jnp.asarray(step_value.T), phases
    )


def solution(mesh):
    placed = (P(("rows", "kern"), None), P("kern", None, None, None, None), P("rows", "kern"))
    return jax.shard_map(
        local, mesh=mesh, in_specs=placed, out_specs=P(("rows", "kern"), None), check_vma=False
    )
```

```python
import math

import jax
import jax.numpy as jnp
import numpy as np
from jax import lax
from jax.experimental import pallas as pl
from jax.experimental.pallas import tpu as pltpu
from jax.sharding import PartitionSpec as P

MASK = 16384
GRID = 4096
BAND = 256
HALF = BAND // 2
COARSE = 512
STEP = 256
STEPS = MASK // STEP
ROWS = 16
KERN = 8
DEVICES = ROWS * KERN
CHUNK = 16
QUARTERS = 4

steepness = 4.0
threshold = 0.75
step_size = 1.0
dose_levels = (1.0, 1.15)

VMEM_LIMIT = 24 * 1024 * 1024
STREAM_LIMIT = 53 * 1024 * 1024


def tables(positions, period, count=BAND):
    frequency = np.arange(count) - BAND // 2
    angles = (np.outer(positions, frequency) % period) * (2.0 * math.pi / period)
    return np.cos(angles), np.sin(angles)


def bfloat(values):
    return np.asarray(values, np.float32).astype(jnp.bfloat16)


def wide_table(positions, period, count=BAND):
    return np.concatenate(tables(positions, period, count), 1).astype(np.float32)


def step_table():
    cosine, sine = tables(np.arange(STEP), MASK, HALF)
    return bfloat(np.concatenate([cosine, -sine], 1) / MASK)


def row_transform(rows):
    table = wide_table(np.arange(rows), MASK).T
    high = bfloat(table)
    return np.concatenate([high, bfloat(table - high.astype(np.float32))], 0)


TABLE_ROWS = {"grid": GRID, "base": 128, "shift": DEVICES, "phase": STEPS, "step": STEP, "transform": STEP}


def constant_table(rows):
    step = step_table().astype(np.float32)
    transform = row_transform(rows).astype(np.float32)
    parts = {
        "grid": wide_table(np.arange(GRID), GRID),
        "base": wide_table(np.arange(rows), MASK),
        "shift": wide_table(np.arange(DEVICES) * rows, MASK),
        "phase": np.pad(wide_table(np.arange(STEPS) * STEP, MASK, HALF), ((0, 0), (0, BAND))),
        "step": np.concatenate([step, step.T], 1),
        "transform": np.concatenate(np.split(transform, 4, 0), 1),
    }
    return np.concatenate([parts[name] for name in TABLE_ROWS], 0)


def table_rows(name, start=0, count=None):
    names = list(TABLE_ROWS)
    first = sum(TABLE_ROWS[before] for before in names[: names.index(name)])
    return pl.ds(pl.multiple_of(first + start, 8), TABLE_ROWS[name] if count is None else count)


def shift_group():
    return table_rows("shift", 8 * (device_place() // 8), 8)


def own_shift(shifts_ref):
    return shifts_ref[pl.ds(lax.rem(device_place(), 8), 1), :]


def coarse_map():
    cosine, sine = tables(np.arange(COARSE), COARSE)
    upper = np.concatenate([cosine.T, sine.T], 1)
    lower = np.concatenate([-sine.T, cosine.T], 1)
    return bfloat(np.concatenate([upper, lower], 0))


def interpolation():
    ratio = GRID // COARSE
    frequency = np.arange(1, COARSE // 2)
    offset = np.arange(GRID)
    profile = 1.0 + 2.0 * np.cos(2.0 * math.pi * (np.outer(offset, frequency) % GRID) / GRID).sum(1)
    profile = (profile + np.cos(math.pi * offset / ratio)) / COARSE
    return bfloat(profile[(offset[None, :] - ratio * np.arange(COARSE)[:, None]) % GRID])


def device_place():
    return lax.axis_index("rows") * KERN + lax.axis_index("kern")


def turned_table(base, shift):
    cosine = base[:, :BAND] * shift[:, :BAND] - base[:, BAND:] * shift[:, BAND:]
    sine = base[:, BAND:] * shift[:, :BAND] + base[:, :BAND] * shift[:, BAND:]
    return cosine, sine


def params(limit=VMEM_LIMIT):
    return pltpu.CompilerParams(vmem_limit_bytes=limit)


def float_dot(left, right):
    return jnp.dot(left, right, preferred_element_type=jnp.float32)


def dot_first(left, right, precision=None):
    return lax.dot_general(
        left, right, (((0,), (0,)), ((), ())), precision=precision, preferred_element_type=jnp.float32
    )


def dot_last(left, right):
    return lax.dot_general(left, right, (((1,), (1,)), ((), ())), preferred_element_type=jnp.float32)


def split(values):
    high = values.astype(jnp.bfloat16)
    return high, (values - high.astype(jnp.float32)).astype(jnp.bfloat16)


def iotas(shape):
    return lax.broadcasted_iota(jnp.int32, shape, 0), lax.broadcasted_iota(jnp.int32, shape, 1)


def conjugate_mirror():
    row, column = iotas((BAND, BAND))
    real = (row + column == HALF) & (row < HALF) & (column > 0) & (column < HALF)
    imag = (row + column == 2 * HALF + HALF) & (row >= HALF) & (column > HALF)
    return (jnp.where(real, 1.0, 0.0) - jnp.where(imag, 1.0, 0.0)).astype(jnp.bfloat16)


def store_tiles(out_ref, real, imag):
    for part, value in enumerate((real, imag)):
        for i in range(BAND // 8):
            for j in range(2):
                out_ref[4 * i + 2 * part + j] = value[8 * i : 8 * i + 8, 128 * j : 128 * j + 128].astype(
                    out_ref.dtype
                )


def load_tiles(tiles_ref, held_ref):
    for part in range(2):
        for i in range(BAND // 8):
            for j in range(2):
                held_ref[part, 8 * i : 8 * i + 8, 128 * j : 128 * j + 128] = tiles_ref[
                    4 * i + 2 * part + j
                ].astype(jnp.float32)


def spectrum_kernel(
    mask_ref, constant_ref, target_ref, out_ref, grid_out_ref,
    grid_ref, held_ref, steps_ref, phases_ref, bases_ref, shifts_ref, grid_rows_ref, targets_ref,
    stack_a, stack_b, product_a, product_b, re_ref, im_ref, flat_ref, sems,
):
    rows = mask_ref.shape[0]
    grid_rows = target_ref.shape[0]
    stacks = (stack_a, stack_b)
    products = (product_a, product_b)
    count = rows // CHUNK
    places = [pl.ds(i * CHUNK, CHUNK) for i in range(count)]
    chunks = [
        pltpu.make_async_copy(mask_ref.at[places[i]], held_ref.at[places[i]], sems.at[i]) for i in range(count)
    ]
    small = [
        pltpu.make_async_copy(source, target, sems.at[count + i])
        for i, (source, target) in enumerate(
            (
                (constant_ref.at[table_rows("step")], steps_ref),
                (constant_ref.at[table_rows("phase")], phases_ref),
                (constant_ref.at[table_rows("grid", lax.axis_index("rows") * grid_rows, grid_rows)], grid_rows_ref),
                (target_ref, targets_ref),
                (constant_ref.at[table_rows("transform")], bases_ref),
                (constant_ref.at[shift_group()], shifts_ref),
            )
        )
    ]
    grid_copy = pltpu.make_async_copy(grid_ref, grid_out_ref, sems.at[count + 6])
    chunks[0].start()
    small[0].start()
    small[1].start()
    chunks[1].start()
    for copy in small[2:4] + chunks[2:] + small[4:]:
        copy.start()

    def steps_of(quarter):
        return range(quarter * STEPS // QUARTERS, (quarter + 1) * STEPS // QUARTERS)

    def transmit(i, quarter):
        total = None
        for step in steps_of(quarter):
            value = jnp.tanh(held_ref[places[i], step * STEP : (step + 1) * STEP])
            stacks[i % 2][step * CHUNK : (step + 1) * CHUNK] = value.astype(jnp.bfloat16)
            both = value[:, :HALF] + value[:, HALF:]
            total = both if total is None else total + both
        flat_ref[places[i]] = total if quarter == 0 else flat_ref[places[i]] + total

    def multiply(i, quarter):
        here = slice(steps_of(quarter).start * CHUNK, steps_of(quarter).stop * CHUNK)
        products[i % 2][here] = float_dot(stacks[i % 2][here], step_value)

    def gather(i, quarter):
        totals = [None] * 4
        for step in steps_of(quarter):
            cosine = phases_ref[step : step + 1, :HALF]
            sine = phases_ref[step : step + 1, HALF:BAND]
            first = products[i % 2][step * CHUNK : (step + 1) * CHUNK, :HALF]
            second = products[i % 2][step * CHUNK : (step + 1) * CHUNK, HALF:]
            at = 2 * (step % 2)
            for part, turned in enumerate(
                (first * cosine + second * sine, second * cosine - first * sine)
            ):
                totals[at + part] = turned if totals[at + part] is None else totals[at + part] + turned
        total_re = totals[0] + totals[2]
        total_im = totals[1] + totals[3]
        re_ref[places[i]] = total_re if quarter == 0 else re_ref[places[i]] + total_re
        im_ref[places[i]] = total_im if quarter == 0 else im_ref[places[i]] + total_im

    chunks[0].wait()
    for quarter in range(QUARTERS):
        transmit(0, quarter)
    small[0].wait()
    small[1].wait()
    step_value = steps_ref[:, :BAND].astype(jnp.bfloat16)
    for i in range(count):
        if i + 1 < count:
            chunks[i + 1].wait()
        for quarter in range(QUARTERS):
            multiply(i, quarter)
            if i + 1 < count:
                transmit(i + 1, quarter)
            if i > 0:
                gather(i - 1, quarter)
        if i == 1:
            for copy in small[2:4]:
                copy.wait()
            grid_ref[:grid_rows] = grid_rows_ref[...].astype(jnp.bfloat16)
            grid_ref[grid_rows:] = targets_ref[...].astype(jnp.float32).astype(jnp.bfloat16)
            grid_copy.start()
    for quarter in range(QUARTERS):
        gather(count - 1, quarter)
    for copy in small[4:]:
        copy.wait()
    _, lane = iotas((rows, HALF))
    mirror = conjugate_mirror()
    half_high, half_low = split(jnp.concatenate([re_ref[...], im_ref[...]], 1))
    other = float_dot(half_high, mirror) + float_dot(half_low, mirror)
    centre = jnp.sum(flat_ref[...], 1, keepdims=True) * (1.0 / MASK)
    other_high, other_low = split(
        jnp.concatenate([jnp.where(lane == 0, centre, other[:, :HALF]), other[:, HALF:]], 1)
    )
    high = jnp.concatenate([half_high, other_high], 1)
    low = jnp.concatenate([half_low, other_low], 1)
    transform = [bases_ref[:, at * rows : (at + 1) * rows].astype(jnp.bfloat16) for at in range(4)]
    product = float_dot(jnp.concatenate(transform, 0), high)
    rest = float_dot(jnp.concatenate(transform[:2], 0), low)
    product = product[: 2 * BAND] + (product[2 * BAND :] + rest)
    diagonal = jnp.equal(*iotas((BAND, BAND)))
    shift = own_shift(shifts_ref)
    turn_cos, turn_sin = [
        jnp.sum(jnp.where(diagonal, shift[:, part * BAND : (part + 1) * BAND], 0.0), 1, keepdims=True)
        for part in range(2)
    ]
    by_cos = product[:BAND]
    by_sin = product[BAND:]
    real = []
    imag = []
    for at in (0, 2 * HALF):
        part_re = by_cos[:, at : at + HALF] + by_sin[:, at + HALF : at + 2 * HALF]
        part_im = by_cos[:, at + HALF : at + 2 * HALF] - by_sin[:, at : at + HALF]
        real.append(turn_cos * part_re + turn_sin * part_im)
        imag.append(turn_cos * part_im - turn_sin * part_re)
    store_tiles(out_ref, jnp.concatenate(real, 1), jnp.concatenate(imag, 1))
    grid_copy.wait()


def mask_spectrum(mask_params, constants, target):
    rows = mask_params.shape[0]
    stacked = STEPS * CHUNK
    arguments = (mask_params, constants, target)
    grid_rows = target.shape[0]
    return pl.pallas_call(
        spectrum_kernel,
        in_specs=[pl.BlockSpec(memory_space=pltpu.HBM)] * len(arguments),
        out_specs=[pl.BlockSpec(memory_space=pltpu.VMEM), pl.BlockSpec(memory_space=pltpu.HBM)],
        out_shape=[
            jax.ShapeDtypeStruct((DEVICES, 8, 128), jnp.bfloat16),
            jax.ShapeDtypeStruct((2 * grid_rows, 2 * BAND), jnp.bfloat16),
        ],
        scratch_shapes=[
            pltpu.VMEM((2 * grid_rows, 2 * BAND), jnp.bfloat16),
            pltpu.VMEM((rows, MASK), jnp.float32),
            pltpu.VMEM((STEP, 2 * BAND), jnp.float32),
            pltpu.VMEM((STEPS, 2 * BAND), jnp.float32),
            pltpu.VMEM((STEP, 2 * BAND), jnp.float32),
            pltpu.VMEM((8, 2 * BAND), jnp.float32),
            pltpu.VMEM((grid_rows, 2 * BAND), jnp.float32),
            pltpu.VMEM(target.shape, jnp.int32),
            pltpu.VMEM((stacked, STEP), jnp.bfloat16),
            pltpu.VMEM((stacked, STEP), jnp.bfloat16),
            pltpu.VMEM((stacked, BAND), jnp.float32),
            pltpu.VMEM((stacked, BAND), jnp.float32),
            pltpu.VMEM((rows, HALF), jnp.float32),
            pltpu.VMEM((rows, HALF), jnp.float32),
            pltpu.VMEM((rows, HALF), jnp.float32),
            pltpu.SemaphoreType.DMA((rows // CHUNK + 7,)),
        ],
        compiler_params=params(STREAM_LIMIT),
        name="mask_spectrum",
    )(*arguments)


def field_kernel(tiles_ref, pupil_ref, grid_ref, map_ref, field_ref, power_ref, spec_ref, partial_ref):
    members = pupil_ref.shape[0]
    rows = grid_ref.shape[0] // 2
    slab = rows // KERN
    load_tiles(tiles_ref, spec_ref)
    spec_re = spec_ref[0]
    spec_im = spec_ref[1]
    for member in range(members):
        for corner in range(2):
            kernel_re = pupil_ref[member, corner, 0]
            kernel_im = pupil_ref[member, corner, 1]
            amp_re = (kernel_re * spec_re - kernel_im * spec_im).astype(jnp.bfloat16)
            amp_im = (kernel_re * spec_im + kernel_im * spec_re).astype(jnp.bfloat16)
            block = jnp.concatenate(
                [jnp.concatenate([amp_re, amp_im], 1), jnp.concatenate([-amp_im, amp_re], 1)], 0
            )
            partial_ref[member, corner * rows : (corner + 1) * rows] = float_dot(grid_ref[:rows], block).astype(
                jnp.bfloat16
            )
        field_ref[member] = float_dot(partial_ref[member], map_ref[...])
    for owner in range(KERN):
        power_ref[owner, 2] = grid_ref[rows + owner * slab : rows + (owner + 1) * slab]
        for corner in range(2):
            at = corner * rows + owner * slab
            power = None
            for member in range(members):
                real = field_ref[member, at : at + slab, :COARSE]
                imag = field_ref[member, at : at + slab, COARSE:]
                term = real * real + imag * imag
                power = term if member == 0 else power + term
            power_ref[owner, corner] = power.astype(jnp.bfloat16)


def coarse_fields(tiles, pupils, grid_table, column_map):
    members = pupils.shape[0]
    rows = grid_table.shape[0] // 2
    vmem = pl.BlockSpec(memory_space=pltpu.VMEM)
    return pl.pallas_call(
        field_kernel,
        in_specs=[vmem] * 4,
        out_specs=[vmem] * 2,
        out_shape=[
            jax.ShapeDtypeStruct((members, 2 * rows, 2 * COARSE), jnp.float32),
            jax.ShapeDtypeStruct((KERN, 3, rows // KERN, COARSE), jnp.bfloat16),
        ],
        scratch_shapes=[
            pltpu.VMEM((2, BAND, BAND), jnp.float32),
            pltpu.VMEM((members, 2 * rows, 2 * BAND), jnp.bfloat16),
        ],
        compiler_params=params(),
        name="coarse_fields",
    )(tiles, pupils, grid_table, column_map)


def adjoint_kernel(parts_ref, matrix_ref, out_ref):
    rows = parts_ref.shape[2]
    width = GRID // KERN
    powers = []
    for corner in range(2):
        total = parts_ref[0, corner].astype(jnp.float32)
        for owner in range(1, KERN):
            total = total + parts_ref[owner, corner].astype(jnp.float32)
        powers.append(total.astype(jnp.bfloat16))
    power = jnp.concatenate(powers, 0)
    folded = None
    for slab in range(KERN):
        columns = slice(slab * width, (slab + 1) * width)
        fine = float_dot(power, matrix_ref[:, columns])
        wanted = parts_ref[slab, 2].astype(jnp.float32)
        corners = []
        for corner in range(2):
            dose = dose_levels[corner]
            resist = jax.nn.sigmoid(steepness * (dose * fine[corner * rows : (corner + 1) * rows] - threshold))
            corners.append(
                (2.0 * (resist - wanted) * resist * (1.0 - resist) * steepness * dose).astype(jnp.bfloat16)
            )
        term = dot_last(jnp.concatenate(corners, 0), matrix_ref[:, columns])
        folded = term if slab == 0 else folded + term
    folded = folded.reshape(2, rows, COARSE).astype(jnp.bfloat16)
    for owner in range(KERN):
        out_ref[owner] = folded


def coarse_adjoint(parts, matrix):
    rows = parts.shape[2]
    return pl.pallas_call(
        adjoint_kernel,
        in_specs=[pl.BlockSpec(memory_space=pltpu.VMEM)] * 2,
        out_specs=pl.BlockSpec(memory_space=pltpu.VMEM),
        out_shape=jax.ShapeDtypeStruct((KERN, 2, rows, COARSE), jnp.bfloat16),
        compiler_params=params(),
        name="coarse_adjoint",
    )(parts, matrix)


def gradient_kernel(field_ref, adjoint_ref, pupil_ref, grid_ref, map_ref, out_ref, weighted_ref, back_ref, acc_ref):
    members = pupil_ref.shape[0]
    slab = adjoint_ref.shape[2]
    rows = slab * KERN
    for member in range(members):
        for corner in range(2):
            for owner in range(KERN):
                at = corner * rows + owner * slab
                adjoint = 2.0 * adjoint_ref[owner, corner].astype(jnp.float32)
                for half in range(2):
                    columns = slice(half * COARSE, (half + 1) * COARSE)
                    weighted_ref[member, at : at + slab, columns] = (
                        field_ref[member, at : at + slab, columns] * adjoint
                    ).astype(jnp.bfloat16)
        back_ref[member] = dot_last(weighted_ref[member], map_ref[...]).astype(jnp.bfloat16)
        for corner in range(2):
            grads = dot_first(grid_ref[:rows], back_ref[member, corner * rows : (corner + 1) * rows])
            grad_re = grads[:BAND, :BAND] + grads[BAND:, BAND:]
            grad_im = grads[:BAND, BAND:] - grads[BAND:, :BAND]
            kernel_re = pupil_ref[member, corner, 0]
            kernel_im = pupil_ref[member, corner, 1]
            term_re = kernel_re * grad_re + kernel_im * grad_im
            term_im = kernel_re * grad_im - kernel_im * grad_re
            first = member == 0 and corner == 0
            acc_ref[0] = term_re if first else acc_ref[0] + term_re
            acc_ref[1] = term_im if first else acc_ref[1] + term_im
    store_tiles(out_ref, acc_ref[0], acc_ref[1])


def spectrum_gradient(fields, adjoint, pupils, grid_table, column_map):
    members = pupils.shape[0]
    rows = grid_table.shape[0] // 2
    vmem = pl.BlockSpec(memory_space=pltpu.VMEM)
    return pl.pallas_call(
        gradient_kernel,
        in_specs=[vmem] * 5,
        out_specs=vmem,
        out_shape=jax.ShapeDtypeStruct((DEVICES, 8, 128), jnp.bfloat16),
        scratch_shapes=[
            pltpu.VMEM((members, 2 * rows, 2 * COARSE), jnp.bfloat16),
            pltpu.VMEM((members, 2 * rows, 2 * BAND), jnp.bfloat16),
            pltpu.VMEM((2, BAND, BAND), jnp.float32),
        ],
        compiler_params=params(),
        name="spectrum_gradient",
    )(fields, adjoint, pupils, grid_table, column_map)


def update_kernel(
    tiles_ref, constant_ref, mask_ref, out_ref,
    tile_ref, spec_ref, bases_ref, shifts_ref, held_ref, steps_ref, phases_ref, re_ref, im_ref, flat_ref, stack_a, stack_b, product_a, product_b, sems,
):
    rows = mask_ref.shape[0]
    stacks = (stack_a, stack_b)
    products = (product_a, product_b)
    count = rows // CHUNK
    places = [pl.ds(i * CHUNK, CHUNK) for i in range(count)]
    chunks = [
        pltpu.make_async_copy(mask_ref.at[places[i]], held_ref.at[places[i]], sems.at[i]) for i in range(count)
    ]
    results = [
        pltpu.make_async_copy(held_ref.at[places[i]], out_ref.at[places[i]], sems.at[count + i])
        for i in range(count)
    ]
    small = [
        pltpu.make_async_copy(source, target, sems.at[2 * count + i])
        for i, (source, target) in enumerate(
            (
                (constant_ref.at[table_rows("base")], bases_ref),
                (constant_ref.at[shift_group()], shifts_ref),
                (tiles_ref, tile_ref),
                (constant_ref.at[table_rows("phase")], phases_ref),
                (constant_ref.at[table_rows("step")], steps_ref),
            )
        )
    ]
    for copy in small + chunks:
        copy.start()

    small[0].wait()
    small[1].wait()
    cosine, sine = turned_table(bases_ref[...], own_shift(shifts_ref))
    small[2].wait()
    load_tiles(tile_ref, spec_ref)
    gradient = jnp.concatenate([spec_ref[0], spec_ref[1]], 1).astype(jnp.bfloat16)
    product = float_dot(jnp.concatenate(split(cosine) + split(sine), 0), gradient)
    by_cos = product[:rows] + product[rows : 2 * rows]
    by_sin = product[2 * rows : 3 * rows] + product[3 * rows :]
    col_re = by_cos[:, :BAND] - by_sin[:, BAND:]
    col_im = by_sin[:, :BAND] + by_cos[:, BAND:]
    flat_ref[...] = jnp.broadcast_to(col_re[:, HALF : HALF + 1] * (1.0 / MASK), flat_ref.shape)
    mirror = conjugate_mirror()
    high, low = split(jnp.concatenate([col_re[:, HALF:], col_im[:, HALF:]], 1))
    other = float_dot(high, mirror) + float_dot(low, mirror)
    re_ref[...] = col_re[:, :HALF] + other[:, :HALF]
    im_ref[...] = col_im[:, :HALF] + other[:, HALF:]

    def steps_of(quarter):
        return range(quarter * STEPS // QUARTERS, (quarter + 1) * STEPS // QUARTERS)

    def turn(i, quarter):
        col_re = re_ref[places[i]]
        col_im = im_ref[places[i]]
        for step in steps_of(quarter):
            cosine = phases_ref[step : step + 1, :HALF]
            sine = phases_ref[step : step + 1, HALF:BAND]
            here = slice(step * CHUNK, (step + 1) * CHUNK)
            stacks[i % 2][here, :HALF] = (col_re * cosine - col_im * sine).astype(jnp.bfloat16)
            stacks[i % 2][here, HALF:] = (col_re * sine + col_im * cosine).astype(jnp.bfloat16)

    def multiply(i, quarter):
        here = slice(steps_of(quarter).start * CHUNK, steps_of(quarter).stop * CHUNK)
        products[i % 2][here] = float_dot(stacks[i % 2][here], step_value)

    def finish(i, quarter):
        centre = flat_ref[places[i]]
        for step in steps_of(quarter):
            here = slice(step * STEP, (step + 1) * STEP)
            mask = held_ref[places[i], here]
            transmit = jnp.tanh(mask)
            pixel_grad = products[i % 2][step * CHUNK : (step + 1) * CHUNK] + centre
            held_ref[places[i], here] = mask - step_size * pixel_grad * (1.0 - transmit * transmit)

    small[3].wait()
    for quarter in range(QUARTERS):
        turn(0, quarter)
    small[4].wait()
    step_value = steps_ref[:, BAND:].astype(jnp.bfloat16)
    for i in range(count + 1):
        if i > 0:
            chunks[i - 1].wait()
        for quarter in range(QUARTERS):
            if i < count:
                multiply(i, quarter)
            if i + 1 < count:
                turn(i + 1, quarter)
            if i > 0:
                finish(i - 1, quarter)
        if i > 0:
            results[i - 1].start()
    for copy in results:
        copy.wait()


def mask_update(tiles, constants, mask_params):
    rows = mask_params.shape[0]
    stacked = STEPS * CHUNK
    hbm = pl.BlockSpec(memory_space=pltpu.HBM)
    return pl.pallas_call(
        update_kernel,
        in_specs=[hbm] * 3,
        out_specs=hbm,
        out_shape=jax.ShapeDtypeStruct((rows, MASK), jnp.float32),
        scratch_shapes=[
            pltpu.VMEM(tiles.shape, jnp.bfloat16),
            pltpu.VMEM((2, BAND, BAND), jnp.float32),
            pltpu.VMEM((rows, 2 * BAND), jnp.float32),
            pltpu.VMEM((8, 2 * BAND), jnp.float32),
            pltpu.VMEM((rows, MASK), jnp.float32),
            pltpu.VMEM((STEP, 2 * BAND), jnp.float32),
            pltpu.VMEM((STEPS, 2 * BAND), jnp.float32),
            pltpu.VMEM((rows, HALF), jnp.float32),
            pltpu.VMEM((rows, HALF), jnp.float32),
            pltpu.VMEM((rows, STEP), jnp.float32),
            pltpu.VMEM((stacked, BAND), jnp.bfloat16),
            pltpu.VMEM((stacked, BAND), jnp.bfloat16),
            pltpu.VMEM((stacked, STEP), jnp.float32),
            pltpu.VMEM((stacked, STEP), jnp.float32),
            pltpu.SemaphoreType.DMA((2 * (rows // CHUNK) + 5,)),
        ],
        compiler_params=params(STREAM_LIMIT),
        name="mask_update",
    )(tiles, constants, mask_params)


def exchange(values, axes):
    return lax.all_to_all(values, axes, 0, 0, tiled=True)


def summed(parts, copies):
    total = jnp.sum(parts.astype(jnp.float32), 0).astype(parts.dtype)
    return jnp.broadcast_to(total[None], (copies,) + total.shape)


def total_kernel(parts_ref, out_ref):
    total = jnp.sum(parts_ref[...].astype(jnp.float32), 0).astype(out_ref.dtype)
    for owner in range(DEVICES):
        out_ref[owner] = total


def total_tiles(parts):
    vmem = pl.BlockSpec(memory_space=pltpu.VMEM)
    return pl.pallas_call(
        total_kernel,
        in_specs=[vmem],
        out_specs=vmem,
        out_shape=jax.ShapeDtypeStruct(parts.shape, parts.dtype),
        compiler_params=params(),
        cost_estimate=pl.CostEstimate(flops=10**10, bytes_accessed=2 * parts.size, transcendentals=0),
        name="total_tiles",
    )(parts)


def local(mask_params, pupil_kernels, target_pattern):
    rows = mask_params.shape[0]
    constants = jnp.asarray(constant_table(rows))
    column_map = jnp.asarray(coarse_map())

    everyone = ("rows", "kern")
    tiles, grid_table = mask_spectrum(mask_params, constants, target_pattern)
    spectrum = exchange(total_tiles(exchange(tiles, everyone)), everyone)
    fields, powers = coarse_fields(spectrum, pupil_kernels, grid_table, column_map)
    adjoint = coarse_adjoint(exchange(powers, "kern"), jnp.asarray(interpolation()))
    gradient = spectrum_gradient(fields, exchange(adjoint, "kern"), pupil_kernels, grid_table, column_map)
    gradient = exchange(summed(exchange(gradient, everyone), DEVICES), everyone)
    return mask_update(gradient, constants, mask_params)


def solution(mesh):
    placed = (P(("rows", "kern"), None), P("kern", None, None, None, None), P("rows", "kern"))
    return jax.shard_map(
        local, mesh=mesh, in_specs=placed, out_specs=P(("rows", "kern"), None), check_vma=False
    )
```

```python
import math

import jax
import jax.numpy as jnp
import numpy as np
from jax import lax
from jax.experimental import pallas as pl
from jax.experimental.pallas import tpu as pltpu
from jax.sharding import PartitionSpec as P

MASK = 16384
GRID = 4096
BAND = 256
HALF = BAND // 2
COARSE = 512
STEP = 256
STEPS = MASK // STEP
ROWS = 16
KERN = 8
DEVICES = ROWS * KERN
CHUNK = 16
QUARTERS = 4

steepness = 4.0
threshold = 0.75
step_size = 1.0
dose_levels = (1.0, 1.15)

VMEM_LIMIT = 24 * 1024 * 1024
STREAM_LIMIT = 53 * 1024 * 1024


def tables(positions, period, count=BAND):
    frequency = np.arange(count) - BAND // 2
    angles = (np.outer(positions, frequency) % period) * (2.0 * math.pi / period)
    return np.cos(angles), np.sin(angles)


def bfloat(values):
    return np.asarray(values, np.float32).astype(jnp.bfloat16)


def wide_table(positions, period, count=BAND):
    return np.concatenate(tables(positions, period, count), 1).astype(np.float32)


def step_table():
    cosine, sine = tables(np.arange(STEP), MASK, HALF)
    return bfloat(np.concatenate([cosine, -sine], 1) / MASK)


def row_transform(rows):
    table = wide_table(np.arange(rows), MASK).T
    high = bfloat(table)
    return np.concatenate([high, bfloat(table - high.astype(np.float32))], 0)


TABLE_ROWS = {"grid": GRID, "base": 128, "shift": DEVICES, "phase": STEPS, "step": STEP, "transform": STEP}


def constant_table(rows):
    step = step_table().astype(np.float32)
    transform = row_transform(rows).astype(np.float32)
    parts = {
        "grid": wide_table(np.arange(GRID), GRID),
        "base": wide_table(np.arange(rows), MASK),
        "shift": wide_table(np.arange(DEVICES) * rows, MASK),
        "phase": np.pad(wide_table(np.arange(STEPS) * STEP, MASK, HALF), ((0, 0), (0, BAND))),
        "step": np.concatenate([step, step.T], 1),
        "transform": np.concatenate(np.split(transform, 4, 0), 1),
    }
    return np.concatenate([parts[name] for name in TABLE_ROWS], 0)


def table_rows(name, start=0, count=None):
    names = list(TABLE_ROWS)
    first = sum(TABLE_ROWS[before] for before in names[: names.index(name)])
    return pl.ds(pl.multiple_of(first + start, 8), TABLE_ROWS[name] if count is None else count)


def shift_group():
    return table_rows("shift", 8 * (device_place() // 8), 8)


def own_shift(shifts_ref):
    return shifts_ref[pl.ds(lax.rem(device_place(), 8), 1), :]


def coarse_map():
    cosine, sine = tables(np.arange(COARSE), COARSE)
    upper = np.concatenate([cosine.T, sine.T], 1)
    lower = np.concatenate([-sine.T, cosine.T], 1)
    return bfloat(np.concatenate([upper, lower], 0))


def interpolation():
    ratio = GRID // COARSE
    frequency = np.arange(1, COARSE // 2)
    offset = np.arange(GRID)
    profile = 1.0 + 2.0 * np.cos(2.0 * math.pi * (np.outer(offset, frequency) % GRID) / GRID).sum(1)
    profile = (profile + np.cos(math.pi * offset / ratio)) / COARSE
    return bfloat(profile[(offset[None, :] - ratio * np.arange(COARSE)[:, None]) % GRID])


def device_place():
    return lax.axis_index("rows") * KERN + lax.axis_index("kern")


def turned_table(base, shift):
    cosine = base[:, :BAND] * shift[:, :BAND] - base[:, BAND:] * shift[:, BAND:]
    sine = base[:, BAND:] * shift[:, :BAND] + base[:, :BAND] * shift[:, BAND:]
    return cosine, sine


def params(limit=VMEM_LIMIT):
    return pltpu.CompilerParams(vmem_limit_bytes=limit)


def float_dot(left, right):
    return jnp.dot(left, right, preferred_element_type=jnp.float32)


def dot_first(left, right, precision=None):
    return lax.dot_general(
        left, right, (((0,), (0,)), ((), ())), precision=precision, preferred_element_type=jnp.float32
    )


def dot_last(left, right):
    return lax.dot_general(left, right, (((1,), (1,)), ((), ())), preferred_element_type=jnp.float32)


def split(values):
    high = values.astype(jnp.bfloat16)
    return high, (values - high.astype(jnp.float32)).astype(jnp.bfloat16)


def iotas(shape):
    return lax.broadcasted_iota(jnp.int32, shape, 0), lax.broadcasted_iota(jnp.int32, shape, 1)


def conjugate_mirror():
    row, column = iotas((BAND, BAND))
    real = (row + column == HALF) & (row < HALF) & (column > 0) & (column < HALF)
    imag = (row + column == 2 * HALF + HALF) & (row >= HALF) & (column > HALF)
    return (jnp.where(real, 1.0, 0.0) - jnp.where(imag, 1.0, 0.0)).astype(jnp.bfloat16)


def store_tiles(out_ref, real, imag):
    for part, value in enumerate((real, imag)):
        for i in range(BAND // 8):
            for j in range(2):
                out_ref[4 * i + 2 * part + j] = value[8 * i : 8 * i + 8, 128 * j : 128 * j + 128].astype(
                    out_ref.dtype
                )


def load_tiles(tiles_ref, held_ref):
    for part in range(2):
        for i in range(BAND // 8):
            for j in range(2):
                held_ref[part, 8 * i : 8 * i + 8, 128 * j : 128 * j + 128] = tiles_ref[
                    4 * i + 2 * part + j
                ].astype(jnp.float32)


def spectrum_kernel(
    mask_ref, constant_ref, target_ref, out_ref, grid_out_ref,
    grid_ref, held_ref, steps_ref, phases_ref, bases_ref, shifts_ref, grid_rows_ref, targets_ref,
    stack_a, stack_b, product_a, product_b, re_ref, im_ref, flat_ref, sems,
):
    rows = mask_ref.shape[0]
    grid_rows = target_ref.shape[0]
    stacks = (stack_a, stack_b)
    products = (product_a, product_b)
    count = rows // CHUNK
    places = [pl.ds(i * CHUNK, CHUNK) for i in range(count)]
    chunks = [
        pltpu.make_async_copy(mask_ref.at[places[i]], held_ref.at[places[i]], sems.at[i]) for i in range(count)
    ]
    small = [
        pltpu.make_async_copy(source, target, sems.at[count + i])
        for i, (source, target) in enumerate(
            (
                (constant_ref.at[table_rows("step"), pl.ds(0, BAND)], steps_ref),
                (constant_ref.at[table_rows("phase"), pl.ds(0, BAND)], phases_ref),
                (constant_ref.at[table_rows("grid", lax.axis_index("rows") * grid_rows, grid_rows)], grid_rows_ref),
                (target_ref, targets_ref),
                (constant_ref.at[table_rows("transform")], bases_ref),
                (constant_ref.at[shift_group()], shifts_ref),
            )
        )
    ]
    grid_copy = pltpu.make_async_copy(grid_ref, grid_out_ref, sems.at[count + 6])
    chunks[0].start()
    small[0].start()
    small[1].start()
    chunks[1].start()
    for copy in small[2:4] + chunks[2:] + small[4:]:
        copy.start()

    def steps_of(quarter):
        return range(quarter * STEPS // QUARTERS, (quarter + 1) * STEPS // QUARTERS)

    def transmit(i, quarter):
        total = None
        for step in steps_of(quarter):
            value = jnp.tanh(held_ref[places[i], step * STEP : (step + 1) * STEP])
            stacks[i % 2][step * CHUNK : (step + 1) * CHUNK] = value.astype(jnp.bfloat16)
            both = value[:, :HALF] + value[:, HALF:]
            total = both if total is None else total + both
        flat_ref[places[i]] = total if quarter == 0 else flat_ref[places[i]] + total

    def multiply(i, quarter):
        here = slice(steps_of(quarter).start * CHUNK, steps_of(quarter).stop * CHUNK)
        products[i % 2][here] = float_dot(stacks[i % 2][here], step_value)

    def gather(i, quarter):
        totals = [None] * 4
        for step in steps_of(quarter):
            cosine = phases_ref[step : step + 1, :HALF]
            sine = phases_ref[step : step + 1, HALF:BAND]
            first = products[i % 2][step * CHUNK : (step + 1) * CHUNK, :HALF]
            second = products[i % 2][step * CHUNK : (step + 1) * CHUNK, HALF:]
            at = 2 * (step % 2)
            for part, turned in enumerate(
                (first * cosine + second * sine, second * cosine - first * sine)
            ):
                totals[at + part] = turned if totals[at + part] is None else totals[at + part] + turned
        total_re = totals[0] + totals[2]
        total_im = totals[1] + totals[3]
        re_ref[places[i]] = total_re if quarter == 0 else re_ref[places[i]] + total_re
        im_ref[places[i]] = total_im if quarter == 0 else im_ref[places[i]] + total_im

    chunks[0].wait()
    for quarter in range(QUARTERS):
        transmit(0, quarter)
    small[0].wait()
    small[1].wait()
    step_value = steps_ref[...].astype(jnp.bfloat16)
    for i in range(count):
        if i + 1 < count:
            chunks[i + 1].wait()
        for quarter in range(QUARTERS):
            multiply(i, quarter)
            if i + 1 < count:
                transmit(i + 1, quarter)
            if i > 0:
                gather(i - 1, quarter)
        if i == 1:
            for copy in small[2:4]:
                copy.wait()
            grid_ref[:grid_rows] = grid_rows_ref[...].astype(jnp.bfloat16)
            grid_ref[grid_rows:] = targets_ref[...].astype(jnp.float32).astype(jnp.bfloat16)
            grid_copy.start()
    for quarter in range(QUARTERS):
        gather(count - 1, quarter)
    for copy in small[4:]:
        copy.wait()
    _, lane = iotas((rows, HALF))
    mirror = conjugate_mirror()
    half_high, half_low = split(jnp.concatenate([re_ref[...], im_ref[...]], 1))
    other = float_dot(half_high, mirror) + float_dot(half_low, mirror)
    centre = jnp.sum(flat_ref[...], 1, keepdims=True) * (1.0 / MASK)
    other_high, other_low = split(
        jnp.concatenate([jnp.where(lane == 0, centre, other[:, :HALF]), other[:, HALF:]], 1)
    )
    high = jnp.concatenate([half_high, other_high], 1)
    low = jnp.concatenate([half_low, other_low], 1)
    transform = [bases_ref[:, at * rows : (at + 1) * rows].astype(jnp.bfloat16) for at in range(4)]
    product = float_dot(jnp.concatenate(transform, 0), high)
    rest = float_dot(jnp.concatenate(transform[:2], 0), low)
    product = product[: 2 * BAND] + (product[2 * BAND :] + rest)
    diagonal = jnp.equal(*iotas((BAND, BAND)))
    shift = own_shift(shifts_ref)
    turn_cos, turn_sin = [
        jnp.sum(jnp.where(diagonal, shift[:, part * BAND : (part + 1) * BAND], 0.0), 1, keepdims=True)
        for part in range(2)
    ]
    by_cos = product[:BAND]
    by_sin = product[BAND:]
    real = []
    imag = []
    for at in (0, 2 * HALF):
        part_re = by_cos[:, at : at + HALF] + by_sin[:, at + HALF : at + 2 * HALF]
        part_im = by_cos[:, at + HALF : at + 2 * HALF] - by_sin[:, at : at + HALF]
        real.append(turn_cos * part_re + turn_sin * part_im)
        imag.append(turn_cos * part_im - turn_sin * part_re)
    store_tiles(out_ref, jnp.concatenate(real, 1), jnp.concatenate(imag, 1))
    grid_copy.wait()


def mask_spectrum(mask_params, constants, target):
    rows = mask_params.shape[0]
    stacked = STEPS * CHUNK
    arguments = (mask_params, constants, target)
    grid_rows = target.shape[0]
    return pl.pallas_call(
        spectrum_kernel,
        in_specs=[pl.BlockSpec(memory_space=pltpu.HBM)] * len(arguments),
        out_specs=[pl.BlockSpec(memory_space=pltpu.VMEM), pl.BlockSpec(memory_space=pltpu.HBM)],
        out_shape=[
            jax.ShapeDtypeStruct((DEVICES, 8, 128), jnp.bfloat16),
            jax.ShapeDtypeStruct((2 * grid_rows, 2 * BAND), jnp.bfloat16),
        ],
        scratch_shapes=[
            pltpu.VMEM((2 * grid_rows, 2 * BAND), jnp.bfloat16),
            pltpu.VMEM((rows, MASK), jnp.float32),
            pltpu.VMEM((STEP, BAND), jnp.float32),
            pltpu.VMEM((STEPS, BAND), jnp.float32),
            pltpu.VMEM((STEP, 2 * BAND), jnp.float32),
            pltpu.VMEM((8, 2 * BAND), jnp.float32),
            pltpu.VMEM((grid_rows, 2 * BAND), jnp.float32),
            pltpu.VMEM(target.shape, jnp.int32),
            pltpu.VMEM((stacked, STEP), jnp.bfloat16),
            pltpu.VMEM((stacked, STEP), jnp.bfloat16),
            pltpu.VMEM((stacked, BAND), jnp.float32),
            pltpu.VMEM((stacked, BAND), jnp.float32),
            pltpu.VMEM((rows, HALF), jnp.float32),
            pltpu.VMEM((rows, HALF), jnp.float32),
            pltpu.VMEM((rows, HALF), jnp.float32),
            pltpu.SemaphoreType.DMA((rows // CHUNK + 7,)),
        ],
        compiler_params=params(STREAM_LIMIT),
        name="mask_spectrum",
    )(*arguments)


def field_kernel(tiles_ref, pupil_ref, grid_ref, map_ref, field_ref, power_ref, spec_ref, partial_ref):
    members = pupil_ref.shape[0]
    rows = grid_ref.shape[0] // 2
    slab = rows // KERN
    load_tiles(tiles_ref, spec_ref)
    spec_re = spec_ref[0]
    spec_im = spec_ref[1]
    table = jnp.concatenate([grid_ref[:rows, :BAND], grid_ref[:rows, BAND:]], 0)
    for member in range(members):
        for corner in range(2):
            kernel_re = pupil_ref[member, corner, 0]
            kernel_im = pupil_ref[member, corner, 1]
            amp_re = (kernel_re * spec_re - kernel_im * spec_im).astype(jnp.bfloat16)
            amp_im = (kernel_re * spec_im + kernel_im * spec_re).astype(jnp.bfloat16)
            product = float_dot(table, jnp.concatenate([amp_re, amp_im], 1))
            here = slice(corner * rows, (corner + 1) * rows)
            partial_ref[member, here, :BAND] = (product[:rows, :BAND] - product[rows:, BAND:]).astype(jnp.bfloat16)
            partial_ref[member, here, BAND:] = (product[:rows, BAND:] + product[rows:, :BAND]).astype(jnp.bfloat16)
        field_ref[member] = float_dot(partial_ref[member], map_ref[...])
    for owner in range(KERN):
        power_ref[owner, 2] = grid_ref[rows + owner * slab : rows + (owner + 1) * slab]
        for corner in range(2):
            at = corner * rows + owner * slab
            power = None
            for member in range(members):
                real = field_ref[member, at : at + slab, :COARSE]
                imag = field_ref[member, at : at + slab, COARSE:]
                term = real * real + imag * imag
                power = term if member == 0 else power + term
            power_ref[owner, corner] = power.astype(jnp.bfloat16)


def coarse_fields(tiles, pupils, grid_table, column_map):
    members = pupils.shape[0]
    rows = grid_table.shape[0] // 2
    vmem = pl.BlockSpec(memory_space=pltpu.VMEM)
    return pl.pallas_call(
        field_kernel,
        in_specs=[vmem] * 4,
        out_specs=[vmem] * 2,
        out_shape=[
            jax.ShapeDtypeStruct((members, 2 * rows, 2 * COARSE), jnp.float32),
            jax.ShapeDtypeStruct((KERN, 3, rows // KERN, COARSE), jnp.bfloat16),
        ],
        scratch_shapes=[
            pltpu.VMEM((2, BAND, BAND), jnp.float32),
            pltpu.VMEM((members, 2 * rows, 2 * BAND), jnp.bfloat16),
        ],
        compiler_params=params(),
        name="coarse_fields",
    )(tiles, pupils, grid_table, column_map)


def adjoint_kernel(parts_ref, matrix_ref, out_ref):
    rows = parts_ref.shape[2]
    width = GRID // KERN
    powers = []
    for corner in range(2):
        total = parts_ref[0, corner].astype(jnp.float32)
        for owner in range(1, KERN):
            total = total + parts_ref[owner, corner].astype(jnp.float32)
        powers.append(total.astype(jnp.bfloat16))
    power = jnp.concatenate(powers, 0)
    folded = None
    for slab in range(KERN):
        columns = slice(slab * width, (slab + 1) * width)
        fine = float_dot(power, matrix_ref[:, columns])
        wanted = parts_ref[slab, 2].astype(jnp.float32)
        corners = []
        for corner in range(2):
            dose = dose_levels[corner]
            resist = jax.nn.sigmoid(steepness * (dose * fine[corner * rows : (corner + 1) * rows] - threshold))
            corners.append(
                (2.0 * (resist - wanted) * resist * (1.0 - resist) * steepness * dose).astype(jnp.bfloat16)
            )
        term = dot_last(jnp.concatenate(corners, 0), matrix_ref[:, columns])
        folded = term if slab == 0 else folded + term
    folded = folded.reshape(2, rows, COARSE).astype(jnp.bfloat16)
    for owner in range(KERN):
        out_ref[owner] = folded


def coarse_adjoint(parts, matrix):
    rows = parts.shape[2]
    return pl.pallas_call(
        adjoint_kernel,
        in_specs=[pl.BlockSpec(memory_space=pltpu.VMEM)] * 2,
        out_specs=pl.BlockSpec(memory_space=pltpu.VMEM),
        out_shape=jax.ShapeDtypeStruct((KERN, 2, rows, COARSE), jnp.bfloat16),
        compiler_params=params(),
        name="coarse_adjoint",
    )(parts, matrix)


def gradient_kernel(field_ref, adjoint_ref, pupil_ref, grid_ref, map_ref, out_ref, weighted_ref, back_ref, acc_ref):
    members = pupil_ref.shape[0]
    slab = adjoint_ref.shape[2]
    rows = slab * KERN
    table = grid_ref[:rows].T
    for member in range(members):
        for corner in range(2):
            for owner in range(KERN):
                at = corner * rows + owner * slab
                adjoint = 2.0 * adjoint_ref[owner, corner].astype(jnp.float32)
                for half in range(2):
                    columns = slice(half * COARSE, (half + 1) * COARSE)
                    weighted_ref[member, at : at + slab, columns] = (
                        field_ref[member, at : at + slab, columns] * adjoint
                    ).astype(jnp.bfloat16)
        back_ref[member] = dot_last(weighted_ref[member], map_ref[...]).astype(jnp.bfloat16)
        for corner in range(2):
            grads = float_dot(table, back_ref[member, corner * rows : (corner + 1) * rows])
            grad_re = grads[:BAND, :BAND] + grads[BAND:, BAND:]
            grad_im = grads[:BAND, BAND:] - grads[BAND:, :BAND]
            kernel_re = pupil_ref[member, corner, 0]
            kernel_im = pupil_ref[member, corner, 1]
            term_re = kernel_re * grad_re + kernel_im * grad_im
            term_im = kernel_re * grad_im - kernel_im * grad_re
            first = member == 0 and corner == 0
            acc_ref[0] = term_re if first else acc_ref[0] + term_re
            acc_ref[1] = term_im if first else acc_ref[1] + term_im
    store_tiles(out_ref, acc_ref[0], acc_ref[1])


def spectrum_gradient(fields, adjoint, pupils, grid_table, column_map):
    members = pupils.shape[0]
    rows = grid_table.shape[0] // 2
    vmem = pl.BlockSpec(memory_space=pltpu.VMEM)
    return pl.pallas_call(
        gradient_kernel,
        in_specs=[vmem] * 5,
        out_specs=vmem,
        out_shape=jax.ShapeDtypeStruct((DEVICES, 8, 128), jnp.bfloat16),
        scratch_shapes=[
            pltpu.VMEM((members, 2 * rows, 2 * COARSE), jnp.bfloat16),
            pltpu.VMEM((members, 2 * rows, 2 * BAND), jnp.bfloat16),
            pltpu.VMEM((2, BAND, BAND), jnp.float32),
        ],
        compiler_params=params(),
        name="spectrum_gradient",
    )(fields, adjoint, pupils, grid_table, column_map)


def update_kernel(
    tiles_ref, constant_ref, mask_ref, out_ref,
    tile_ref, spec_ref, bases_ref, shifts_ref, held_ref, steps_ref, phases_ref, re_ref, im_ref, flat_ref, stack_a, stack_b, product_a, product_b, sems,
):
    rows = mask_ref.shape[0]
    stacks = (stack_a, stack_b)
    products = (product_a, product_b)
    count = rows // CHUNK
    places = [pl.ds(i * CHUNK, CHUNK) for i in range(count)]
    chunks = [
        pltpu.make_async_copy(mask_ref.at[places[i]], held_ref.at[places[i]], sems.at[i]) for i in range(count)
    ]
    results = [
        pltpu.make_async_copy(held_ref.at[places[i]], out_ref.at[places[i]], sems.at[count + i])
        for i in range(count)
    ]
    small = [
        pltpu.make_async_copy(source, target, sems.at[2 * count + i])
        for i, (source, target) in enumerate(
            (
                (constant_ref.at[table_rows("base")], bases_ref),
                (constant_ref.at[shift_group()], shifts_ref),
                (tiles_ref, tile_ref),
                (constant_ref.at[table_rows("phase"), pl.ds(0, BAND)], phases_ref),
                (constant_ref.at[table_rows("step"), pl.ds(BAND, BAND)], steps_ref),
            )
        )
    ]
    for copy in small + chunks:
        copy.start()

    small[0].wait()
    small[1].wait()
    cosine, sine = turned_table(bases_ref[...], own_shift(shifts_ref))
    small[2].wait()
    load_tiles(tile_ref, spec_ref)
    gradient = jnp.concatenate([spec_ref[0], spec_ref[1]], 1).astype(jnp.bfloat16)
    product = float_dot(jnp.concatenate(split(cosine) + split(sine), 0), gradient)
    by_cos = product[:rows] + product[rows : 2 * rows]
    by_sin = product[2 * rows : 3 * rows] + product[3 * rows :]
    col_re = by_cos[:, :BAND] - by_sin[:, BAND:]
    col_im = by_sin[:, :BAND] + by_cos[:, BAND:]
    flat_ref[...] = jnp.broadcast_to(col_re[:, HALF : HALF + 1] * (1.0 / MASK), flat_ref.shape)
    mirror = conjugate_mirror()
    high, low = split(jnp.concatenate([col_re[:, HALF:], col_im[:, HALF:]], 1))
    other = float_dot(high, mirror) + float_dot(low, mirror)
    re_ref[...] = col_re[:, :HALF] + other[:, :HALF]
    im_ref[...] = col_im[:, :HALF] + other[:, HALF:]

    def steps_of(quarter):
        return range(quarter * STEPS // QUARTERS, (quarter + 1) * STEPS // QUARTERS)

    def turn(i, quarter):
        col_re = re_ref[places[i]]
        col_im = im_ref[places[i]]
        for step in steps_of(quarter):
            cosine = phases_ref[step : step + 1, :HALF]
            sine = phases_ref[step : step + 1, HALF:BAND]
            here = slice(step * CHUNK, (step + 1) * CHUNK)
            stacks[i % 2][here, :HALF] = (col_re * cosine - col_im * sine).astype(jnp.bfloat16)
            stacks[i % 2][here, HALF:] = (col_re * sine + col_im * cosine).astype(jnp.bfloat16)

    def multiply(i, quarter):
        here = slice(steps_of(quarter).start * CHUNK, steps_of(quarter).stop * CHUNK)
        products[i % 2][here] = float_dot(stacks[i % 2][here], step_value)

    def finish(i, quarter):
        centre = flat_ref[places[i]]
        for step in steps_of(quarter):
            here = slice(step * STEP, (step + 1) * STEP)
            mask = held_ref[places[i], here]
            transmit = jnp.tanh(mask)
            pixel_grad = products[i % 2][step * CHUNK : (step + 1) * CHUNK] + centre
            held_ref[places[i], here] = mask - step_size * pixel_grad * (1.0 - transmit * transmit)

    small[3].wait()
    for quarter in range(QUARTERS):
        turn(0, quarter)
    small[4].wait()
    step_value = steps_ref[...].astype(jnp.bfloat16)
    for i in range(count + 1):
        if i > 0:
            chunks[i - 1].wait()
        for quarter in range(QUARTERS):
            if i < count:
                multiply(i, quarter)
            if i + 1 < count:
                turn(i + 1, quarter)
            if i > 0:
                finish(i - 1, quarter)
        if i > 0:
            results[i - 1].start()
    for copy in results:
        copy.wait()


def mask_update(tiles, constants, mask_params):
    rows = mask_params.shape[0]
    stacked = STEPS * CHUNK
    hbm = pl.BlockSpec(memory_space=pltpu.HBM)
    return pl.pallas_call(
        update_kernel,
        in_specs=[hbm] * 3,
        out_specs=hbm,
        out_shape=jax.ShapeDtypeStruct((rows, MASK), jnp.float32),
        scratch_shapes=[
            pltpu.VMEM(tiles.shape, jnp.bfloat16),
            pltpu.VMEM((2, BAND, BAND), jnp.float32),
            pltpu.VMEM((rows, 2 * BAND), jnp.float32),
            pltpu.VMEM((8, 2 * BAND), jnp.float32),
            pltpu.VMEM((rows, MASK), jnp.float32),
            pltpu.VMEM((STEP, BAND), jnp.float32),
            pltpu.VMEM((STEPS, BAND), jnp.float32),
            pltpu.VMEM((rows, HALF), jnp.float32),
            pltpu.VMEM((rows, HALF), jnp.float32),
            pltpu.VMEM((rows, STEP), jnp.float32),
            pltpu.VMEM((stacked, BAND), jnp.bfloat16),
            pltpu.VMEM((stacked, BAND), jnp.bfloat16),
            pltpu.VMEM((stacked, STEP), jnp.float32),
            pltpu.VMEM((stacked, STEP), jnp.float32),
            pltpu.SemaphoreType.DMA((2 * (rows // CHUNK) + 5,)),
        ],
        compiler_params=params(STREAM_LIMIT),
        name="mask_update",
    )(tiles, constants, mask_params)


def exchange(values, axes):
    return lax.all_to_all(values, axes, 0, 0, tiled=True)


def summed(parts, copies):
    total = jnp.sum(parts.astype(jnp.float32), 0).astype(parts.dtype)
    return jnp.broadcast_to(total[None], (copies,) + total.shape)


def total_kernel(parts_ref, out_ref):
    total = jnp.sum(parts_ref[...].astype(jnp.float32), 0).astype(out_ref.dtype)
    for owner in range(DEVICES):
        out_ref[owner] = total


def total_tiles(parts):
    vmem = pl.BlockSpec(memory_space=pltpu.VMEM)
    return pl.pallas_call(
        total_kernel,
        in_specs=[vmem],
        out_specs=vmem,
        out_shape=jax.ShapeDtypeStruct(parts.shape, parts.dtype),
        compiler_params=params(),
        cost_estimate=pl.CostEstimate(flops=10**10, bytes_accessed=2 * parts.size, transcendentals=0),
        name="total_tiles",
    )(parts)


def local(mask_params, pupil_kernels, target_pattern):
    rows = mask_params.shape[0]
    constants = jnp.asarray(constant_table(rows))
    column_map = jnp.asarray(coarse_map())

    everyone = ("kern", "rows")
    tiles, grid_table = mask_spectrum(mask_params, constants, target_pattern)
    spectrum = exchange(total_tiles(exchange(tiles, everyone)), everyone)
    fields, powers = coarse_fields(spectrum, pupil_kernels, grid_table, column_map)
    adjoint = coarse_adjoint(exchange(powers, "kern"), jnp.asarray(interpolation()))
    gradient = spectrum_gradient(fields, exchange(adjoint, "kern"), pupil_kernels, grid_table, column_map)
    gradient = exchange(summed(exchange(gradient, everyone), DEVICES), everyone)
    return mask_update(gradient, constants, mask_params)


def solution(mesh):
    placed = (P(("rows", "kern"), None), P("kern", None, None, None, None), P("rows", "kern"))
    return jax.shard_map(
        local, mesh=mesh, in_specs=placed, out_specs=P(("rows", "kern"), None), check_vma=False
    )
```

```python
import math

import jax
import jax.numpy as jnp
import numpy as np
from jax import lax
from jax.experimental import pallas as pl
from jax.experimental.pallas import tpu as pltpu
from jax.sharding import PartitionSpec as P

MASK = 16384
GRID = 4096
BAND = 256
HALF = BAND // 2
COARSE = 512
STEP = 256
STEPS = MASK // STEP
ROWS = 16
KERN = 8
DEVICES = ROWS * KERN
CHUNK = 16
QUARTERS = 4
QUARTER = MASK // QUARTERS

steepness = 4.0
threshold = 0.75
step_size = 1.0
dose_levels = (1.0, 1.15)

VMEM_LIMIT = 24 * 1024 * 1024
STREAM_LIMIT = 53 * 1024 * 1024


def tables(positions, period, count=BAND):
    frequency = np.arange(count) - BAND // 2
    angles = (np.outer(positions, frequency) % period) * (2.0 * math.pi / period)
    return np.cos(angles), np.sin(angles)


def bfloat(values):
    return np.asarray(values, np.float32).astype(jnp.bfloat16)


def wide_table(positions, period, count=BAND):
    return np.concatenate(tables(positions, period, count), 1).astype(np.float32)


def step_table():
    cosine, sine = tables(np.arange(STEP), MASK, HALF)
    return bfloat(np.concatenate([cosine, -sine], 1) / MASK)


def row_transform(rows):
    table = wide_table(np.arange(rows), MASK).T
    high = bfloat(table)
    return np.concatenate([high, bfloat(table - high.astype(np.float32))], 0)


TABLE_ROWS = {"grid": GRID, "base": 128, "shift": DEVICES, "phase": STEPS, "step": STEP, "transform": STEP}


def constant_table(rows):
    step = step_table().astype(np.float32)
    transform = row_transform(rows).astype(np.float32)
    parts = {
        "grid": wide_table(np.arange(GRID), GRID),
        "base": wide_table(np.arange(rows), MASK),
        "shift": wide_table(np.arange(DEVICES) * rows, MASK),
        "phase": np.pad(wide_table(np.arange(STEPS) * STEP, MASK, HALF), ((0, 0), (0, BAND))),
        "step": np.concatenate([step, step.T], 1),
        "transform": np.concatenate(np.split(transform, 4, 0), 1),
    }
    return np.concatenate([parts[name] for name in TABLE_ROWS], 0)


def table_rows(name, start=0, count=None):
    names = list(TABLE_ROWS)
    first = sum(TABLE_ROWS[before] for before in names[: names.index(name)])
    return pl.ds(pl.multiple_of(first + start, 8), TABLE_ROWS[name] if count is None else count)


def shift_group():
    return table_rows("shift", 8 * (device_place() // 8), 8)


def own_shift(shifts_ref):
    return shifts_ref[pl.ds(lax.rem(device_place(), 8), 1), :]


def coarse_map():
    cosine, sine = tables(np.arange(COARSE), COARSE)
    upper = np.concatenate([cosine.T, sine.T], 1)
    lower = np.concatenate([-sine.T, cosine.T], 1)
    return bfloat(np.concatenate([upper, lower], 0))


def interpolation():
    ratio = GRID // COARSE
    frequency = np.arange(1, COARSE // 2)
    offset = np.arange(GRID)
    profile = 1.0 + 2.0 * np.cos(2.0 * math.pi * (np.outer(offset, frequency) % GRID) / GRID).sum(1)
    profile = (profile + np.cos(math.pi * offset / ratio)) / COARSE
    return bfloat(profile[(offset[None, :] - ratio * np.arange(COARSE)[:, None]) % GRID])


def device_place():
    return lax.axis_index("rows") * KERN + lax.axis_index("kern")


def turned_table(base, shift):
    cosine = base[:, :BAND] * shift[:, :BAND] - base[:, BAND:] * shift[:, BAND:]
    sine = base[:, BAND:] * shift[:, :BAND] + base[:, :BAND] * shift[:, BAND:]
    return cosine, sine


def params(limit=VMEM_LIMIT):
    return pltpu.CompilerParams(vmem_limit_bytes=limit)


def float_dot(left, right):
    return jnp.dot(left, right, preferred_element_type=jnp.float32)


def dot_first(left, right, precision=None):
    return lax.dot_general(
        left, right, (((0,), (0,)), ((), ())), precision=precision, preferred_element_type=jnp.float32
    )


def dot_last(left, right):
    return lax.dot_general(left, right, (((1,), (1,)), ((), ())), preferred_element_type=jnp.float32)


def split(values):
    high = values.astype(jnp.bfloat16)
    return high, (values - high.astype(jnp.float32)).astype(jnp.bfloat16)


def iotas(shape):
    return lax.broadcasted_iota(jnp.int32, shape, 0), lax.broadcasted_iota(jnp.int32, shape, 1)


def conjugate_mirror():
    row, column = iotas((BAND, BAND))
    real = (row + column == HALF) & (row < HALF) & (column > 0) & (column < HALF)
    imag = (row + column == 2 * HALF + HALF) & (row >= HALF) & (column > HALF)
    return (jnp.where(real, 1.0, 0.0) - jnp.where(imag, 1.0, 0.0)).astype(jnp.bfloat16)


def store_tiles(out_ref, real, imag):
    for part, value in enumerate((real, imag)):
        for i in range(BAND // 8):
            for j in range(2):
                out_ref[4 * i + 2 * part + j] = value[8 * i : 8 * i + 8, 128 * j : 128 * j + 128].astype(
                    out_ref.dtype
                )


def load_tiles(tiles_ref, held_ref):
    for part in range(2):
        for i in range(BAND // 8):
            for j in range(2):
                held_ref[part, 8 * i : 8 * i + 8, 128 * j : 128 * j + 128] = tiles_ref[
                    4 * i + 2 * part + j
                ].astype(jnp.float32)


def spectrum_kernel(
    mask_ref, constant_ref, target_ref, out_ref, grid_out_ref,
    grid_ref, held_ref, steps_ref, phases_ref, bases_ref, shifts_ref, grid_rows_ref, targets_ref,
    stack_a, stack_b, product_a, product_b, re_ref, im_ref, flat_ref, sems,
):
    rows = mask_ref.shape[0]
    grid_rows = target_ref.shape[0]
    stacks = (stack_a, stack_b)
    products = (product_a, product_b)
    count = rows // CHUNK
    places = [pl.ds(i * CHUNK, CHUNK) for i in range(count)]
    chunks = [None] + [
        pltpu.make_async_copy(mask_ref.at[places[i]], held_ref.at[places[i]], sems.at[i]) for i in range(1, count)
    ]
    columns = [pl.ds(quarter * QUARTER, QUARTER) for quarter in range(QUARTERS)]
    heads = [
        pltpu.make_async_copy(
            mask_ref.at[places[0], columns[quarter]],
            held_ref.at[places[0], columns[quarter]],
            sems.at[count + 7 + quarter],
        )
        for quarter in range(QUARTERS)
    ]
    small = [
        pltpu.make_async_copy(source, target, sems.at[count + i])
        for i, (source, target) in enumerate(
            (
                (constant_ref.at[table_rows("step"), pl.ds(0, BAND)], steps_ref),
                (constant_ref.at[table_rows("phase"), pl.ds(0, BAND)], phases_ref),
                (constant_ref.at[table_rows("grid", lax.axis_index("rows") * grid_rows, grid_rows)], grid_rows_ref),
                (target_ref, targets_ref),
                (constant_ref.at[table_rows("transform")], bases_ref),
                (constant_ref.at[shift_group()], shifts_ref),
            )
        )
    ]
    grid_copy = pltpu.make_async_copy(grid_ref, grid_out_ref, sems.at[count + 6])
    for copy in heads:
        copy.start()
    small[0].start()
    small[1].start()
    chunks[1].start()
    for copy in small[2:4] + chunks[2:] + small[4:]:
        copy.start()

    def steps_of(quarter):
        return range(quarter * STEPS // QUARTERS, (quarter + 1) * STEPS // QUARTERS)

    def transmit(i, quarter):
        total = None
        for step in steps_of(quarter):
            value = jnp.tanh(held_ref[places[i], step * STEP : (step + 1) * STEP])
            stacks[i % 2][step * CHUNK : (step + 1) * CHUNK] = value.astype(jnp.bfloat16)
            both = value[:, :HALF] + value[:, HALF:]
            total = both if total is None else total + both
        flat_ref[places[i]] = total if quarter == 0 else flat_ref[places[i]] + total

    def multiply(i, quarter):
        here = slice(steps_of(quarter).start * CHUNK, steps_of(quarter).stop * CHUNK)
        products[i % 2][here] = float_dot(stacks[i % 2][here], step_value)

    def gather(i, quarter):
        totals = [None] * 4
        for step in steps_of(quarter):
            cosine = phases_ref[step : step + 1, :HALF]
            sine = phases_ref[step : step + 1, HALF:BAND]
            first = products[i % 2][step * CHUNK : (step + 1) * CHUNK, :HALF]
            second = products[i % 2][step * CHUNK : (step + 1) * CHUNK, HALF:]
            at = 2 * (step % 2)
            for part, turned in enumerate(
                (first * cosine + second * sine, second * cosine - first * sine)
            ):
                totals[at + part] = turned if totals[at + part] is None else totals[at + part] + turned
        total_re = totals[0] + totals[2]
        total_im = totals[1] + totals[3]
        re_ref[places[i]] = total_re if quarter == 0 else re_ref[places[i]] + total_re
        im_ref[places[i]] = total_im if quarter == 0 else im_ref[places[i]] + total_im

    for quarter in range(QUARTERS):
        heads[quarter].wait()
        transmit(0, quarter)
    small[0].wait()
    small[1].wait()
    step_value = steps_ref[...].astype(jnp.bfloat16)
    for i in range(count):
        if i + 1 < count:
            chunks[i + 1].wait()
        for quarter in range(QUARTERS):
            multiply(i, quarter)
            if i + 1 < count:
                transmit(i + 1, quarter)
            if i > 0:
                gather(i - 1, quarter)
        if i == 1:
            for copy in small[2:4]:
                copy.wait()
            grid_ref[:grid_rows] = grid_rows_ref[...].astype(jnp.bfloat16)
            grid_ref[grid_rows:] = targets_ref[...].astype(jnp.float32).astype(jnp.bfloat16)
            grid_copy.start()
    for quarter in range(QUARTERS):
        gather(count - 1, quarter)
    for copy in small[4:]:
        copy.wait()
    _, lane = iotas((rows, HALF))
    mirror = conjugate_mirror()
    half_high, half_low = split(jnp.concatenate([re_ref[...], im_ref[...]], 1))
    other = float_dot(half_high, mirror) + float_dot(half_low, mirror)
    centre = jnp.sum(flat_ref[...], 1, keepdims=True) * (1.0 / MASK)
    other_high, other_low = split(
        jnp.concatenate([jnp.where(lane == 0, centre, other[:, :HALF]), other[:, HALF:]], 1)
    )
    high = jnp.concatenate([half_high, other_high], 1)
    low = jnp.concatenate([half_low, other_low], 1)
    transform = [bases_ref[:, at * rows : (at + 1) * rows].astype(jnp.bfloat16) for at in range(4)]
    product = float_dot(jnp.concatenate(transform, 0), high)
    rest = float_dot(jnp.concatenate(transform[:2], 0), low)
    product = product[: 2 * BAND] + (product[2 * BAND :] + rest)
    diagonal = jnp.equal(*iotas((BAND, BAND)))
    shift = own_shift(shifts_ref)
    turn_cos, turn_sin = [
        jnp.sum(jnp.where(diagonal, shift[:, part * BAND : (part + 1) * BAND], 0.0), 1, keepdims=True)
        for part in range(2)
    ]
    by_cos = product[:BAND]
    by_sin = product[BAND:]
    real = []
    imag = []
    for at in (0, 2 * HALF):
        part_re = by_cos[:, at : at + HALF] + by_sin[:, at + HALF : at + 2 * HALF]
        part_im = by_cos[:, at + HALF : at + 2 * HALF] - by_sin[:, at : at + HALF]
        real.append(turn_cos * part_re + turn_sin * part_im)
        imag.append(turn_cos * part_im - turn_sin * part_re)
    store_tiles(out_ref, jnp.concatenate(real, 1), jnp.concatenate(imag, 1))
    grid_copy.wait()


def mask_spectrum(mask_params, constants, target):
    rows = mask_params.shape[0]
    stacked = STEPS * CHUNK
    arguments = (mask_params, constants, target)
    grid_rows = target.shape[0]
    return pl.pallas_call(
        spectrum_kernel,
        in_specs=[pl.BlockSpec(memory_space=pltpu.HBM)] * len(arguments),
        out_specs=[pl.BlockSpec(memory_space=pltpu.VMEM), pl.BlockSpec(memory_space=pltpu.HBM)],
        out_shape=[
            jax.ShapeDtypeStruct((DEVICES, 8, 128), jnp.bfloat16),
            jax.ShapeDtypeStruct((2 * grid_rows, 2 * BAND), jnp.bfloat16),
        ],
        scratch_shapes=[
            pltpu.VMEM((2 * grid_rows, 2 * BAND), jnp.bfloat16),
            pltpu.VMEM((rows, MASK), jnp.float32),
            pltpu.VMEM((STEP, BAND), jnp.float32),
            pltpu.VMEM((STEPS, BAND), jnp.float32),
            pltpu.VMEM((STEP, 2 * BAND), jnp.float32),
            pltpu.VMEM((8, 2 * BAND), jnp.float32),
            pltpu.VMEM((grid_rows, 2 * BAND), jnp.float32),
            pltpu.VMEM(target.shape, jnp.int32),
            pltpu.VMEM((stacked, STEP), jnp.bfloat16),
            pltpu.VMEM((stacked, STEP), jnp.bfloat16),
            pltpu.VMEM((stacked, BAND), jnp.float32),
            pltpu.VMEM((stacked, BAND), jnp.float32),
            pltpu.VMEM((rows, HALF), jnp.float32),
            pltpu.VMEM((rows, HALF), jnp.float32),
            pltpu.VMEM((rows, HALF), jnp.float32),
            pltpu.SemaphoreType.DMA((rows // CHUNK + 7 + QUARTERS,)),
        ],
        compiler_params=params(STREAM_LIMIT),
        name="mask_spectrum",
    )(*arguments)


def field_kernel(tiles_ref, pupil_ref, grid_ref, map_ref, field_ref, power_ref, spec_ref, partial_ref):
    members = pupil_ref.shape[0]
    rows = grid_ref.shape[0] // 2
    slab = rows // KERN
    load_tiles(tiles_ref, spec_ref)
    spec_re = spec_ref[0]
    spec_im = spec_ref[1]
    for member in range(members):
        for corner in range(2):
            kernel_re = pupil_ref[member, corner, 0]
            kernel_im = pupil_ref[member, corner, 1]
            amp_re = (kernel_re * spec_re - kernel_im * spec_im).astype(jnp.bfloat16)
            amp_im = (kernel_re * spec_im + kernel_im * spec_re).astype(jnp.bfloat16)
            block = jnp.concatenate(
                [jnp.concatenate([amp_re, amp_im], 1), jnp.concatenate([-amp_im, amp_re], 1)], 0
            )
            partial_ref[member, corner * rows : (corner + 1) * rows] = float_dot(grid_ref[:rows], block).astype(
                jnp.bfloat16
            )
        field_ref[member] = float_dot(partial_ref[member], map_ref[...])
    for owner in range(KERN):
        power_ref[owner, 2] = grid_ref[rows + owner * slab : rows + (owner + 1) * slab]
        for corner in range(2):
            at = corner * rows + owner * slab
            power = None
            for member in range(members):
                real = field_ref[member, at : at + slab, :COARSE]
                imag = field_ref[member, at : at + slab, COARSE:]
                term = real * real + imag * imag
                power = term if member == 0 else power + term
            power_ref[owner, corner] = power.astype(jnp.bfloat16)


def coarse_fields(tiles, pupils, grid_table, column_map):
    members = pupils.shape[0]
    rows = grid_table.shape[0] // 2
    vmem = pl.BlockSpec(memory_space=pltpu.VMEM)
    return pl.pallas_call(
        field_kernel,
        in_specs=[vmem] * 4,
        out_specs=[vmem] * 2,
        out_shape=[
            jax.ShapeDtypeStruct((members, 2 * rows, 2 * COARSE), jnp.float32),
            jax.ShapeDtypeStruct((KERN, 3, rows // KERN, COARSE), jnp.bfloat16),
        ],
        scratch_shapes=[
            pltpu.VMEM((2, BAND, BAND), jnp.float32),
            pltpu.VMEM((members, 2 * rows, 2 * BAND), jnp.bfloat16),
        ],
        compiler_params=params(),
        name="coarse_fields",
    )(tiles, pupils, grid_table, column_map)


def adjoint_kernel(parts_ref, matrix_ref, out_ref):
    rows = parts_ref.shape[2]
    width = GRID // KERN
    powers = []
    for corner in range(2):
        total = parts_ref[0, corner].astype(jnp.float32)
        for owner in range(1, KERN):
            total = total + parts_ref[owner, corner].astype(jnp.float32)
        powers.append(total.astype(jnp.bfloat16))
    power = jnp.concatenate(powers, 0)
    folded = None
    for slab in range(KERN):
        columns = slice(slab * width, (slab + 1) * width)
        fine = float_dot(power, matrix_ref[:, columns])
        wanted = parts_ref[slab, 2].astype(jnp.float32)
        corners = []
        for corner in range(2):
            dose = dose_levels[corner]
            resist = jax.nn.sigmoid(steepness * (dose * fine[corner * rows : (corner + 1) * rows] - threshold))
            corners.append(
                (2.0 * (resist - wanted) * resist * (1.0 - resist) * steepness * dose).astype(jnp.bfloat16)
            )
        term = dot_last(jnp.concatenate(corners, 0), matrix_ref[:, columns])
        folded = term if slab == 0 else folded + term
    folded = folded.reshape(2, rows, COARSE).astype(jnp.bfloat16)
    for owner in range(KERN):
        out_ref[owner] = folded


def coarse_adjoint(parts, matrix):
    rows = parts.shape[2]
    return pl.pallas_call(
        adjoint_kernel,
        in_specs=[pl.BlockSpec(memory_space=pltpu.VMEM)] * 2,
        out_specs=pl.BlockSpec(memory_space=pltpu.VMEM),
        out_shape=jax.ShapeDtypeStruct((KERN, 2, rows, COARSE), jnp.bfloat16),
        compiler_params=params(),
        name="coarse_adjoint",
    )(parts, matrix)


def gradient_kernel(field_ref, adjoint_ref, pupil_ref, grid_ref, map_ref, out_ref, weighted_ref, back_ref, acc_ref):
    members = pupil_ref.shape[0]
    slab = adjoint_ref.shape[2]
    rows = slab * KERN
    table = grid_ref[:rows].T
    for member in range(members):
        for corner in range(2):
            for owner in range(KERN):
                at = corner * rows + owner * slab
                adjoint = 2.0 * adjoint_ref[owner, corner].astype(jnp.float32)
                for half in range(2):
                    columns = slice(half * COARSE, (half + 1) * COARSE)
                    weighted_ref[member, at : at + slab, columns] = (
                        field_ref[member, at : at + slab, columns] * adjoint
                    ).astype(jnp.bfloat16)
        back_ref[member] = dot_last(weighted_ref[member], map_ref[...]).astype(jnp.bfloat16)
        for corner in range(2):
            grads = float_dot(table, back_ref[member, corner * rows : (corner + 1) * rows])
            grad_re = grads[:BAND, :BAND] + grads[BAND:, BAND:]
            grad_im = grads[:BAND, BAND:] - grads[BAND:, :BAND]
            kernel_re = pupil_ref[member, corner, 0]
            kernel_im = pupil_ref[member, corner, 1]
            term_re = kernel_re * grad_re + kernel_im * grad_im
            term_im = kernel_re * grad_im - kernel_im * grad_re
            first = member == 0 and corner == 0
            acc_ref[0] = term_re if first else acc_ref[0] + term_re
            acc_ref[1] = term_im if first else acc_ref[1] + term_im
    store_tiles(out_ref, acc_ref[0], acc_ref[1])


def spectrum_gradient(fields, adjoint, pupils, grid_table, column_map):
    members = pupils.shape[0]
    rows = grid_table.shape[0] // 2
    vmem = pl.BlockSpec(memory_space=pltpu.VMEM)
    return pl.pallas_call(
        gradient_kernel,
        in_specs=[vmem] * 5,
        out_specs=vmem,
        out_shape=jax.ShapeDtypeStruct((DEVICES, 8, 128), jnp.bfloat16),
        scratch_shapes=[
            pltpu.VMEM((members, 2 * rows, 2 * COARSE), jnp.bfloat16),
            pltpu.VMEM((members, 2 * rows, 2 * BAND), jnp.bfloat16),
            pltpu.VMEM((2, BAND, BAND), jnp.float32),
        ],
        compiler_params=params(),
        name="spectrum_gradient",
    )(fields, adjoint, pupils, grid_table, column_map)


def update_kernel(
    tiles_ref, constant_ref, mask_ref, out_ref,
    tile_ref, spec_ref, bases_ref, shifts_ref, held_ref, steps_ref, phases_ref, re_ref, im_ref, flat_ref, stack_a, stack_b, product_a, product_b, sems,
):
    rows = mask_ref.shape[0]
    stacks = (stack_a, stack_b)
    products = (product_a, product_b)
    count = rows // CHUNK
    places = [pl.ds(i * CHUNK, CHUNK) for i in range(count)]
    chunks = [
        pltpu.make_async_copy(mask_ref.at[places[i]], held_ref.at[places[i]], sems.at[i]) for i in range(count)
    ]
    columns = [pl.ds(quarter * QUARTER, QUARTER) for quarter in range(QUARTERS)]
    results = [
        pltpu.make_async_copy(
            held_ref.at[places[i], columns[quarter]],
            out_ref.at[places[i], columns[quarter]],
            sems.at[count + 5 + QUARTERS * i + quarter],
        )
        for i in range(count)
        for quarter in range(QUARTERS)
    ]
    small = [
        pltpu.make_async_copy(source, target, sems.at[count + i])
        for i, (source, target) in enumerate(
            (
                (constant_ref.at[table_rows("base")], bases_ref),
                (constant_ref.at[shift_group()], shifts_ref),
                (tiles_ref, tile_ref),
                (constant_ref.at[table_rows("phase"), pl.ds(0, BAND)], phases_ref),
                (constant_ref.at[table_rows("step"), pl.ds(BAND, BAND)], steps_ref),
            )
        )
    ]
    for copy in small + chunks:
        copy.start()

    small[0].wait()
    small[1].wait()
    cosine, sine = turned_table(bases_ref[...], own_shift(shifts_ref))
    small[2].wait()
    load_tiles(tile_ref, spec_ref)
    gradient = jnp.concatenate([spec_ref[0], spec_ref[1]], 1).astype(jnp.bfloat16)
    product = float_dot(jnp.concatenate(split(cosine) + split(sine), 0), gradient)
    by_cos = product[:rows] + product[rows : 2 * rows]
    by_sin = product[2 * rows : 3 * rows] + product[3 * rows :]
    col_re = by_cos[:, :BAND] - by_sin[:, BAND:]
    col_im = by_sin[:, :BAND] + by_cos[:, BAND:]
    flat_ref[...] = jnp.broadcast_to(col_re[:, HALF : HALF + 1] * (1.0 / MASK), flat_ref.shape)
    mirror = conjugate_mirror()
    high, low = split(jnp.concatenate([col_re[:, HALF:], col_im[:, HALF:]], 1))
    other = float_dot(high, mirror) + float_dot(low, mirror)
    re_ref[...] = col_re[:, :HALF] + other[:, :HALF]
    im_ref[...] = col_im[:, :HALF] + other[:, HALF:]

    def steps_of(quarter):
        return range(quarter * STEPS // QUARTERS, (quarter + 1) * STEPS // QUARTERS)

    def turn(i, quarter):
        col_re = re_ref[places[i]]
        col_im = im_ref[places[i]]
        for step in steps_of(quarter):
            cosine = phases_ref[step : step + 1, :HALF]
            sine = phases_ref[step : step + 1, HALF:BAND]
            here = slice(step * CHUNK, (step + 1) * CHUNK)
            stacks[i % 2][here, :HALF] = (col_re * cosine - col_im * sine).astype(jnp.bfloat16)
            stacks[i % 2][here, HALF:] = (col_re * sine + col_im * cosine).astype(jnp.bfloat16)

    def multiply(i, quarter):
        here = slice(steps_of(quarter).start * CHUNK, steps_of(quarter).stop * CHUNK)
        products[i % 2][here] = float_dot(stacks[i % 2][here], step_value)

    def finish(i, quarter):
        centre = flat_ref[places[i]]
        for step in steps_of(quarter):
            here = slice(step * STEP, (step + 1) * STEP)
            mask = held_ref[places[i], here]
            transmit = jnp.tanh(mask)
            pixel_grad = products[i % 2][step * CHUNK : (step + 1) * CHUNK] + centre
            held_ref[places[i], here] = mask - step_size * pixel_grad * (1.0 - transmit * transmit)

    small[3].wait()
    for quarter in range(QUARTERS):
        turn(0, quarter)
    small[4].wait()
    step_value = steps_ref[...].astype(jnp.bfloat16)
    for i in range(count + 1):
        if i > 0:
            chunks[i - 1].wait()
        for quarter in range(QUARTERS):
            if i < count:
                multiply(i, quarter)
            if i + 1 < count:
                turn(i + 1, quarter)
            if i > 0:
                finish(i - 1, quarter)
                results[QUARTERS * (i - 1) + quarter].start()
    for copy in results:
        copy.wait()


def mask_update(tiles, constants, mask_params):
    rows = mask_params.shape[0]
    stacked = STEPS * CHUNK
    hbm = pl.BlockSpec(memory_space=pltpu.HBM)
    return pl.pallas_call(
        update_kernel,
        in_specs=[hbm] * 3,
        out_specs=hbm,
        out_shape=jax.ShapeDtypeStruct((rows, MASK), jnp.float32),
        scratch_shapes=[
            pltpu.VMEM(tiles.shape, jnp.bfloat16),
            pltpu.VMEM((2, BAND, BAND), jnp.float32),
            pltpu.VMEM((rows, 2 * BAND), jnp.float32),
            pltpu.VMEM((8, 2 * BAND), jnp.float32),
            pltpu.VMEM((rows, MASK), jnp.float32),
            pltpu.VMEM((STEP, BAND), jnp.float32),
            pltpu.VMEM((STEPS, BAND), jnp.float32),
            pltpu.VMEM((rows, HALF), jnp.float32),
            pltpu.VMEM((rows, HALF), jnp.float32),
            pltpu.VMEM((rows, STEP), jnp.float32),
            pltpu.VMEM((stacked, BAND), jnp.bfloat16),
            pltpu.VMEM((stacked, BAND), jnp.bfloat16),
            pltpu.VMEM((stacked, STEP), jnp.float32),
            pltpu.VMEM((stacked, STEP), jnp.float32),
            pltpu.SemaphoreType.DMA(((QUARTERS + 1) * (rows // CHUNK) + 5,)),
        ],
        compiler_params=params(STREAM_LIMIT),
        name="mask_update",
    )(tiles, constants, mask_params)


def exchange(values, axes):
    return lax.all_to_all(values, axes, 0, 0, tiled=True)


def summed(parts, copies):
    total = jnp.sum(parts.astype(jnp.float32), 0).astype(parts.dtype)
    return jnp.broadcast_to(total[None], (copies,) + total.shape)


def total_kernel(parts_ref, out_ref):
    total = jnp.sum(parts_ref[...].astype(jnp.float32), 0).astype(out_ref.dtype)
    for owner in range(DEVICES):
        out_ref[owner] = total


def total_tiles(parts):
    vmem = pl.BlockSpec(memory_space=pltpu.VMEM)
    return pl.pallas_call(
        total_kernel,
        in_specs=[vmem],
        out_specs=vmem,
        out_shape=jax.ShapeDtypeStruct(parts.shape, parts.dtype),
        compiler_params=params(),
        cost_estimate=pl.CostEstimate(flops=10**10, bytes_accessed=2 * parts.size, transcendentals=0),
        name="total_tiles",
    )(parts)


def local(mask_params, pupil_kernels, target_pattern):
    rows = mask_params.shape[0]
    constants = jnp.asarray(constant_table(rows))
    column_map = jnp.asarray(coarse_map())

    everyone = ("kern", "rows")
    tiles, grid_table = mask_spectrum(mask_params, constants, target_pattern)
    spectrum = exchange(total_tiles(exchange(tiles, everyone)), everyone)
    fields, powers = coarse_fields(spectrum, pupil_kernels, grid_table, column_map)
    adjoint = coarse_adjoint(exchange(powers, "kern"), jnp.asarray(interpolation()))
    gradient = spectrum_gradient(fields, exchange(adjoint, "kern"), pupil_kernels, grid_table, column_map)
    gradient = exchange(summed(exchange(gradient, everyone), DEVICES), everyone)
    return mask_update(gradient, constants, mask_params)


def solution(mesh):
    placed = (P(("rows", "kern"), None), P("kern", None, None, None, None), P("rows", "kern"))
    return jax.shard_map(
        local, mesh=mesh, in_specs=placed, out_specs=P(("rows", "kern"), None), check_vma=False
    )
```

```python
import math

import jax
import jax.numpy as jnp
import numpy as np
from jax import lax
from jax.experimental import pallas as pl
from jax.experimental.pallas import tpu as pltpu
from jax.sharding import PartitionSpec as P

MASK = 16384
GRID = 4096
BAND = 256
HALF = BAND // 2
COARSE = 512
STEP = 256
STEPS = MASK // STEP
ROWS = 16
KERN = 8
DEVICES = ROWS * KERN
CHUNK = 16
QUARTERS = 4
QUARTER = MASK // QUARTERS

steepness = 4.0
threshold = 0.75
step_size = 1.0
dose_levels = (1.0, 1.15)

VMEM_LIMIT = 24 * 1024 * 1024
STREAM_LIMIT = 53 * 1024 * 1024


def tables(positions, period, count=BAND):
    frequency = np.arange(count) - BAND // 2
    angles = (np.outer(positions, frequency) % period) * (2.0 * math.pi / period)
    return np.cos(angles), np.sin(angles)


def bfloat(values):
    return np.asarray(values, np.float32).astype(jnp.bfloat16)


def wide_table(positions, period, count=BAND):
    return np.concatenate(tables(positions, period, count), 1).astype(np.float32)


def step_table():
    cosine, sine = tables(np.arange(STEP), MASK, HALF)
    return bfloat(np.concatenate([cosine, -sine], 1) / MASK)


def row_transform(rows):
    table = wide_table(np.arange(rows), MASK).T
    high = bfloat(table)
    return np.concatenate([high, bfloat(table - high.astype(np.float32))], 0)


TABLE_ROWS = {"grid": GRID, "base": 128, "shift": DEVICES, "phase": STEPS, "step": STEP, "transform": STEP}


def constant_table(rows):
    step = step_table().astype(np.float32)
    transform = row_transform(rows).astype(np.float32)
    parts = {
        "grid": wide_table(np.arange(GRID), GRID),
        "base": wide_table(np.arange(rows), MASK),
        "shift": wide_table(np.arange(DEVICES) * rows, MASK),
        "phase": np.pad(wide_table(np.arange(STEPS) * STEP, MASK, HALF), ((0, 0), (0, BAND))),
        "step": np.concatenate([step, step.T], 1),
        "transform": np.concatenate(np.split(transform, 4, 0), 1),
    }
    return np.concatenate([parts[name] for name in TABLE_ROWS], 0)


def table_rows(name, start=0, count=None):
    names = list(TABLE_ROWS)
    first = sum(TABLE_ROWS[before] for before in names[: names.index(name)])
    return pl.ds(pl.multiple_of(first + start, 8), TABLE_ROWS[name] if count is None else count)


def shift_group():
    return table_rows("shift", 8 * (device_place() // 8), 8)


def own_shift(shifts_ref):
    return shifts_ref[pl.ds(lax.rem(device_place(), 8), 1), :]


def coarse_map():
    cosine, sine = tables(np.arange(COARSE), COARSE)
    upper = np.concatenate([cosine.T, sine.T], 1)
    lower = np.concatenate([-sine.T, cosine.T], 1)
    return bfloat(np.concatenate([upper, lower], 0))


def interpolation():
    ratio = GRID // COARSE
    frequency = np.arange(1, COARSE // 2)
    offset = np.arange(GRID)
    profile = 1.0 + 2.0 * np.cos(2.0 * math.pi * (np.outer(offset, frequency) % GRID) / GRID).sum(1)
    profile = (profile + np.cos(math.pi * offset / ratio)) / COARSE
    return bfloat(profile[(offset[None, :] - ratio * np.arange(COARSE)[:, None]) % GRID])


def device_place():
    return lax.axis_index("rows") * KERN + lax.axis_index("kern")


def turned_table(base, shift):
    cosine = base[:, :BAND] * shift[:, :BAND] - base[:, BAND:] * shift[:, BAND:]
    sine = base[:, BAND:] * shift[:, :BAND] + base[:, :BAND] * shift[:, BAND:]
    return cosine, sine


def params(limit=VMEM_LIMIT):
    return pltpu.CompilerParams(vmem_limit_bytes=limit)


def float_dot(left, right):
    return jnp.dot(left, right, preferred_element_type=jnp.float32)


def dot_first(left, right, precision=None):
    return lax.dot_general(
        left, right, (((0,), (0,)), ((), ())), precision=precision, preferred_element_type=jnp.float32
    )


def dot_last(left, right):
    return lax.dot_general(left, right, (((1,), (1,)), ((), ())), preferred_element_type=jnp.float32)


def split(values):
    high = values.astype(jnp.bfloat16)
    return high, (values - high.astype(jnp.float32)).astype(jnp.bfloat16)


def iotas(shape):
    return lax.broadcasted_iota(jnp.int32, shape, 0), lax.broadcasted_iota(jnp.int32, shape, 1)


def conjugate_mirror():
    row, column = iotas((BAND, BAND))
    real = (row + column == HALF) & (row < HALF) & (column > 0) & (column < HALF)
    imag = (row + column == 2 * HALF + HALF) & (row >= HALF) & (column > HALF)
    return (jnp.where(real, 1.0, 0.0) - jnp.where(imag, 1.0, 0.0)).astype(jnp.bfloat16)


def store_tiles(out_ref, real, imag):
    for part, value in enumerate((real, imag)):
        for i in range(BAND // 8):
            for j in range(2):
                out_ref[4 * i + 2 * part + j] = value[8 * i : 8 * i + 8, 128 * j : 128 * j + 128].astype(
                    out_ref.dtype
                )


def load_tiles(tiles_ref, held_ref):
    for part in range(2):
        for i in range(BAND // 8):
            for j in range(2):
                held_ref[part, 8 * i : 8 * i + 8, 128 * j : 128 * j + 128] = tiles_ref[
                    4 * i + 2 * part + j
                ].astype(jnp.float32)


def spectrum_kernel(
    mask_ref, constant_ref, target_ref, out_ref, grid_out_ref,
    grid_ref, held_ref, steps_ref, phases_ref, bases_ref, shifts_ref, grid_rows_ref, targets_ref,
    stack_a, stack_b, product_a, product_b, re_ref, im_ref, flat_ref, sems,
):
    rows = mask_ref.shape[0]
    grid_rows = target_ref.shape[0]
    stacks = (stack_a, stack_b)
    products = (product_a, product_b)
    count = rows // CHUNK
    places = [pl.ds(i * CHUNK, CHUNK) for i in range(count)]
    chunks = [None] + [
        pltpu.make_async_copy(mask_ref.at[places[i]], held_ref.at[places[i]], sems.at[i]) for i in range(1, count)
    ]
    columns = [pl.ds(quarter * QUARTER, QUARTER) for quarter in range(QUARTERS)]
    heads = [
        pltpu.make_async_copy(
            mask_ref.at[places[0], columns[quarter]],
            held_ref.at[places[0], columns[quarter]],
            sems.at[count + 7 + quarter],
        )
        for quarter in range(QUARTERS)
    ]
    small = [
        pltpu.make_async_copy(source, target, sems.at[count + i])
        for i, (source, target) in enumerate(
            (
                (constant_ref.at[table_rows("step"), pl.ds(0, BAND)], steps_ref),
                (constant_ref.at[table_rows("phase"), pl.ds(0, BAND)], phases_ref),
                (constant_ref.at[table_rows("grid", lax.axis_index("rows") * grid_rows, grid_rows)], grid_rows_ref),
                (target_ref, targets_ref),
                (constant_ref.at[table_rows("transform")], bases_ref),
                (constant_ref.at[shift_group()], shifts_ref),
            )
        )
    ]
    grid_copy = pltpu.make_async_copy(grid_ref, grid_out_ref, sems.at[count + 6])
    for copy in heads:
        copy.start()
    small[0].start()
    small[1].start()
    chunks[1].start()
    for copy in small[2:4] + chunks[2:] + small[4:]:
        copy.start()

    def steps_of(quarter):
        return range(quarter * STEPS // QUARTERS, (quarter + 1) * STEPS // QUARTERS)

    def transmit(i, quarter):
        total = None
        for step in steps_of(quarter):
            value = jnp.tanh(held_ref[places[i], step * STEP : (step + 1) * STEP])
            stacks[i % 2][step * CHUNK : (step + 1) * CHUNK] = value.astype(jnp.bfloat16)
            both = value[:, :HALF] + value[:, HALF:]
            total = both if total is None else total + both
        flat_ref[places[i]] = total if quarter == 0 else flat_ref[places[i]] + total

    def multiply(i, quarter):
        here = slice(steps_of(quarter).start * CHUNK, steps_of(quarter).stop * CHUNK)
        products[i % 2][here] = float_dot(stacks[i % 2][here], step_value)

    def gather(i, quarter):
        totals = [None] * 4
        for step in steps_of(quarter):
            cosine = phases_ref[step : step + 1, :HALF]
            sine = phases_ref[step : step + 1, HALF:BAND]
            first = products[i % 2][step * CHUNK : (step + 1) * CHUNK, :HALF]
            second = products[i % 2][step * CHUNK : (step + 1) * CHUNK, HALF:]
            at = 2 * (step % 2)
            for part, turned in enumerate(
                (first * cosine + second * sine, second * cosine - first * sine)
            ):
                totals[at + part] = turned if totals[at + part] is None else totals[at + part] + turned
        total_re = totals[0] + totals[2]
        total_im = totals[1] + totals[3]
        re_ref[places[i]] = total_re if quarter == 0 else re_ref[places[i]] + total_re
        im_ref[places[i]] = total_im if quarter == 0 else im_ref[places[i]] + total_im

    for quarter in range(QUARTERS):
        heads[quarter].wait()
        transmit(0, quarter)
    small[0].wait()
    small[1].wait()
    step_value = steps_ref[...].astype(jnp.bfloat16)
    for i in range(count):
        if i + 1 < count:
            chunks[i + 1].wait()
        for quarter in range(QUARTERS):
            multiply(i, quarter)
            if i + 1 < count:
                transmit(i + 1, quarter)
            if i > 0:
                gather(i - 1, quarter)
        if i == 1:
            for copy in small[2:4]:
                copy.wait()
            grid_ref[:grid_rows] = grid_rows_ref[...].astype(jnp.bfloat16)
            grid_ref[grid_rows:] = targets_ref[...].astype(jnp.float32).astype(jnp.bfloat16)
            grid_copy.start()
    for quarter in range(QUARTERS):
        gather(count - 1, quarter)
    for copy in small[4:]:
        copy.wait()
    _, lane = iotas((rows, HALF))
    mirror = conjugate_mirror()
    half_high, half_low = split(jnp.concatenate([re_ref[...], im_ref[...]], 1))
    other = float_dot(half_high, mirror) + float_dot(half_low, mirror)
    centre = jnp.sum(flat_ref[...], 1, keepdims=True) * (1.0 / MASK)
    other_high, other_low = split(
        jnp.concatenate([jnp.where(lane == 0, centre, other[:, :HALF]), other[:, HALF:]], 1)
    )
    high = jnp.concatenate([half_high, other_high], 1)
    low = jnp.concatenate([half_low, other_low], 1)
    transform = [bases_ref[:, at * rows : (at + 1) * rows].astype(jnp.bfloat16) for at in range(4)]
    product = float_dot(jnp.concatenate(transform, 0), high)
    rest = float_dot(jnp.concatenate(transform[:2], 0), low)
    product = product[: 2 * BAND] + (product[2 * BAND :] + rest)
    diagonal = jnp.equal(*iotas((BAND, BAND)))
    shift = own_shift(shifts_ref)
    turn_cos, turn_sin = [
        jnp.sum(jnp.where(diagonal, shift[:, part * BAND : (part + 1) * BAND], 0.0), 1, keepdims=True)
        for part in range(2)
    ]
    by_cos = product[:BAND]
    by_sin = product[BAND:]
    real = []
    imag = []
    for at in (0, 2 * HALF):
        part_re = by_cos[:, at : at + HALF] + by_sin[:, at + HALF : at + 2 * HALF]
        part_im = by_cos[:, at + HALF : at + 2 * HALF] - by_sin[:, at : at + HALF]
        real.append(turn_cos * part_re + turn_sin * part_im)
        imag.append(turn_cos * part_im - turn_sin * part_re)
    store_tiles(out_ref, jnp.concatenate(real, 1), jnp.concatenate(imag, 1))
    grid_copy.wait()


def mask_spectrum(mask_params, constants, target):
    rows = mask_params.shape[0]
    stacked = STEPS * CHUNK
    arguments = (mask_params, constants, target)
    grid_rows = target.shape[0]
    return pl.pallas_call(
        spectrum_kernel,
        in_specs=[pl.BlockSpec(memory_space=pltpu.HBM)] * len(arguments),
        out_specs=[pl.BlockSpec(memory_space=pltpu.VMEM), pl.BlockSpec(memory_space=pltpu.HBM)],
        out_shape=[
            jax.ShapeDtypeStruct((DEVICES, 8, 128), jnp.bfloat16),
            jax.ShapeDtypeStruct((2 * grid_rows, 2 * BAND), jnp.bfloat16),
        ],
        scratch_shapes=[
            pltpu.VMEM((2 * grid_rows, 2 * BAND), jnp.bfloat16),
            pltpu.VMEM((rows, MASK), jnp.float32),
            pltpu.VMEM((STEP, BAND), jnp.float32),
            pltpu.VMEM((STEPS, BAND), jnp.float32),
            pltpu.VMEM((STEP, 2 * BAND), jnp.float32),
            pltpu.VMEM((8, 2 * BAND), jnp.float32),
            pltpu.VMEM((grid_rows, 2 * BAND), jnp.float32),
            pltpu.VMEM(target.shape, jnp.int32),
            pltpu.VMEM((stacked, STEP), jnp.bfloat16),
            pltpu.VMEM((stacked, STEP), jnp.bfloat16),
            pltpu.VMEM((stacked, BAND), jnp.float32),
            pltpu.VMEM((stacked, BAND), jnp.float32),
            pltpu.VMEM((rows, HALF), jnp.float32),
            pltpu.VMEM((rows, HALF), jnp.float32),
            pltpu.VMEM((rows, HALF), jnp.float32),
            pltpu.SemaphoreType.DMA((rows // CHUNK + 7 + QUARTERS,)),
        ],
        compiler_params=params(STREAM_LIMIT),
        name="mask_spectrum",
    )(*arguments)


def field_kernel(tiles_ref, pupil_ref, grid_ref, map_ref, field_ref, power_ref, spec_ref, partial_ref):
    members = pupil_ref.shape[0]
    rows = grid_ref.shape[0] // 2
    slab = rows // KERN
    load_tiles(tiles_ref, spec_ref)
    spec_re = spec_ref[0]
    spec_im = spec_ref[1]
    for member in range(members):
        for corner in range(2):
            kernel_re = pupil_ref[member, corner, 0]
            kernel_im = pupil_ref[member, corner, 1]
            amp_re = (kernel_re * spec_re - kernel_im * spec_im).astype(jnp.bfloat16)
            amp_im = (kernel_re * spec_im + kernel_im * spec_re).astype(jnp.bfloat16)
            block = jnp.concatenate(
                [jnp.concatenate([amp_re, amp_im], 1), jnp.concatenate([-amp_im, amp_re], 1)], 0
            )
            partial_ref[member, corner * rows : (corner + 1) * rows] = float_dot(grid_ref[:rows], block).astype(
                jnp.bfloat16
            )
        field_ref[member] = float_dot(partial_ref[member], map_ref[...])
    for owner in range(KERN):
        power_ref[owner, 2] = grid_ref[rows + owner * slab : rows + (owner + 1) * slab]
        for corner in range(2):
            at = corner * rows + owner * slab
            power = None
            for member in range(members):
                real = field_ref[member, at : at + slab, :COARSE]
                imag = field_ref[member, at : at + slab, COARSE:]
                term = real * real + imag * imag
                power = term if member == 0 else power + term
            power_ref[owner, corner] = power.astype(jnp.bfloat16)


def coarse_fields(tiles, pupils, grid_table, column_map):
    members = pupils.shape[0]
    rows = grid_table.shape[0] // 2
    vmem = pl.BlockSpec(memory_space=pltpu.VMEM)
    return pl.pallas_call(
        field_kernel,
        in_specs=[vmem] * 4,
        out_specs=[vmem] * 2,
        out_shape=[
            jax.ShapeDtypeStruct((members, 2 * rows, 2 * COARSE), jnp.float32),
            jax.ShapeDtypeStruct((KERN, 3, rows // KERN, COARSE), jnp.bfloat16),
        ],
        scratch_shapes=[
            pltpu.VMEM((2, BAND, BAND), jnp.float32),
            pltpu.VMEM((members, 2 * rows, 2 * BAND), jnp.bfloat16),
        ],
        compiler_params=params(),
        name="coarse_fields",
    )(tiles, pupils, grid_table, column_map)


def adjoint_kernel(parts_ref, matrix_ref, out_ref):
    rows = parts_ref.shape[2]
    width = GRID // KERN
    powers = []
    for corner in range(2):
        total = parts_ref[0, corner].astype(jnp.float32)
        for owner in range(1, KERN):
            total = total + parts_ref[owner, corner].astype(jnp.float32)
        powers.append(total.astype(jnp.bfloat16))
    power = jnp.concatenate(powers, 0)
    folded = None
    for slab in range(KERN):
        columns = slice(slab * width, (slab + 1) * width)
        fine = float_dot(power, matrix_ref[:, columns])
        wanted = parts_ref[slab, 2].astype(jnp.float32)
        corners = []
        for corner in range(2):
            dose = dose_levels[corner]
            resist = jax.nn.sigmoid(steepness * (dose * fine[corner * rows : (corner + 1) * rows] - threshold))
            corners.append(
                (2.0 * (resist - wanted) * resist * (1.0 - resist) * steepness * dose).astype(jnp.bfloat16)
            )
        term = dot_last(jnp.concatenate(corners, 0), matrix_ref[:, columns])
        folded = term if slab == 0 else folded + term
    folded = folded.reshape(2, rows, COARSE).astype(jnp.bfloat16)
    for owner in range(KERN):
        out_ref[owner] = folded


def coarse_adjoint(parts, matrix):
    rows = parts.shape[2]
    return pl.pallas_call(
        adjoint_kernel,
        in_specs=[pl.BlockSpec(memory_space=pltpu.VMEM)] * 2,
        out_specs=pl.BlockSpec(memory_space=pltpu.VMEM),
        out_shape=jax.ShapeDtypeStruct((KERN, 2, rows, COARSE), jnp.bfloat16),
        compiler_params=params(),
        name="coarse_adjoint",
    )(parts, matrix)


def gradient_kernel(field_ref, adjoint_ref, pupil_ref, grid_ref, map_ref, out_ref, weighted_ref, back_ref, acc_ref):
    members = pupil_ref.shape[0]
    slab = adjoint_ref.shape[2]
    rows = slab * KERN
    table = grid_ref[:rows].T
    for member in range(members):
        for corner in range(2):
            for owner in range(KERN):
                at = corner * rows + owner * slab
                adjoint = 2.0 * adjoint_ref[owner, corner].astype(jnp.float32)
                for half in range(2):
                    columns = slice(half * COARSE, (half + 1) * COARSE)
                    weighted_ref[member, at : at + slab, columns] = (
                        field_ref[member, at : at + slab, columns] * adjoint
                    ).astype(jnp.bfloat16)
        back_ref[member] = float_dot(weighted_ref[member], map_ref[...]).astype(jnp.bfloat16)
        for corner in range(2):
            grads = float_dot(table, back_ref[member, corner * rows : (corner + 1) * rows])
            grad_re = grads[:BAND, :BAND] + grads[BAND:, BAND:]
            grad_im = grads[:BAND, BAND:] - grads[BAND:, :BAND]
            kernel_re = pupil_ref[member, corner, 0]
            kernel_im = pupil_ref[member, corner, 1]
            term_re = kernel_re * grad_re + kernel_im * grad_im
            term_im = kernel_re * grad_im - kernel_im * grad_re
            first = member == 0 and corner == 0
            acc_ref[0] = term_re if first else acc_ref[0] + term_re
            acc_ref[1] = term_im if first else acc_ref[1] + term_im
    store_tiles(out_ref, acc_ref[0], acc_ref[1])


def spectrum_gradient(fields, adjoint, pupils, grid_table, column_map):
    members = pupils.shape[0]
    rows = grid_table.shape[0] // 2
    vmem = pl.BlockSpec(memory_space=pltpu.VMEM)
    return pl.pallas_call(
        gradient_kernel,
        in_specs=[vmem] * 5,
        out_specs=vmem,
        out_shape=jax.ShapeDtypeStruct((DEVICES, 8, 128), jnp.bfloat16),
        scratch_shapes=[
            pltpu.VMEM((members, 2 * rows, 2 * COARSE), jnp.bfloat16),
            pltpu.VMEM((members, 2 * rows, 2 * BAND), jnp.bfloat16),
            pltpu.VMEM((2, BAND, BAND), jnp.float32),
        ],
        compiler_params=params(),
        name="spectrum_gradient",
    )(fields, adjoint, pupils, grid_table, column_map)


def update_kernel(
    tiles_ref, constant_ref, mask_ref, out_ref,
    tile_ref, spec_ref, bases_ref, shifts_ref, held_ref, steps_ref, phases_ref, re_ref, im_ref, flat_ref, stack_a, stack_b, product_a, product_b, sems,
):
    rows = mask_ref.shape[0]
    stacks = (stack_a, stack_b)
    products = (product_a, product_b)
    count = rows // CHUNK
    places = [pl.ds(i * CHUNK, CHUNK) for i in range(count)]
    chunks = [
        pltpu.make_async_copy(mask_ref.at[places[i]], held_ref.at[places[i]], sems.at[i]) for i in range(count)
    ]
    columns = [pl.ds(quarter * QUARTER, QUARTER) for quarter in range(QUARTERS)]
    results = [
        pltpu.make_async_copy(
            held_ref.at[places[i], columns[quarter]],
            out_ref.at[places[i], columns[quarter]],
            sems.at[count + 5 + QUARTERS * i + quarter],
        )
        for i in range(count)
        for quarter in range(QUARTERS)
    ]
    small = [
        pltpu.make_async_copy(source, target, sems.at[count + i])
        for i, (source, target) in enumerate(
            (
                (constant_ref.at[table_rows("base")], bases_ref),
                (constant_ref.at[shift_group()], shifts_ref),
                (tiles_ref, tile_ref),
                (constant_ref.at[table_rows("phase"), pl.ds(0, BAND)], phases_ref),
                (constant_ref.at[table_rows("step"), pl.ds(BAND, BAND)], steps_ref),
            )
        )
    ]
    for copy in small + chunks:
        copy.start()

    small[0].wait()
    small[1].wait()
    cosine, sine = turned_table(bases_ref[...], own_shift(shifts_ref))
    small[2].wait()
    load_tiles(tile_ref, spec_ref)
    gradient = jnp.concatenate([spec_ref[0], spec_ref[1]], 1).astype(jnp.bfloat16)
    product = float_dot(jnp.concatenate(split(cosine) + split(sine), 0), gradient)
    by_cos = product[:rows] + product[rows : 2 * rows]
    by_sin = product[2 * rows : 3 * rows] + product[3 * rows :]
    col_re = by_cos[:, :BAND] - by_sin[:, BAND:]
    col_im = by_sin[:, :BAND] + by_cos[:, BAND:]
    flat_ref[...] = jnp.broadcast_to(col_re[:, HALF : HALF + 1] * (1.0 / MASK), flat_ref.shape)
    mirror = conjugate_mirror()
    right = jnp.concatenate([col_re[:, HALF:], col_im[:, HALF:]], 1).astype(jnp.bfloat16)
    other = float_dot(right, mirror)
    re_ref[...] = col_re[:, :HALF] + other[:, :HALF]
    im_ref[...] = col_im[:, :HALF] + other[:, HALF:]

    def steps_of(quarter):
        return range(quarter * STEPS // QUARTERS, (quarter + 1) * STEPS // QUARTERS)

    def turn(i, quarter):
        col_re = re_ref[places[i]]
        col_im = im_ref[places[i]]
        for step in steps_of(quarter):
            cosine = phases_ref[step : step + 1, :HALF]
            sine = phases_ref[step : step + 1, HALF:BAND]
            here = slice(step * CHUNK, (step + 1) * CHUNK)
            stacks[i % 2][here, :HALF] = (col_re * cosine - col_im * sine).astype(jnp.bfloat16)
            stacks[i % 2][here, HALF:] = (col_re * sine + col_im * cosine).astype(jnp.bfloat16)

    def multiply(i, quarter):
        here = slice(steps_of(quarter).start * CHUNK, steps_of(quarter).stop * CHUNK)
        products[i % 2][here] = float_dot(stacks[i % 2][here], step_value)

    def finish(i, quarter):
        centre = flat_ref[places[i]]
        for step in steps_of(quarter):
            here = slice(step * STEP, (step + 1) * STEP)
            mask = held_ref[places[i], here]
            transmit = jnp.tanh(mask)
            pixel_grad = products[i % 2][step * CHUNK : (step + 1) * CHUNK] + centre
            held_ref[places[i], here] = mask - step_size * pixel_grad * (1.0 - transmit * transmit)

    small[3].wait()
    for quarter in range(QUARTERS):
        turn(0, quarter)
    small[4].wait()
    step_value = steps_ref[...].astype(jnp.bfloat16)
    for i in range(count + 1):
        if i > 0:
            chunks[i - 1].wait()
        for quarter in range(QUARTERS):
            if i < count:
                multiply(i, quarter)
            if i + 1 < count:
                turn(i + 1, quarter)
            if i > 0:
                finish(i - 1, quarter)
                results[QUARTERS * (i - 1) + quarter].start()
    for copy in results:
        copy.wait()


def mask_update(tiles, constants, mask_params):
    rows = mask_params.shape[0]
    stacked = STEPS * CHUNK
    hbm = pl.BlockSpec(memory_space=pltpu.HBM)
    return pl.pallas_call(
        update_kernel,
        in_specs=[hbm] * 3,
        out_specs=hbm,
        out_shape=jax.ShapeDtypeStruct((rows, MASK), jnp.float32),
        scratch_shapes=[
            pltpu.VMEM(tiles.shape, jnp.bfloat16),
            pltpu.VMEM((2, BAND, BAND), jnp.float32),
            pltpu.VMEM((rows, 2 * BAND), jnp.float32),
            pltpu.VMEM((8, 2 * BAND), jnp.float32),
            pltpu.VMEM((rows, MASK), jnp.float32),
            pltpu.VMEM((STEP, BAND), jnp.float32),
            pltpu.VMEM((STEPS, BAND), jnp.float32),
            pltpu.VMEM((rows, HALF), jnp.float32),
            pltpu.VMEM((rows, HALF), jnp.float32),
            pltpu.VMEM((rows, STEP), jnp.float32),
            pltpu.VMEM((stacked, BAND), jnp.bfloat16),
            pltpu.VMEM((stacked, BAND), jnp.bfloat16),
            pltpu.VMEM((stacked, STEP), jnp.float32),
            pltpu.VMEM((stacked, STEP), jnp.float32),
            pltpu.SemaphoreType.DMA(((QUARTERS + 1) * (rows // CHUNK) + 5,)),
        ],
        compiler_params=params(STREAM_LIMIT),
        name="mask_update",
    )(tiles, constants, mask_params)


def exchange(values, axes):
    return lax.all_to_all(values, axes, 0, 0, tiled=True)


def summed(parts, copies):
    total = jnp.sum(parts.astype(jnp.float32), 0).astype(parts.dtype)
    return jnp.broadcast_to(total[None], (copies,) + total.shape)


def total_kernel(parts_ref, out_ref):
    total = jnp.sum(parts_ref[...].astype(jnp.float32), 0).astype(out_ref.dtype)
    for owner in range(DEVICES):
        out_ref[owner] = total


def total_tiles(parts):
    vmem = pl.BlockSpec(memory_space=pltpu.VMEM)
    return pl.pallas_call(
        total_kernel,
        in_specs=[vmem],
        out_specs=vmem,
        out_shape=jax.ShapeDtypeStruct(parts.shape, parts.dtype),
        compiler_params=params(),
        cost_estimate=pl.CostEstimate(flops=10**10, bytes_accessed=2 * parts.size, transcendentals=0),
        name="total_tiles",
    )(parts)


def local(mask_params, pupil_kernels, target_pattern):
    rows = mask_params.shape[0]
    constants = jnp.asarray(constant_table(rows))
    column_map = jnp.asarray(coarse_map())

    everyone = ("kern", "rows")
    tiles, grid_table = mask_spectrum(mask_params, constants, target_pattern)
    spectrum = exchange(total_tiles(exchange(tiles, everyone)), everyone)
    fields, powers = coarse_fields(spectrum, pupil_kernels, grid_table, column_map)
    adjoint = coarse_adjoint(exchange(powers, "kern"), jnp.asarray(interpolation()))
    column_back = jnp.asarray(coarse_map().T.copy())
    gradient = spectrum_gradient(fields, exchange(adjoint, "kern"), pupil_kernels, grid_table, column_back)
    gradient = exchange(summed(exchange(gradient, everyone), DEVICES), everyone)
    return mask_update(gradient, constants, mask_params)


def solution(mesh):
    placed = (P(("rows", "kern"), None), P("kern", None, None, None, None), P("rows", "kern"))
    return jax.shard_map(
        local, mesh=mesh, in_specs=placed, out_specs=P(("rows", "kern"), None), check_vma=False
    )
```

```python
import math

import jax
import jax.numpy as jnp
import numpy as np
from jax import lax
from jax.experimental import pallas as pl
from jax.experimental.pallas import tpu as pltpu
from jax.sharding import PartitionSpec as P

MASK = 16384
GRID = 4096
BAND = 256
HALF = BAND // 2
COARSE = 512
STEP = 256
STEPS = MASK // STEP
ROWS = 16
KERN = 8
DEVICES = ROWS * KERN
CHUNK = 16
QUARTERS = 2
QUARTER = MASK // QUARTERS

steepness = 4.0
threshold = 0.75
step_size = 1.0
dose_levels = (1.0, 1.15)

VMEM_LIMIT = 24 * 1024 * 1024
STREAM_LIMIT = 53 * 1024 * 1024


def tables(positions, period, count=BAND):
    frequency = np.arange(count) - BAND // 2
    angles = (np.outer(positions, frequency) % period) * (2.0 * math.pi / period)
    return np.cos(angles), np.sin(angles)


def bfloat(values):
    return np.asarray(values, np.float32).astype(jnp.bfloat16)


def wide_table(positions, period, count=BAND):
    return np.concatenate(tables(positions, period, count), 1).astype(np.float32)


def step_table():
    cosine, sine = tables(np.arange(STEP), MASK, HALF)
    return bfloat(np.concatenate([cosine, -sine], 1) / MASK)


def row_transform(rows):
    table = wide_table(np.arange(rows), MASK).T
    high = bfloat(table)
    return np.concatenate([high, bfloat(table - high.astype(np.float32))], 0)


TABLE_ROWS = {"grid": GRID, "base": 128, "shift": DEVICES, "phase": STEPS, "step": STEP, "transform": STEP}


def constant_table(rows):
    step = step_table().astype(np.float32)
    transform = row_transform(rows).astype(np.float32)
    parts = {
        "grid": wide_table(np.arange(GRID), GRID),
        "base": wide_table(np.arange(rows), MASK),
        "shift": wide_table(np.arange(DEVICES) * rows, MASK),
        "phase": np.pad(wide_table(np.arange(STEPS) * STEP, MASK, HALF), ((0, 0), (0, BAND))),
        "step": np.concatenate([step, step.T], 1),
        "transform": np.concatenate(np.split(transform, 4, 0), 1),
    }
    return np.concatenate([parts[name] for name in TABLE_ROWS], 0)


def table_rows(name, start=0, count=None):
    names = list(TABLE_ROWS)
    first = sum(TABLE_ROWS[before] for before in names[: names.index(name)])
    return pl.ds(pl.multiple_of(first + start, 8), TABLE_ROWS[name] if count is None else count)


def shift_group():
    return table_rows("shift", 8 * (device_place() // 8), 8)


def own_shift(shifts_ref):
    return shifts_ref[pl.ds(lax.rem(device_place(), 8), 1), :]


def coarse_map():
    cosine, sine = tables(np.arange(COARSE), COARSE)
    upper = np.concatenate([cosine.T, sine.T], 1)
    lower = np.concatenate([-sine.T, cosine.T], 1)
    return bfloat(np.concatenate([upper, lower], 0))


def interpolation():
    ratio = GRID // COARSE
    frequency = np.arange(1, COARSE // 2)
    offset = np.arange(GRID)
    profile = 1.0 + 2.0 * np.cos(2.0 * math.pi * (np.outer(offset, frequency) % GRID) / GRID).sum(1)
    profile = (profile + np.cos(math.pi * offset / ratio)) / COARSE
    return bfloat(profile[(offset[None, :] - ratio * np.arange(COARSE)[:, None]) % GRID])


def device_place():
    return lax.axis_index("rows") * KERN + lax.axis_index("kern")


def turned_table(base, shift):
    cosine = base[:, :BAND] * shift[:, :BAND] - base[:, BAND:] * shift[:, BAND:]
    sine = base[:, BAND:] * shift[:, :BAND] + base[:, :BAND] * shift[:, BAND:]
    return cosine, sine


def params(limit=VMEM_LIMIT):
    return pltpu.CompilerParams(vmem_limit_bytes=limit)


def float_dot(left, right):
    return jnp.dot(left, right, preferred_element_type=jnp.float32)


def dot_first(left, right, precision=None):
    return lax.dot_general(
        left, right, (((0,), (0,)), ((), ())), precision=precision, preferred_element_type=jnp.float32
    )


def dot_last(left, right):
    return lax.dot_general(left, right, (((1,), (1,)), ((), ())), preferred_element_type=jnp.float32)


def split(values):
    high = values.astype(jnp.bfloat16)
    return high, (values - high.astype(jnp.float32)).astype(jnp.bfloat16)


def iotas(shape):
    return lax.broadcasted_iota(jnp.int32, shape, 0), lax.broadcasted_iota(jnp.int32, shape, 1)


def conjugate_mirror():
    row, column = iotas((BAND, BAND))
    real = (row + column == HALF) & (row < HALF) & (column > 0) & (column < HALF)
    imag = (row + column == 2 * HALF + HALF) & (row >= HALF) & (column > HALF)
    return (jnp.where(real, 1.0, 0.0) - jnp.where(imag, 1.0, 0.0)).astype(jnp.bfloat16)


def store_tiles(out_ref, real, imag):
    for part, value in enumerate((real, imag)):
        for i in range(BAND // 8):
            for j in range(2):
                out_ref[4 * i + 2 * part + j] = value[8 * i : 8 * i + 8, 128 * j : 128 * j + 128].astype(
                    out_ref.dtype
                )


def load_tiles(tiles_ref, held_ref):
    for part in range(2):
        for i in range(BAND // 8):
            for j in range(2):
                held_ref[part, 8 * i : 8 * i + 8, 128 * j : 128 * j + 128] = tiles_ref[
                    4 * i + 2 * part + j
                ].astype(jnp.float32)


def spectrum_kernel(
    mask_ref, constant_ref, target_ref, out_ref, grid_out_ref,
    grid_ref, held_ref, steps_ref, phases_ref, bases_ref, shifts_ref, grid_rows_ref, targets_ref,
    stack_a, stack_b, product_a, product_b, re_ref, im_ref, flat_ref, sems,
):
    rows = mask_ref.shape[0]
    grid_rows = target_ref.shape[0]
    stacks = (stack_a, stack_b)
    products = (product_a, product_b)
    count = rows // CHUNK
    places = [pl.ds(i * CHUNK, CHUNK) for i in range(count)]
    chunks = [None] + [
        pltpu.make_async_copy(mask_ref.at[places[i]], held_ref.at[places[i]], sems.at[i]) for i in range(1, count)
    ]
    columns = [pl.ds(quarter * QUARTER, QUARTER) for quarter in range(QUARTERS)]
    heads = [
        pltpu.make_async_copy(
            mask_ref.at[places[0], columns[quarter]],
            held_ref.at[places[0], columns[quarter]],
            sems.at[count + 7 + quarter],
        )
        for quarter in range(QUARTERS)
    ]
    small = [
        pltpu.make_async_copy(source, target, sems.at[count + i])
        for i, (source, target) in enumerate(
            (
                (constant_ref.at[table_rows("step"), pl.ds(0, BAND)], steps_ref),
                (constant_ref.at[table_rows("phase"), pl.ds(0, BAND)], phases_ref),
                (constant_ref.at[table_rows("grid", lax.axis_index("rows") * grid_rows, grid_rows)], grid_rows_ref),
                (target_ref, targets_ref),
                (constant_ref.at[table_rows("transform")], bases_ref),
                (constant_ref.at[shift_group()], shifts_ref),
            )
        )
    ]
    grid_copy = pltpu.make_async_copy(grid_ref, grid_out_ref, sems.at[count + 6])
    for copy in heads:
        copy.start()
    small[0].start()
    small[1].start()
    chunks[1].start()
    for copy in small[2:4] + chunks[2:] + small[4:]:
        copy.start()

    def steps_of(quarter):
        return range(quarter * STEPS // QUARTERS, (quarter + 1) * STEPS // QUARTERS)

    def transmit(i, quarter):
        total = None
        for step in steps_of(quarter):
            value = jnp.tanh(held_ref[places[i], step * STEP : (step + 1) * STEP])
            stacks[i % 2][step * CHUNK : (step + 1) * CHUNK] = value.astype(jnp.bfloat16)
            both = value[:, :HALF] + value[:, HALF:]
            total = both if total is None else total + both
        flat_ref[places[i]] = total if quarter == 0 else flat_ref[places[i]] + total

    def multiply(i, quarter):
        here = slice(steps_of(quarter).start * CHUNK, steps_of(quarter).stop * CHUNK)
        products[i % 2][here] = float_dot(stacks[i % 2][here], step_value)

    def gather(i, quarter):
        totals = [None] * 4
        for step in steps_of(quarter):
            cosine = phases_ref[step : step + 1, :HALF]
            sine = phases_ref[step : step + 1, HALF:BAND]
            first = products[i % 2][step * CHUNK : (step + 1) * CHUNK, :HALF]
            second = products[i % 2][step * CHUNK : (step + 1) * CHUNK, HALF:]
            at = 2 * (step % 2)
            for part, turned in enumerate(
                (first * cosine + second * sine, second * cosine - first * sine)
            ):
                totals[at + part] = turned if totals[at + part] is None else totals[at + part] + turned
        total_re = totals[0] + totals[2]
        total_im = totals[1] + totals[3]
        re_ref[places[i]] = total_re if quarter == 0 else re_ref[places[i]] + total_re
        im_ref[places[i]] = total_im if quarter == 0 else im_ref[places[i]] + total_im

    for quarter in range(QUARTERS):
        heads[quarter].wait()
        transmit(0, quarter)
    small[0].wait()
    small[1].wait()
    step_value = steps_ref[...].astype(jnp.bfloat16)
    for i in range(count):
        if i + 1 < count:
            chunks[i + 1].wait()
        for quarter in range(QUARTERS):
            multiply(i, quarter)
            if i + 1 < count:
                transmit(i + 1, quarter)
            if i > 0:
                gather(i - 1, quarter)
        if i == 1:
            for copy in small[2:4]:
                copy.wait()
            grid_ref[:grid_rows] = grid_rows_ref[...].astype(jnp.bfloat16)
            grid_ref[grid_rows:] = targets_ref[...].astype(jnp.float32).astype(jnp.bfloat16)
            grid_copy.start()
    for quarter in range(QUARTERS):
        gather(count - 1, quarter)
    for copy in small[4:]:
        copy.wait()
    _, lane = iotas((rows, HALF))
    mirror = conjugate_mirror()
    half_high, half_low = split(jnp.concatenate([re_ref[...], im_ref[...]], 1))
    other = float_dot(half_high, mirror) + float_dot(half_low, mirror)
    centre = jnp.sum(flat_ref[...], 1, keepdims=True) * (1.0 / MASK)
    other_high, other_low = split(
        jnp.concatenate([jnp.where(lane == 0, centre, other[:, :HALF]), other[:, HALF:]], 1)
    )
    high = jnp.concatenate([half_high, other_high], 1)
    low = jnp.concatenate([half_low, other_low], 1)
    transform = [bases_ref[:, at * rows : (at + 1) * rows].astype(jnp.bfloat16) for at in range(4)]
    product = float_dot(jnp.concatenate(transform, 0), high)
    rest = float_dot(jnp.concatenate(transform[:2], 0), low)
    product = product[: 2 * BAND] + (product[2 * BAND :] + rest)
    diagonal = jnp.equal(*iotas((BAND, BAND)))
    shift = own_shift(shifts_ref)
    turn_cos, turn_sin = [
        jnp.sum(jnp.where(diagonal, shift[:, part * BAND : (part + 1) * BAND], 0.0), 1, keepdims=True)
        for part in range(2)
    ]
    by_cos = product[:BAND]
    by_sin = product[BAND:]
    real = []
    imag = []
    for at in (0, 2 * HALF):
        part_re = by_cos[:, at : at + HALF] + by_sin[:, at + HALF : at + 2 * HALF]
        part_im = by_cos[:, at + HALF : at + 2 * HALF] - by_sin[:, at : at + HALF]
        real.append(turn_cos * part_re + turn_sin * part_im)
        imag.append(turn_cos * part_im - turn_sin * part_re)
    store_tiles(out_ref, jnp.concatenate(real, 1), jnp.concatenate(imag, 1))
    grid_copy.wait()


def mask_spectrum(mask_params, constants, target):
    rows = mask_params.shape[0]
    stacked = STEPS * CHUNK
    arguments = (mask_params, constants, target)
    grid_rows = target.shape[0]
    return pl.pallas_call(
        spectrum_kernel,
        in_specs=[pl.BlockSpec(memory_space=pltpu.HBM)] * len(arguments),
        out_specs=[pl.BlockSpec(memory_space=pltpu.VMEM), pl.BlockSpec(memory_space=pltpu.HBM)],
        out_shape=[
            jax.ShapeDtypeStruct((DEVICES, 8, 128), jnp.bfloat16),
            jax.ShapeDtypeStruct((2 * grid_rows, 2 * BAND), jnp.bfloat16),
        ],
        scratch_shapes=[
            pltpu.VMEM((2 * grid_rows, 2 * BAND), jnp.bfloat16),
            pltpu.VMEM((rows, MASK), jnp.float32),
            pltpu.VMEM((STEP, BAND), jnp.float32),
            pltpu.VMEM((STEPS, BAND), jnp.float32),
            pltpu.VMEM((STEP, 2 * BAND), jnp.float32),
            pltpu.VMEM((8, 2 * BAND), jnp.float32),
            pltpu.VMEM((grid_rows, 2 * BAND), jnp.float32),
            pltpu.VMEM(target.shape, jnp.int32),
            pltpu.VMEM((stacked, STEP), jnp.bfloat16),
            pltpu.VMEM((stacked, STEP), jnp.bfloat16),
            pltpu.VMEM((stacked, BAND), jnp.float32),
            pltpu.VMEM((stacked, BAND), jnp.float32),
            pltpu.VMEM((rows, HALF), jnp.float32),
            pltpu.VMEM((rows, HALF), jnp.float32),
            pltpu.VMEM((rows, HALF), jnp.float32),
            pltpu.SemaphoreType.DMA((rows // CHUNK + 7 + QUARTERS,)),
        ],
        compiler_params=params(STREAM_LIMIT),
        name="mask_spectrum",
    )(*arguments)


def field_kernel(tiles_ref, pupil_ref, grid_ref, map_ref, field_ref, power_ref, spec_ref, partial_ref):
    members = pupil_ref.shape[0]
    rows = grid_ref.shape[0] // 2
    slab = rows // KERN
    load_tiles(tiles_ref, spec_ref)
    spec_re = spec_ref[0]
    spec_im = spec_ref[1]
    for member in range(members):
        for corner in range(2):
            kernel_re = pupil_ref[member, corner, 0]
            kernel_im = pupil_ref[member, corner, 1]
            amp_re = (kernel_re * spec_re - kernel_im * spec_im).astype(jnp.bfloat16)
            amp_im = (kernel_re * spec_im + kernel_im * spec_re).astype(jnp.bfloat16)
            block = jnp.concatenate(
                [jnp.concatenate([amp_re, amp_im], 1), jnp.concatenate([-amp_im, amp_re], 1)], 0
            )
            partial_ref[member, corner * rows : (corner + 1) * rows] = float_dot(grid_ref[:rows], block).astype(
                jnp.bfloat16
            )
        field_ref[member] = float_dot(partial_ref[member], map_ref[...])
    for owner in range(KERN):
        power_ref[owner, 2] = grid_ref[rows + owner * slab : rows + (owner + 1) * slab]
        for corner in range(2):
            at = corner * rows + owner * slab
            power = None
            for member in range(members):
                real = field_ref[member, at : at + slab, :COARSE]
                imag = field_ref[member, at : at + slab, COARSE:]
                term = real * real + imag * imag
                power = term if member == 0 else power + term
            power_ref[owner, corner] = power.astype(jnp.bfloat16)


def coarse_fields(tiles, pupils, grid_table, column_map):
    members = pupils.shape[0]
    rows = grid_table.shape[0] // 2
    vmem = pl.BlockSpec(memory_space=pltpu.VMEM)
    return pl.pallas_call(
        field_kernel,
        in_specs=[vmem] * 4,
        out_specs=[vmem] * 2,
        out_shape=[
            jax.ShapeDtypeStruct((members, 2 * rows, 2 * COARSE), jnp.float32),
            jax.ShapeDtypeStruct((KERN, 3, rows // KERN, COARSE), jnp.bfloat16),
        ],
        scratch_shapes=[
            pltpu.VMEM((2, BAND, BAND), jnp.float32),
            pltpu.VMEM((members, 2 * rows, 2 * BAND), jnp.bfloat16),
        ],
        compiler_params=params(),
        name="coarse_fields",
    )(tiles, pupils, grid_table, column_map)


def adjoint_kernel(parts_ref, matrix_ref, out_ref):
    rows = parts_ref.shape[2]
    width = GRID // KERN
    powers = []
    for corner in range(2):
        total = parts_ref[0, corner].astype(jnp.float32)
        for owner in range(1, KERN):
            total = total + parts_ref[owner, corner].astype(jnp.float32)
        powers.append(total.astype(jnp.bfloat16))
    power = jnp.concatenate(powers, 0)
    folded = None
    for slab in range(KERN):
        columns = slice(slab * width, (slab + 1) * width)
        fine = float_dot(power, matrix_ref[:, columns])
        wanted = parts_ref[slab, 2].astype(jnp.float32)
        corners = []
        for corner in range(2):
            dose = dose_levels[corner]
            resist = jax.nn.sigmoid(steepness * (dose * fine[corner * rows : (corner + 1) * rows] - threshold))
            corners.append(
                (2.0 * (resist - wanted) * resist * (1.0 - resist) * steepness * dose).astype(jnp.bfloat16)
            )
        term = dot_last(jnp.concatenate(corners, 0), matrix_ref[:, columns])
        folded = term if slab == 0 else folded + term
    folded = folded.reshape(2, rows, COARSE).astype(jnp.bfloat16)
    for owner in range(KERN):
        out_ref[owner] = folded


def coarse_adjoint(parts, matrix):
    rows = parts.shape[2]
    return pl.pallas_call(
        adjoint_kernel,
        in_specs=[pl.BlockSpec(memory_space=pltpu.VMEM)] * 2,
        out_specs=pl.BlockSpec(memory_space=pltpu.VMEM),
        out_shape=jax.ShapeDtypeStruct((KERN, 2, rows, COARSE), jnp.bfloat16),
        compiler_params=params(),
        name="coarse_adjoint",
    )(parts, matrix)


def gradient_kernel(field_ref, adjoint_ref, pupil_ref, grid_ref, map_ref, out_ref, weighted_ref, back_ref, acc_ref):
    members = pupil_ref.shape[0]
    slab = adjoint_ref.shape[2]
    rows = slab * KERN
    table = grid_ref[:rows].T
    for member in range(members):
        for corner in range(2):
            for owner in range(KERN):
                at = corner * rows + owner * slab
                adjoint = 2.0 * adjoint_ref[owner, corner].astype(jnp.float32)
                for half in range(2):
                    columns = slice(half * COARSE, (half + 1) * COARSE)
                    weighted_ref[member, at : at + slab, columns] = (
                        field_ref[member, at : at + slab, columns] * adjoint
                    ).astype(jnp.bfloat16)
        back_ref[member] = dot_last(weighted_ref[member], map_ref[...]).astype(jnp.bfloat16)
        for corner in range(2):
            grads = float_dot(table, back_ref[member, corner * rows : (corner + 1) * rows])
            grad_re = grads[:BAND, :BAND] + grads[BAND:, BAND:]
            grad_im = grads[:BAND, BAND:] - grads[BAND:, :BAND]
            kernel_re = pupil_ref[member, corner, 0]
            kernel_im = pupil_ref[member, corner, 1]
            term_re = kernel_re * grad_re + kernel_im * grad_im
            term_im = kernel_re * grad_im - kernel_im * grad_re
            first = member == 0 and corner == 0
            acc_ref[0] = term_re if first else acc_ref[0] + term_re
            acc_ref[1] = term_im if first else acc_ref[1] + term_im
    store_tiles(out_ref, acc_ref[0], acc_ref[1])


def spectrum_gradient(fields, adjoint, pupils, grid_table, column_map):
    members = pupils.shape[0]
    rows = grid_table.shape[0] // 2
    vmem = pl.BlockSpec(memory_space=pltpu.VMEM)
    return pl.pallas_call(
        gradient_kernel,
        in_specs=[vmem] * 5,
        out_specs=vmem,
        out_shape=jax.ShapeDtypeStruct((DEVICES, 8, 128), jnp.bfloat16),
        scratch_shapes=[
            pltpu.VMEM((members, 2 * rows, 2 * COARSE), jnp.bfloat16),
            pltpu.VMEM((members, 2 * rows, 2 * BAND), jnp.bfloat16),
            pltpu.VMEM((2, BAND, BAND), jnp.float32),
        ],
        compiler_params=params(),
        name="spectrum_gradient",
    )(fields, adjoint, pupils, grid_table, column_map)


def update_kernel(
    tiles_ref, constant_ref, mask_ref, out_ref,
    tile_ref, spec_ref, bases_ref, shifts_ref, held_ref, steps_ref, phases_ref, re_ref, im_ref, flat_ref, stack_a, stack_b, product_a, product_b, sems,
):
    rows = mask_ref.shape[0]
    stacks = (stack_a, stack_b)
    products = (product_a, product_b)
    count = rows // CHUNK
    places = [pl.ds(i * CHUNK, CHUNK) for i in range(count)]
    chunks = [
        pltpu.make_async_copy(mask_ref.at[places[i]], held_ref.at[places[i]], sems.at[i]) for i in range(count)
    ]
    columns = [pl.ds(quarter * QUARTER, QUARTER) for quarter in range(QUARTERS)]
    results = [
        pltpu.make_async_copy(
            held_ref.at[places[i], columns[quarter]],
            out_ref.at[places[i], columns[quarter]],
            sems.at[count + 5 + QUARTERS * i + quarter],
        )
        for i in range(count)
        for quarter in range(QUARTERS)
    ]
    small = [
        pltpu.make_async_copy(source, target, sems.at[count + i])
        for i, (source, target) in enumerate(
            (
                (constant_ref.at[table_rows("base")], bases_ref),
                (constant_ref.at[shift_group()], shifts_ref),
                (tiles_ref, tile_ref),
                (constant_ref.at[table_rows("phase"), pl.ds(0, BAND)], phases_ref),
                (constant_ref.at[table_rows("step"), pl.ds(BAND, BAND)], steps_ref),
            )
        )
    ]
    for copy in small + chunks:
        copy.start()

    small[0].wait()
    small[1].wait()
    cosine, sine = turned_table(bases_ref[...], own_shift(shifts_ref))
    small[2].wait()
    load_tiles(tile_ref, spec_ref)
    gradient = jnp.concatenate([spec_ref[0], spec_ref[1]], 1).astype(jnp.bfloat16)
    product = float_dot(jnp.concatenate(split(cosine) + split(sine), 0), gradient)
    by_cos = product[:rows] + product[rows : 2 * rows]
    by_sin = product[2 * rows : 3 * rows] + product[3 * rows :]
    col_re = by_cos[:, :BAND] - by_sin[:, BAND:]
    col_im = by_sin[:, :BAND] + by_cos[:, BAND:]
    flat_ref[...] = jnp.broadcast_to(col_re[:, HALF : HALF + 1] * (1.0 / MASK), flat_ref.shape)
    mirror = conjugate_mirror()
    high, low = split(jnp.concatenate([col_re[:, HALF:], col_im[:, HALF:]], 1))
    other = float_dot(high, mirror) + float_dot(low, mirror)
    re_ref[...] = col_re[:, :HALF] + other[:, :HALF]
    im_ref[...] = col_im[:, :HALF] + other[:, HALF:]

    def steps_of(quarter):
        return range(quarter * STEPS // QUARTERS, (quarter + 1) * STEPS // QUARTERS)

    def turn(i, quarter):
        col_re = re_ref[places[i]]
        col_im = im_ref[places[i]]
        for step in steps_of(quarter):
            cosine = phases_ref[step : step + 1, :HALF]
            sine = phases_ref[step : step + 1, HALF:BAND]
            here = slice(step * CHUNK, (step + 1) * CHUNK)
            stacks[i % 2][here, :HALF] = (col_re * cosine - col_im * sine).astype(jnp.bfloat16)
            stacks[i % 2][here, HALF:] = (col_re * sine + col_im * cosine).astype(jnp.bfloat16)

    def multiply(i, quarter):
        here = slice(steps_of(quarter).start * CHUNK, steps_of(quarter).stop * CHUNK)
        products[i % 2][here] = float_dot(stacks[i % 2][here], step_value)

    def finish(i, quarter):
        centre = flat_ref[places[i]]
        for step in steps_of(quarter):
            here = slice(step * STEP, (step + 1) * STEP)
            mask = held_ref[places[i], here]
            transmit = jnp.tanh(mask)
            pixel_grad = products[i % 2][step * CHUNK : (step + 1) * CHUNK] + centre
            held_ref[places[i], here] = mask - step_size * pixel_grad * (1.0 - transmit * transmit)

    small[3].wait()
    for quarter in range(QUARTERS):
        turn(0, quarter)
    small[4].wait()
    step_value = steps_ref[...].astype(jnp.bfloat16)
    for i in range(count + 1):
        if i > 0:
            chunks[i - 1].wait()
        for quarter in range(QUARTERS):
            if i < count:
                multiply(i, quarter)
            if i + 1 < count:
                turn(i + 1, quarter)
            if i > 0:
                finish(i - 1, quarter)
                results[QUARTERS * (i - 1) + quarter].start()
    for copy in results:
        copy.wait()


def mask_update(tiles, constants, mask_params):
    rows = mask_params.shape[0]
    stacked = STEPS * CHUNK
    hbm = pl.BlockSpec(memory_space=pltpu.HBM)
    return pl.pallas_call(
        update_kernel,
        in_specs=[hbm] * 3,
        out_specs=hbm,
        out_shape=jax.ShapeDtypeStruct((rows, MASK), jnp.float32),
        scratch_shapes=[
            pltpu.VMEM(tiles.shape, jnp.bfloat16),
            pltpu.VMEM((2, BAND, BAND), jnp.float32),
            pltpu.VMEM((rows, 2 * BAND), jnp.float32),
            pltpu.VMEM((8, 2 * BAND), jnp.float32),
            pltpu.VMEM((rows, MASK), jnp.float32),
            pltpu.VMEM((STEP, BAND), jnp.float32),
            pltpu.VMEM((STEPS, BAND), jnp.float32),
            pltpu.VMEM((rows, HALF), jnp.float32),
            pltpu.VMEM((rows, HALF), jnp.float32),
            pltpu.VMEM((rows, STEP), jnp.float32),
            pltpu.VMEM((stacked, BAND), jnp.bfloat16),
            pltpu.VMEM((stacked, BAND), jnp.bfloat16),
            pltpu.VMEM((stacked, STEP), jnp.float32),
            pltpu.VMEM((stacked, STEP), jnp.float32),
            pltpu.SemaphoreType.DMA(((QUARTERS + 1) * (rows // CHUNK) + 5,)),
        ],
        compiler_params=params(STREAM_LIMIT),
        name="mask_update",
    )(tiles, constants, mask_params)


def exchange(values, axes):
    return lax.all_to_all(values, axes, 0, 0, tiled=True)


def summed(parts, copies):
    total = jnp.sum(parts.astype(jnp.float32), 0).astype(parts.dtype)
    return jnp.broadcast_to(total[None], (copies,) + total.shape)


def total_kernel(parts_ref, out_ref):
    total = jnp.sum(parts_ref[...].astype(jnp.float32), 0).astype(out_ref.dtype)
    for owner in range(DEVICES):
        out_ref[owner] = total


def total_tiles(parts):
    vmem = pl.BlockSpec(memory_space=pltpu.VMEM)
    return pl.pallas_call(
        total_kernel,
        in_specs=[vmem],
        out_specs=vmem,
        out_shape=jax.ShapeDtypeStruct(parts.shape, parts.dtype),
        compiler_params=params(),
        cost_estimate=pl.CostEstimate(flops=10**10, bytes_accessed=2 * parts.size, transcendentals=0),
        name="total_tiles",
    )(parts)


def local(mask_params, pupil_kernels, target_pattern):
    rows = mask_params.shape[0]
    constants = jnp.asarray(constant_table(rows))
    column_map = jnp.asarray(coarse_map())

    everyone = ("kern", "rows")
    tiles, grid_table = mask_spectrum(mask_params, constants, target_pattern)
    spectrum = exchange(total_tiles(exchange(tiles, everyone)), everyone)
    fields, powers = coarse_fields(spectrum, pupil_kernels, grid_table, column_map)
    adjoint = coarse_adjoint(exchange(powers, "kern"), jnp.asarray(interpolation()))
    gradient = spectrum_gradient(fields, exchange(adjoint, "kern"), pupil_kernels, grid_table, column_map)
    gradient = exchange(summed(exchange(gradient, everyone), DEVICES), everyone)
    return mask_update(gradient, constants, mask_params)


def solution(mesh):
    placed = (P(("rows", "kern"), None), P("kern", None, None, None, None), P("rows", "kern"))
    return jax.shard_map(
        local, mesh=mesh, in_specs=placed, out_specs=P(("rows", "kern"), None), check_vma=False
    )
```
